32 devices in a mesh: groups: 2 (over x), dp: 16 (over z, y, core).
Axes of the slice: x: 2, y: 2, z: 4, core: 2. Of those that a mesh axis runs over, the one named last changes fastest.
Arguments:
- tokens: bfloat16 [8192, 7168], P(('groups', 'dp')), parts along dimension 0, may hold values from -6 to 6
- lengths: int32 [32], P('groups'), parts along dimension 0, may hold values from 0 to 256, as said below
- latent_weight: bfloat16 [7168, 576], P('dp'), may hold values from -0.0625 to 0.0625
- latent_gain: float32 [512], replicated, may hold values from 0.25 to 1.75
- expert_ids: int32 [8192, 1], P(('groups', 'dp')), parts along dimension 0, may hold values from 0 to 1; in each aligned block of 256 rows (0 to 255, 256 to 511, ...) at most 130 rows name the same one
- gate_weights: float32 [8192, 1], P(('groups', 'dp')), parts along dimension 0, may hold values from 0.5 to 1.5
- gate_up: bfloat16 [14336, 2048], P('dp'), may hold values from -0.0625 to 0.0625
- down_weight: bfloat16 [16384, 896], P('dp'), may hold values from -0.1875 to 0.1875
Outputs:
- latent_cache: bfloat16 [8192, 576], P(('groups', 'dp')), parts along dimension 0
- moe_out: bfloat16 [8192, 7168], P(('groups', 'dp')), parts along dimension 0
The draws below stay inside these ranges and needn't reach their ends.
There are 2 independent parts, one for each index of `groups`. The reference program is written for one: setup_inputs(seed, part) draws one part's arguments, and reference() takes and returns one part's arrays. A program takes and returns all parts, laid end to end along the dimension named above; an argument that names none is the same for every part. Nothing has to cross between parts.
Inputs may be any that keep to these rules, and one draw needn't show every extreme that they name: Only the first lengths[r] of rank r's 256 rows are prompt tokens. `expert_ids`: of the 256 rows of one rank, at most 130 name one expert.
All inputs are finite; a program needn't handle non-finite values.
Results may differ from the reference program's by a relative error of at most 0.019.
Values may be sent and summed in bfloat16 or wider, within the bound.
No kernel may reach another device: no remote copies, remote signals or barrier semaphores. Data moves between devices by JAX's collectives and lax.ppermute only.
A program may use at most 128 MiB of HBM per device.

```python
import math
import jax
import jax.numpy as jnp
import numpy as np
from jax import lax

D = 7168
LAT = 512
ROPE = 64
FW = 1024
GROUP = 8
BLOCK = 128
TOPK = 1
BLOCKS = 2
SLOTS = 256
EXPERTS = 2
CAP = 130
TOKENS = 4096
N_DP = 16


def draw_lengths(key, part):
    key = jax.random.fold_in(key, 11)
    half_count = N_DP // 2
    keys = jax.random.split(key, 5)
    pattern = jax.random.randint(keys[0], (half_count,), 0, 3)
    heavy = jax.random.randint(keys[1], (half_count,), (BLOCKS - 1) * BLOCK + 1, SLOTS + 1)
    light_raw = jax.random.randint(keys[2], (half_count,), 0, 2 * BLOCK)
    light = jnp.where(light_raw >= BLOCK, 0, light_raw + 1)
    middle = jax.random.randint(keys[3], (2, half_count), 0, SLOTS + 1)
    flipped = jax.random.randint(keys[4], (half_count,), 0, 2)
    first_half = jnp.where(pattern < 2, jnp.where(flipped == 1, heavy, light), middle[0])
    second_half = jnp.where(pattern < 2, jnp.where(flipped == 1, light, heavy), middle[1])
    first_half = first_half.at[0].set(SLOTS)
    second_half = second_half.at[0].set(0)
    return jnp.concatenate([first_half, second_half]).astype(jnp.int32)


def block_scale(key, extent, shards, low, largest):
    level, own = 1.0, jax.random.fold_in(key, 6)
    for position, parts in shards:
        steps = jnp.exp(jax.random.uniform(jax.random.fold_in(own, position), (parts,), jnp.float32, low / len(shards), largest / len(shards)))
        level = level * jnp.repeat(steps, extent[position] // parts).reshape([-1 if axis == position else 1 for axis in range(len(extent))])
    return level


def assign_block(stream_key, own, number, rows, amount, top, bound, slope):
    sequence = jax.random.permutation(stream_key, amount)
    heavy_load, usual = shares(amount, rows * top, bound, slope, True), shares(amount, rows * top, bound, slope, False)
    places = jnp.arange(amount)

    def named(tallies, rotation):
        used = int((tallies > 0).sum())
        fixed = max(1, used // 4)
        passed = fixed + (places - fixed + rotation * (used - fixed)) % max(1, amount - fixed)
        return jnp.zeros((amount,), jnp.int32).at[sequence[jnp.where(places < fixed, places, passed)]].set(jnp.asarray(tallies, jnp.int32))

    tallies = jnp.where(number % 4 == 0, named(heavy_load, number // 4), named(usual, number - number // 4 - 1))
    mixed = jax.random.permutation(jax.random.fold_in(own, 3), amount)
    source_of, taker = mixed[0:amount // 2 * 2:2], mixed[1:amount // 2 * 2:2]
    margin = jnp.minimum(tallies[source_of] - 1, bound - tallies[taker]) // 2
    margin = jnp.where((source_of == sequence[0]) | (taker == sequence[0]) | (tallies[taker] == 0), 0, jnp.maximum(margin, 0))
    passed = jax.random.randint(jax.random.fold_in(own, 4), (amount // 2,), 0, 1 << 20) % (margin + 1)
    tallies = tallies.at[source_of].add(-passed).at[taker].add(passed)
    labels = jnp.searchsorted(jnp.cumsum(tallies), jnp.arange(rows * top), side="right").astype(jnp.int32)
    listing = labels.reshape(top, rows).T
    listing = listing[jax.random.permutation(jax.random.fold_in(own, 1), rows)]
    rotation = jax.random.randint(jax.random.fold_in(own, 2), (rows, 1), 0, top)
    return jnp.take_along_axis(listing, (jnp.arange(top)[None, :] + rotation) % top, axis=1)


def shares(count, total, reach, skew, full):
    portions = [(1 << 20) // math.isqrt(standing ** skew) + 1 for standing in range(1, count + 1)]
    largest = reach if full else min(reach, max(-(-total // count), total * portions[0] // sum(portions)))
    least = 1 if total - largest >= count - 1 else 0
    counts, surplus = [largest] + [least] * (count - 1), total - largest - least * (count - 1)
    while surplus > 0:
        movable = [i for i in range(1, count) if counts[i] < largest] or [i for i in range(1, count) if counts[i] < reach]
        whole, budget = sum([portions[i] for i in movable]), surplus
        for i in movable:
            more = min(reach - counts[i], max(1, budget * portions[i] // whole), surplus)
            counts[i] = counts[i] + more
            surplus = surplus - more
    return np.array(counts)


def normal_values(key, dims, deviation, bound, pieces=(), held_as=jnp.bfloat16):
    factor_of = block_scale(key, dims, pieces, -0.22, 0.18) if pieces else 1.0
    array = jax.random.normal(key, dims, jnp.float32) * deviation * factor_of
    return jnp.minimum(jnp.maximum(array, -bound), bound).astype(held_as)


def setup_inputs(seed: int = 0, part: int = 0) -> dict:
    arg_keys = jax.random.split(jax.random.key(seed), 9)
    own_keys = jax.random.split(jax.random.fold_in(arg_keys[8], part), 9)
    tokens = normal_values(own_keys[0], (TOKENS, D), 1.0, 6.0, ((0, 16),))
    lengths = draw_lengths(jax.random.fold_in(jax.random.fold_in(arg_keys[8], part), 71), part)
    latent_weight = normal_values(arg_keys[2], (D, LAT + ROPE), D ** -0.5, 0.0625, ((0, 16),))
    latent_gain = jnp.clip(1.0 + 0.15 * jax.random.normal(arg_keys[3], (LAT,), jnp.float32), 0.25, 1.75)
    expert_ids_keys = jax.random.split(jax.random.fold_in(own_keys[4], 1), TOKENS // SLOTS)
    expert_ids_turns = jax.random.permutation(jax.random.fold_in(own_keys[4], 3), TOKENS // SLOTS)
    expert_ids = jax.vmap(lambda own, number: assign_block(jax.random.fold_in(own_keys[4], 2), own, number, SLOTS, EXPERTS, TOPK, CAP, 1))(expert_ids_keys, expert_ids_turns).reshape((TOKENS, TOPK))
    gate_weights = jnp.clip(0.5 + 1.0 * jax.random.uniform(own_keys[5], (TOKENS, TOPK), jnp.float32) ** block_scale(own_keys[5], (TOKENS, TOPK), ((0, 16),), -0.2, 0.2), 0.5, 1.5)
    gate_up = normal_values(arg_keys[6], (EXPERTS * D, 2 * FW), D ** -0.5, 0.0625, ((0, 16),))
    down_weight = normal_values(arg_keys[7], (EXPERTS * GROUP * FW, D // GROUP), FW ** -0.5, 0.1875, ((0, 16),))
    return dict(tokens=tokens, lengths=lengths, latent_weight=latent_weight, latent_gain=latent_gain, expert_ids=expert_ids, gate_weights=gate_weights, gate_up=gate_up, down_weight=down_weight)


rope_base = 10000.0
norm_eps = 1e-06

def latent_rows(token_rows, weight, gain, first_pos, length):
    projected = jnp.dot(token_rows, weight, preferred_element_type=jnp.float32)
    lat_width = gain.shape[0]
    compressed = projected[:, :lat_width]
    rotary = projected[:, lat_width:]
    inverse_rms = lax.rsqrt(lax.optimization_barrier(jnp.mean(compressed * compressed, axis=1, keepdims=True)) + norm_eps)
    normed = compressed * inverse_rms * gain[None, :]
    half_cols = rotary.shape[1] // 2
    positions = first_pos + jnp.arange(token_rows.shape[0], dtype=jnp.int32)
    frequency = rope_base ** (-jnp.arange(half_cols, dtype=jnp.float32) / half_cols)
    angles = positions.astype(jnp.float32)[:, None] * frequency[None, :]
    cosine = jnp.cos(angles)
    sine_part = jnp.sin(angles)
    left_half = rotary[:, :half_cols]
    right_half = rotary[:, half_cols:]
    turned = jnp.concatenate([left_half * cosine - right_half * sine_part, left_half * sine_part + right_half * cosine], axis=1)
    result = jnp.concatenate([normed, turned], axis=1)
    alive_rows = positions < length
    return jnp.where(alive_rows[:, None], result, 0.0).astype(jnp.bfloat16)

def reference(tokens, lengths, latent_weight, latent_gain, expert_ids, gate_weights, gate_up, down_weight):
    row_total = tokens.shape[0]
    per_rank = tokens.reshape(N_DP, SLOTS, D)

    def rank_latent(operands):
        rank_rows, rank_length = operands
        return latent_rows(rank_rows, latent_weight, latent_gain, jnp.int32(0), rank_length)
    latent_cache = lax.map(rank_latent, (per_rank, lengths)).reshape(row_total, LAT + ROPE)
    part_width = D // GROUP
    pairs_per = SLOTS * TOPK
    per_expert = N_DP * CAP
    alive_rows = jnp.arange(SLOTS, dtype=jnp.int32)[None, :] < lengths[:, None]
    live_pair = jnp.repeat(alive_rows, TOPK, axis=1)
    chosen = expert_ids.reshape(N_DP, pairs_per)
    expert_hits = ((chosen[:, :, None] == jnp.arange(EXPERTS, dtype=jnp.int32)[None, None, :]) & live_pair[:, :, None]).astype(jnp.int32)
    slot_place = lax.optimization_barrier(jnp.sum((jnp.cumsum(expert_hits, axis=1) - expert_hits) * expert_hits, axis=2))
    rank_base = jnp.arange(N_DP, dtype=jnp.int32)[:, None] * CAP
    slot_index = jnp.where(live_pair, chosen * per_expert + rank_base + slot_place, EXPERTS * per_expert).reshape(-1).astype(jnp.int32)
    total_pairs = N_DP * pairs_per
    owner = jnp.full((EXPERTS * per_expert,), total_pairs, jnp.int32).at[slot_index].set(jnp.arange(total_pairs, dtype=jnp.int32), mode='drop')
    padded_tokens = jnp.concatenate([tokens, jnp.zeros((1, D), jnp.bfloat16)], axis=0)
    source_row = jnp.where(owner < total_pairs, owner // TOPK, row_total).astype(jnp.int32)
    gate_blocks = gate_up.reshape(EXPERTS, GROUP, part_width, 2 * FW)
    down_blocks = down_weight.reshape(EXPERTS, GROUP, FW, part_width).transpose(0, 2, 1, 3).reshape(EXPERTS, FW, D)

    def one_expert(operands):
        row_picks, weight_in, weight_out = operands
        inputs = padded_tokens[row_picks].reshape(per_expert, GROUP, part_width).astype(jnp.float32)
        partial_value = jnp.einsum('rjd,jdf->jrf', inputs, weight_in.astype(jnp.float32)).astype(jnp.bfloat16)
        summed = lax.optimization_barrier(jnp.sum(partial_value.astype(jnp.float32), axis=0))
        hidden = (jax.nn.silu(summed[:, :FW]) * summed[:, FW:]).astype(jnp.bfloat16)
        return jnp.dot(hidden, weight_out, preferred_element_type=jnp.float32).astype(jnp.bfloat16)
    results = lax.map(one_expert, (source_row.reshape(EXPERTS, per_expert), gate_blocks, down_blocks))
    flat_results = results.reshape(EXPERTS * per_expert, D)
    picked = flat_results[jnp.minimum(slot_index, EXPERTS * per_expert - 1)]
    pair_weight = jnp.where(live_pair.reshape(-1), gate_weights.reshape(-1), 0.0)
    moe_out = (picked.astype(jnp.float32) * pair_weight[:, None]).reshape(row_total, TOPK, D).sum(axis=1).astype(jnp.bfloat16)
    return (latent_cache, moe_out)
```

```python
import functools

import jax
import jax.numpy as jnp
from jax import lax
from jax.experimental import pallas as pl
from jax.experimental.pallas import tpu as pltpu
from jax.sharding import PartitionSpec as P

GROUP = 8
QUAD = 4

rope_base = 10000.0
norm_eps = 1e-06


def swapped(block, bits):
    count = lax.axis_size("dp")
    return lax.ppermute(block, "dp", [(low, low ^ bits) for low in range(count)])


def chosen_slots(meta_ref, column_ids, row_ids):
    rows = column_ids.shape[0]
    length = meta_ref[1]
    own = lax.broadcasted_iota(jnp.int32, (rows, rows), 0)
    other = lax.broadcasted_iota(jnp.int32, (rows, rows), 1)
    earlier = (column_ids == row_ids) & (other < own) & (other < length)
    place = jnp.sum(earlier.astype(jnp.float32), axis=1, keepdims=True).astype(jnp.int32)
    live = lax.broadcasted_iota(jnp.int32, (rows, 1), 0) < length
    return jnp.where(live, column_ids, -1), place


def selector(expert_column, place_column, expert, start, size):
    rows = expert_column.shape[0]
    slot = lax.broadcasted_iota(jnp.int32, (rows, size), 1) + start
    hit = (place_column == slot) & (expert_column == expert)
    return hit.astype(jnp.float32).astype(jnp.bfloat16)


def pack_body(chunks, pieces, meta_ref, column_ref, row_ref, same_ref, other_ref, *outs):
    expert_column, place_column = chosen_slots(meta_ref, column_ref[...], row_ref[...])
    my_expert = meta_ref[0] // GROUP
    same = same_ref[...]
    other = other_ref[...]
    for number, (start, size) in enumerate(chunks):
        for far in range(pieces // 2):
            picks = selector(expert_column, place_column, my_expert ^ far, start, size)
            for side, source in enumerate((same, other)):
                outs[number * pieces + 2 * far + side][...] = lax.dot_general(
                    picks,
                    source,
                    (((0,), (0,)), ((), ())),
                    preferred_element_type=jnp.float32,
                ).astype(jnp.bfloat16)


def pack(meta, ids, tokens, chunks, pieces):
    rows, width = tokens.shape
    part = width // GROUP

    def column_of(side):
        def index(k, meta_ref):
            quarter = meta_ref[0] % QUAD
            high = (meta_ref[0] // QUAD) % 2
            return (0, (high ^ side) * QUAD + (quarter ^ k))

        return index

    whole = lambda k, meta_ref: (0, 0)
    sizes = [size for _, size in chunks for _ in range(pieces)]
    return pl.pallas_call(
        functools.partial(pack_body, chunks, pieces),
        grid_spec=pltpu.PrefetchScalarGridSpec(
            num_scalar_prefetch=1,
            grid=(QUAD,),
            in_specs=[
                pl.BlockSpec((rows, 1), whole),
                pl.BlockSpec((1, rows), whole),
                pl.BlockSpec((rows, part), column_of(0)),
                pl.BlockSpec((rows, part), column_of(1)),
            ],
            out_specs=[pl.BlockSpec((size, part), lambda k, meta_ref: (0, k)) for size in sizes],
        ),
        out_shape=[jax.ShapeDtypeStruct((size, QUAD * part), jnp.bfloat16) for size in sizes],
        compiler_params=pltpu.CompilerParams(vmem_limit_bytes=48 << 20),
        cost_estimate=pl.CostEstimate(
            flops=2 * rows * width * sum(sizes), bytes_accessed=8 * rows * width, transcendentals=0
        ),
        name="pack_rows",
    )(meta, ids, ids.reshape(1, rows), tokens, tokens)


def unpack_body(chunks, pieces, meta_ref, column_ref, row_ref, gate_ref, *refs):
    parts, out_ref = refs[:-1], refs[-1]
    expert_column, place_column = chosen_slots(meta_ref, column_ref[...], row_ref[...])
    my_expert = meta_ref[0] // GROUP
    gate = gate_ref[...]

    def blend(side):
        total = jnp.zeros(out_ref.shape, jnp.float32)
        for number, (start, size) in enumerate(chunks):
            for far in range(pieces // 2):
                picks = selector(expert_column, place_column, my_expert ^ far, start, size)
                part = parts[number * pieces + 2 * far + side]
                total = total + jnp.dot(picks, part[...], preferred_element_type=jnp.float32)
        out_ref[...] = (total * gate).astype(jnp.bfloat16)

    for side in range(2):
        pl.when(pl.program_id(0) == side)(functools.partial(blend, side))


def unpack(meta, ids, gates, returned, chunks, pieces, width):
    rows = ids.shape[0]
    part = width // GROUP

    def out_index(side, k, meta_ref):
        quarter = meta_ref[0] % QUAD
        high = (meta_ref[0] // QUAD) % 2
        return (0, (high ^ side) * QUAD + (quarter ^ k))

    near = lambda side, k, meta_ref: (0, jnp.where(side == 0, k, QUAD - 1))
    far = lambda side, k, meta_ref: (0, jnp.where(side == 1, k, 0))
    whole = lambda side, k, meta_ref: (0, 0)
    specs = []
    for _, size in chunks:
        for piece in range(pieces):
            specs.append(pl.BlockSpec((size, part), far if piece % 2 else near))
    return pl.pallas_call(
        functools.partial(unpack_body, chunks, pieces),
        grid_spec=pltpu.PrefetchScalarGridSpec(
            num_scalar_prefetch=1,
            grid=(2, QUAD),
            in_specs=[
                pl.BlockSpec((rows, 1), whole),
                pl.BlockSpec((1, rows), whole),
                pl.BlockSpec((rows, 1), whole),
            ]
            + specs,
            out_specs=pl.BlockSpec((rows, part), out_index),
        ),
        out_shape=jax.ShapeDtypeStruct((rows, width), jnp.bfloat16),
        compiler_params=pltpu.CompilerParams(vmem_limit_bytes=48 << 20),
        cost_estimate=pl.CostEstimate(
            flops=4 * rows * rows * width, bytes_accessed=4 * rows * width, transcendentals=0
        ),
        name="unpack_rows",
    )(meta, ids, ids.reshape(1, rows), gates, *returned)


def latent_rows(token_rows, weight, gain, length):
    projected = jnp.dot(token_rows, weight, preferred_element_type=jnp.float32)
    lat_width = gain.shape[0]
    compressed = projected[:, :lat_width]
    rotary = projected[:, lat_width:]
    inverse_rms = lax.rsqrt(jnp.mean(compressed * compressed, axis=1, keepdims=True) + norm_eps)
    normed = compressed * inverse_rms * gain[None, :]
    half_cols = rotary.shape[1] // 2
    positions = jnp.arange(token_rows.shape[0], dtype=jnp.int32)
    frequency = rope_base ** (-jnp.arange(half_cols, dtype=jnp.float32) / half_cols)
    angles = positions.astype(jnp.float32)[:, None] * frequency[None, :]
    cosine = jnp.cos(angles)
    sine_part = jnp.sin(angles)
    left_half = rotary[:, :half_cols]
    right_half = rotary[:, half_cols:]
    turned = jnp.concatenate(
        [left_half * cosine - right_half * sine_part, left_half * sine_part + right_half * cosine],
        axis=1,
    )
    result = jnp.concatenate([normed, turned], axis=1)
    return jnp.where((positions < length)[:, None], result, 0.0).astype(jnp.bfloat16)


def gathered_latent(latent_weight, rank, rank_count):
    held = latent_weight
    levels = rank_count.bit_length() - 1
    for step, level in enumerate(range(levels - 1, -1, -1)):
        came = swapped(held, 1 << level)
        upper = (rank >> level) & 1 == 1
        held = jnp.where(
            upper, jnp.stack([came, held], axis=step), jnp.stack([held, came], axis=step)
        )
    return held.reshape(rank_count * latent_weight.shape[0], latent_weight.shape[1])


def four_shards(own):
    next_core = swapped(own, 1)
    across = swapped(own, 2)
    return [own, next_core, across, swapped(across, 1)]


def shards(
    tokens, lengths, latent_weight, latent_gain, expert_ids, gate_weights, gate_up, down_weight
):
    rows, width = tokens.shape
    rank_count = lax.axis_size("dp")
    rank = lax.axis_index("dp")
    experts = rank_count // GROUP
    pieces = rank_count // QUAD
    hidden_units = gate_up.shape[1] // 2
    length = lengths[rank]
    meta = jnp.stack([rank.astype(jnp.int32), length])
    capacity = rows // experts + 2
    chunks = [(0, -(-capacity // 8) * 8)]
    evens, odds = range(0, pieces, 2), range(1, pieces, 2)

    packed = pack(meta, expert_ids, tokens, chunks, pieces)
    weight_in = jnp.concatenate(four_shards(gate_up), axis=0)
    weight_out = jnp.concatenate(four_shards(down_weight), axis=1)

    returned = []
    for number, (_, size) in enumerate(chunks):
        sent = packed[number * pieces : (number + 1) * pieces]
        arrived = [sent[0]] + [swapped(sent[t], QUAD * t) for t in range(1, pieces)]
        theirs = jnp.dot(
            jnp.concatenate([arrived[t] for t in odds], axis=0),
            weight_in,
            preferred_element_type=jnp.float32,
        ).astype(jnp.bfloat16)
        ours = jnp.dot(
            jnp.concatenate([arrived[t] for t in evens], axis=0),
            weight_in,
            preferred_element_type=jnp.float32,
        )
        summed = ours + swapped(theirs, QUAD).astype(jnp.float32)
        hidden = (
            jax.nn.silu(summed[:, :hidden_units]) * summed[:, hidden_units:]
        ).astype(jnp.bfloat16)
        partner = swapped(hidden, QUAD)
        made = [
            jnp.dot(block, weight_out, preferred_element_type=jnp.float32).astype(jnp.bfloat16)
            for block in (hidden, partner)
        ]
        back = []
        for t in range(pieces):
            piece = made[t % 2][t // 2 * size : (t // 2 + 1) * size]
            back.append(swapped(piece, QUAD * t) if t else piece)
        returned += back
    moe_out = unpack(meta, expert_ids, gate_weights, returned, chunks, pieces, width)

    weight = gathered_latent(latent_weight, rank, rank_count)
    latent_cache = latent_rows(tokens, weight, latent_gain, length)
    return (latent_cache, moe_out)


def solution(mesh):
    placed = (
        P(("groups", "dp"), None),
        P("groups"),
        P("dp", None),
        P(),
        P(("groups", "dp"), None),
        P(("groups", "dp"), None),
        P("dp", None),
        P("dp", None),
    )
    return jax.shard_map(
        shards,
        mesh=mesh,
        in_specs=placed,
        out_specs=(P(("groups", "dp"), None), P(("groups", "dp"), None)),
        check_vma=False,
    )
```

```python
import functools

import jax
import jax.numpy as jnp
from jax import lax
from jax.experimental import pallas as pl
from jax.experimental.pallas import tpu as pltpu
from jax.sharding import PartitionSpec as P

GROUP = 8
QUAD = 4

rope_base = 10000.0
norm_eps = 1e-06


def swapped(block, bits):
    count = lax.axis_size("dp")
    return lax.ppermute(block, "dp", [(low, low ^ bits) for low in range(count)])


def chosen_slots(meta_ref, column_ids, row_ids):
    rows = column_ids.shape[0]
    length = meta_ref[1]
    own = lax.broadcasted_iota(jnp.int32, (rows, rows), 0)
    other = lax.broadcasted_iota(jnp.int32, (rows, rows), 1)
    earlier = (column_ids == row_ids) & (other < own) & (other < length)
    place = jnp.sum(earlier.astype(jnp.float32), axis=1, keepdims=True).astype(jnp.int32)
    live = lax.broadcasted_iota(jnp.int32, (rows, 1), 0) < length
    return jnp.where(live, column_ids, -1), place


def selector(expert_column, place_column, expert, start, size):
    rows = expert_column.shape[0]
    slot = lax.broadcasted_iota(jnp.int32, (rows, size), 1) + start
    hit = (place_column == slot) & (expert_column == expert)
    return hit.astype(jnp.float32).astype(jnp.bfloat16)


def pack_body(chunks, meta_ref, column_ref, row_ref, low_ref, high_ref, *outs):
    expert_column, place_column = chosen_slots(meta_ref, column_ref[...], row_ref[...])
    sources = (low_ref[...], high_ref[...])
    for (start, size), out_ref in zip(chunks, outs):
        for expert in range(out_ref.shape[0] // 2):
            picks = selector(expert_column, place_column, expert, start, size)
            for side, source in enumerate(sources):
                out_ref[2 * expert + side] = lax.dot_general(
                    picks,
                    source,
                    (((0,), (0,)), ((), ())),
                    preferred_element_type=jnp.float32,
                ).astype(jnp.bfloat16)


def pack(meta, ids, tokens, chunks, pieces):
    rows, width = tokens.shape
    part = width // GROUP

    def column_of(side):
        return lambda k, meta_ref: (0, side * QUAD + ((meta_ref[0] % QUAD) ^ k))

    whole = lambda k, meta_ref: (0, 0)
    return pl.pallas_call(
        functools.partial(pack_body, chunks),
        grid_spec=pltpu.PrefetchScalarGridSpec(
            num_scalar_prefetch=1,
            grid=(QUAD,),
            in_specs=[
                pl.BlockSpec((rows, 1), whole),
                pl.BlockSpec((1, rows), whole),
                pl.BlockSpec((rows, part), column_of(0)),
                pl.BlockSpec((rows, part), column_of(1)),
            ],
            out_specs=[
                pl.BlockSpec((pieces, size, part), lambda k, meta_ref: (0, 0, k))
                for _, size in chunks
            ],
        ),
        out_shape=[
            jax.ShapeDtypeStruct((pieces, size, QUAD * part), jnp.bfloat16) for _, size in chunks
        ],
        compiler_params=pltpu.CompilerParams(vmem_limit_bytes=58 << 20),
        cost_estimate=pl.CostEstimate(
            flops=4 * rows * rows * width, bytes_accessed=4 * rows * width, transcendentals=0
        ),
        name="pack_rows",
    )(meta, ids, ids.reshape(1, rows), tokens, tokens)


def unpack_body(chunks, pieces, meta_ref, column_ref, row_ref, gate_ref, *refs):
    parts, out_ref = refs[:-1], refs[-1]
    expert_column, place_column = chosen_slots(meta_ref, column_ref[...], row_ref[...])
    my_expert = meta_ref[0] // GROUP
    gate = gate_ref[...]

    def blend(side):
        total = jnp.zeros(out_ref.shape, jnp.float32)
        for number, (start, size) in enumerate(chunks):
            for far in range(pieces // 2):
                picks = selector(expert_column, place_column, my_expert ^ far, start, size)
                part = parts[number * pieces + 2 * far + side]
                total = total + jnp.dot(picks, part[...], preferred_element_type=jnp.float32)
        out_ref[...] = (total * gate).astype(jnp.bfloat16)

    for side in range(2):
        pl.when(pl.program_id(0) == side)(functools.partial(blend, side))


def unpack(meta, ids, gates, returned, chunks, pieces, width):
    rows = ids.shape[0]
    part = width // GROUP

    def out_index(side, k, meta_ref):
        quarter = meta_ref[0] % QUAD
        high = (meta_ref[0] // QUAD) % 2
        return (0, (high ^ side) * QUAD + (quarter ^ k))

    near = lambda side, k, meta_ref: (0, jnp.where(side == 0, k, QUAD - 1))
    far = lambda side, k, meta_ref: (0, jnp.where(side == 1, k, 0))
    whole = lambda side, k, meta_ref: (0, 0)
    specs = []
    for _, size in chunks:
        for piece in range(pieces):
            specs.append(pl.BlockSpec((size, part), far if piece % 2 else near))
    return pl.pallas_call(
        functools.partial(unpack_body, chunks, pieces),
        grid_spec=pltpu.PrefetchScalarGridSpec(
            num_scalar_prefetch=1,
            grid=(2, QUAD),
            in_specs=[
                pl.BlockSpec((rows, 1), whole),
                pl.BlockSpec((1, rows), whole),
                pl.BlockSpec((rows, 1), whole),
            ]
            + specs,
            out_specs=pl.BlockSpec((rows, part), out_index),
        ),
        out_shape=jax.ShapeDtypeStruct((rows, width), jnp.bfloat16),
        compiler_params=pltpu.CompilerParams(vmem_limit_bytes=58 << 20),
        cost_estimate=pl.CostEstimate(
            flops=4 * rows * rows * width, bytes_accessed=4 * rows * width, transcendentals=0
        ),
        name="unpack_rows",
    )(meta, ids, ids.reshape(1, rows), gates, *returned)


def idle_body(*refs):
    del refs


def after(value, *events):
    anywhere = pl.BlockSpec(memory_space=pl.ANY)
    return pl.pallas_call(
        idle_body,
        in_specs=[anywhere] * (1 + len(events)),
        out_specs=anywhere,
        out_shape=jax.ShapeDtypeStruct(value.shape, value.dtype),
        input_output_aliases={0: 0},
        name="after",
    )(value, *events)


def together(*values):
    anywhere = pl.BlockSpec(memory_space=pl.ANY)
    return pl.pallas_call(
        idle_body,
        in_specs=[anywhere] * len(values),
        out_specs=[anywhere] * len(values),
        out_shape=[jax.ShapeDtypeStruct(value.shape, value.dtype) for value in values],
        input_output_aliases={number: number for number in range(len(values))},
        name="together",
    )(*values)


def gate_up_body(count, first, meta_ref, *refs):
    del meta_ref
    parts, rest, out_ref, joined = refs[:count], refs[count:-2], refs[-2], refs[-1]
    size = parts[0].shape[1]

    @pl.when(pl.program_id(0) == 0)
    def _():
        for number, part in enumerate(parts):
            joined[pl.ds(number * size, size), :] = part[0]

    shares, start = rest, first
    total = jnp.zeros(out_ref.shape, jnp.float32)
    if first:
        shares, total = rest[1:], rest[0][...]
    for share in shares:
        depth = share.shape[0]
        total += jnp.dot(
            joined[:, start : start + depth], share[...], preferred_element_type=jnp.float32
        )
        start += depth
    out_ref[...] = total.astype(out_ref.dtype)


def gate_up_product(meta, arrived, shares, side, dtype, first=0, base=()):
    pieces, size, width = arrived.shape
    count = pieces // 2
    rows = size * count
    columns = shares[0].shape[1]
    tile = columns // 4

    def source(number):
        def index(n, meta_ref):
            rank = meta_ref[0]
            return (2 * ((rank // GROUP) ^ number) + (((rank // QUAD) % 2) ^ side), 0, 0)

        return index

    across = lambda n, meta_ref: (0, n)
    return pl.pallas_call(
        functools.partial(gate_up_body, count, first),
        grid_spec=pltpu.PrefetchScalarGridSpec(
            num_scalar_prefetch=1,
            grid=(columns // tile,),
            in_specs=[pl.BlockSpec((1, size, width), source(number)) for number in range(count)]
            + [pl.BlockSpec((rows, tile), across) for _ in base]
            + [pl.BlockSpec((share.shape[0], tile), across) for share in shares],
            out_specs=pl.BlockSpec((rows, tile), across),
            scratch_shapes=[pltpu.VMEM((rows, width), jnp.bfloat16)],
        ),
        out_shape=jax.ShapeDtypeStruct((rows, columns), dtype),
        compiler_params=pltpu.CompilerParams(vmem_limit_bytes=32 << 20),
        cost_estimate=pl.CostEstimate(
            flops=2 * rows * width * columns,
            bytes_accessed=2 * width * (rows + columns),
            transcendentals=0,
        ),
        name="gate_up_product",
    )(meta, *[arrived] * count, *base, *shares)


def down_body(hidden_ref, *refs):
    k = pl.program_id(0)
    shares, outs = refs[:QUAD], refs[QUAD:]
    size = outs[0].shape[0]
    for turn in range(QUAD):

        @pl.when(k == turn)
        def _(turn=turn):
            made = jnp.dot(
                hidden_ref[...], shares[turn][...], preferred_element_type=jnp.float32
            )
            for number, out_ref in enumerate(outs):
                out_ref[...] = made[number * size : (number + 1) * size].astype(jnp.bfloat16)


def down_product(hidden, shares, count):
    rows, depth = hidden.shape
    part = shares[0].shape[1]
    size = rows // count
    return pl.pallas_call(
        down_body,
        grid=(QUAD,),
        in_specs=[pl.BlockSpec((rows, depth), lambda k: (0, 0))]
        + [pl.BlockSpec((depth, part), lambda k: (0, 0)) for _ in shares],
        out_specs=[pl.BlockSpec((size, part), lambda k: (0, k)) for _ in range(count)],
        out_shape=[jax.ShapeDtypeStruct((size, QUAD * part), jnp.bfloat16) for _ in range(count)],
        compiler_params=pltpu.CompilerParams(vmem_limit_bytes=58 << 20),
        cost_estimate=pl.CostEstimate(
            flops=2 * rows * depth * QUAD * part,
            bytes_accessed=2 * (rows * depth + QUAD * part * (rows + depth)),
            transcendentals=0,
        ),
        name="down_product",
    )(hidden, *shares)


def latent_finish(projected, gain, length):
    lat_width = gain.shape[0]
    compressed = projected[:, :lat_width]
    rotary = projected[:, lat_width:]
    inverse_rms = lax.rsqrt(jnp.mean(compressed * compressed, axis=1, keepdims=True) + norm_eps)
    normed = compressed * inverse_rms * gain[None, :]
    half_cols = rotary.shape[1] // 2
    positions = jnp.arange(projected.shape[0], dtype=jnp.int32)
    frequency = rope_base ** (-jnp.arange(half_cols, dtype=jnp.float32) / half_cols)
    angles = positions.astype(jnp.float32)[:, None] * frequency[None, :]
    cosine = jnp.cos(angles)
    sine_part = jnp.sin(angles)
    left_half = rotary[:, :half_cols]
    right_half = rotary[:, half_cols:]
    turned = jnp.concatenate(
        [left_half * cosine - right_half * sine_part, left_half * sine_part + right_half * cosine],
        axis=1,
    )
    result = jnp.concatenate([normed, turned], axis=1)
    return jnp.where((positions < length)[:, None], result, 0.0).astype(jnp.bfloat16)


def latent_body(codes, meta_ref, mine_ref, other_ref, *refs):
    parts, sums, weight, done = refs[: len(codes)], refs[len(codes) : -2], refs[-2], refs[-1]
    size = parts[0].shape[1]
    moves = []
    for part, group in zip(parts, codes):
        for number, code in enumerate(group):
            row = pl.multiple_of(((meta_ref[0] ^ code) // 2) * size, 16)
            move = pltpu.make_async_copy(
                part.at[number], weight.at[pl.ds(row, size), :], done.at[len(moves)]
            )
            move.start()
            moves.append(move)
    for move in moves:
        move.wait()
    for tokens_ref, sum_ref in zip((other_ref, mine_ref), sums):
        product = jnp.dot(tokens_ref[...], weight[...], preferred_element_type=jnp.float32)
        sum_ref[...] = product.astype(sum_ref.dtype)


def latent_product(meta, mine, other, parts, codes):
    rows, width = mine.shape
    columns = parts[0].shape[2]
    total = sum(len(group) for group in codes)
    inside = pl.BlockSpec(memory_space=pltpu.VMEM)
    return pl.pallas_call(
        functools.partial(latent_body, codes),
        in_specs=[pl.BlockSpec(memory_space=pltpu.SMEM), inside, inside]
        + [pl.BlockSpec(memory_space=pl.ANY)] * len(parts),
        out_specs=[inside, inside],
        out_shape=[
            jax.ShapeDtypeStruct((rows, columns), jnp.bfloat16),
            jax.ShapeDtypeStruct((rows, columns), jnp.float32),
        ],
        scratch_shapes=[
            pltpu.VMEM((width, columns), jnp.bfloat16),
            pltpu.SemaphoreType.DMA((total,)),
        ],
        compiler_params=pltpu.CompilerParams(vmem_limit_bytes=32 << 20),
        cost_estimate=pl.CostEstimate(
            flops=4 * rows * width * columns,
            bytes_accessed=2 * width * (2 * rows + columns),
            transcendentals=0,
        ),
        name="latent_product",
    )(meta, mine, other, *parts)


def latent_sums(meta, mine, other, parts, codes):
    if parts[0].shape[1] % 16 == 0:
        return latent_product(meta, mine, other, parts, codes)
    joined = jnp.concatenate(parts, axis=0)
    flat = jnp.array([code for group in codes for code in group], jnp.int32)
    order = jnp.argsort((flat ^ meta[0]) // 2)
    weight = joined[order].reshape(mine.shape[1], joined.shape[2])
    theirs = jnp.dot(other, weight, preferred_element_type=jnp.float32)
    return theirs.astype(jnp.bfloat16), jnp.dot(mine, weight, preferred_element_type=jnp.float32)


def core_columns(tokens, size, core):
    rows, width = tokens.shape
    both = tokens.reshape(rows, width // size // 2, 2, size)
    picked = lax.dynamic_index_in_dim(both, core, axis=2, keepdims=False)
    return picked.reshape(rows, width // 2)


def shards(
    tokens, lengths, latent_weight, latent_gain, expert_ids, gate_weights, gate_up, down_weight
):
    rows, width = tokens.shape
    rank_count = lax.axis_size("dp")
    rank = lax.axis_index("dp")
    experts = rank_count // GROUP
    pieces = rank_count // QUAD
    hidden_units = gate_up.shape[1] // 2
    length = lengths[rank]
    meta = jnp.stack([rank.astype(jnp.int32), length])
    capacity = rows // experts + 2
    chunks = [(0, -(-capacity // 8) * 8)]

    (packed,) = pack(meta, expert_ids, tokens, chunks, pieces)
    columns = [[QUAD * s + low for s in range(pieces)] for low in range(QUAD)]

    core = rank % 2
    size = latent_weight.shape[0]
    arrived, gate_1, gate_2, down_1, latent_1, mine, other = together(
        lax.all_to_all(packed, "dp", 0, 0, axis_index_groups=columns, tiled=True),
        swapped(gate_up, 1),
        swapped(gate_up, 2),
        swapped(down_weight, 1),
        swapped(latent_weight[None], QUAD),
        core_columns(tokens, size, core),
        swapped(core_columns(tokens, size, 1 - core), 1),
    )
    gate_3 = swapped(gate_2, 1)
    down_3 = swapped(down_1, 2)
    held, codes = jnp.concatenate([latent_weight[None], latent_1], axis=0), [0, QUAD]
    for level in range(3, rank_count.bit_length() - 2):
        held = jnp.concatenate([held, swapped(held, 1 << level)], axis=0)
        codes = codes + [code ^ (1 << level) for code in codes]
    bit = rank_count // 2
    half = held.shape[1] // 2
    halved = lax.axis_size("groups") == 2 and half % 16 == 0
    group = lax.axis_index("groups")
    sent = lax.dynamic_slice_in_dim(held, group * half, half, 1) if halved else held
    cut = swapped(sent, bit)

    begun = gate_up_product(meta, arrived, [gate_up, gate_1, gate_2], 1, jnp.float32)
    theirs = gate_up_product(
        meta, arrived, [gate_3], 1, jnp.bfloat16, 3 * gate_up.shape[0], [begun]
    )
    ours = gate_up_product(meta, arrived, [gate_up, gate_1, gate_2, gate_3], 0, jnp.float32)
    came, ours, down_3, cut = together(swapped(theirs, QUAD), ours, down_3, cut)
    summed = ours + came.astype(jnp.float32)
    hidden = (jax.nn.silu(summed[:, :hidden_units]) * summed[:, hidden_units:]).astype(jnp.bfloat16)

    partner, down_2, other_half = together(
        swapped(hidden, QUAD),
        swapped(down_3, 1),
        lax.ppermute(cut, "groups", [(0, 1), (1, 0)]) if halved else cut,
    )
    weight_out = [down_weight, down_1, down_2, down_3]
    made = [down_product(block, weight_out, pieces // 2) for block in (hidden, partner)]
    if halved:
        first = group == 0
        cut = jnp.where(
            first,
            jnp.concatenate([cut, other_half], axis=1),
            jnp.concatenate([other_half, cut], axis=1),
        )
    held = after(jnp.concatenate([held, cut], axis=0), made[1][0])
    codes = codes + [code ^ bit for code in codes]
    latent_parts, latent_codes = [held, swapped(held, 2)], [codes, [code ^ 2 for code in codes]]

    returned = [made[0][0]] + [swapped(made[t % 2][t // 2], QUAD * t) for t in range(1, pieces)]
    moe_out = unpack(meta, expert_ids, gate_weights, returned, chunks, pieces, width)
    given, kept = latent_sums(meta, mine, other, latent_parts, latent_codes)
    projected = kept + swapped(given, 1).astype(jnp.float32)
    latent_cache = latent_finish(projected, latent_gain, length)
    return (latent_cache, moe_out)


def solution(mesh):
    placed = (
        P(("groups", "dp"), None),
        P("groups"),
        P("dp", None),
        P(),
        P(("groups", "dp"), None),
        P(("groups", "dp"), None),
        P("dp", None),
        P("dp", None),
    )
    return jax.shard_map(
        shards,
        mesh=mesh,
        in_specs=placed,
        out_specs=(P(("groups", "dp"), None), P(("groups", "dp"), None)),
        check_vma=False,
    )
```

```python
import functools

import jax
import jax.numpy as jnp
from jax import lax
from jax.experimental import pallas as pl
from jax.experimental.pallas import tpu as pltpu
from jax.sharding import PartitionSpec as P

GROUP = 8
QUAD = 4

rope_base = 10000.0
norm_eps = 1e-06


def swapped(block, bits):
    count = lax.axis_size("dp")
    return lax.ppermute(block, "dp", [(low, low ^ bits) for low in range(count)])


def chosen_slots(meta_ref, column_ids, row_ids):
    rows = column_ids.shape[0]
    length = meta_ref[1]
    own = lax.broadcasted_iota(jnp.int32, (rows, rows), 0)
    other = lax.broadcasted_iota(jnp.int32, (rows, rows), 1)
    earlier = (column_ids == row_ids) & (other < own) & (other < length)
    place = jnp.sum(earlier.astype(jnp.float32), axis=1, keepdims=True).astype(jnp.int32)
    live = lax.broadcasted_iota(jnp.int32, (rows, 1), 0) < length
    return jnp.where(live, column_ids, -1), place


def selector(expert_column, place_column, expert, start, size):
    rows = expert_column.shape[0]
    slot = lax.broadcasted_iota(jnp.int32, (rows, size), 1) + start
    hit = (place_column == slot) & (expert_column == expert)
    return hit.astype(jnp.float32).astype(jnp.bfloat16)


def pack_body(chunks, meta_ref, column_ref, row_ref, low_ref, high_ref, *outs):
    expert_column, place_column = chosen_slots(meta_ref, column_ref[...], row_ref[...])
    sources = (low_ref[...], high_ref[...])
    for (start, size), out_ref in zip(chunks, outs):
        for expert in range(out_ref.shape[0] // 2):
            picks = selector(expert_column, place_column, expert, start, size)
            for side, source in enumerate(sources):
                out_ref[2 * expert + side] = lax.dot_general(
                    picks,
                    source,
                    (((0,), (0,)), ((), ())),
                    preferred_element_type=jnp.float32,
                ).astype(jnp.bfloat16)


def pack(meta, ids, tokens, chunks, pieces):
    rows, width = tokens.shape
    part = width // GROUP

    def column_of(side):
        return lambda k, meta_ref: (0, side * QUAD + ((meta_ref[0] % QUAD) ^ k))

    whole = lambda k, meta_ref: (0, 0)
    return pl.pallas_call(
        functools.partial(pack_body, chunks),
        grid_spec=pltpu.PrefetchScalarGridSpec(
            num_scalar_prefetch=1,
            grid=(QUAD,),
            in_specs=[
                pl.BlockSpec((rows, 1), whole),
                pl.BlockSpec((1, rows), whole),
                pl.BlockSpec((rows, part), column_of(0)),
                pl.BlockSpec((rows, part), column_of(1)),
            ],
            out_specs=[
                pl.BlockSpec((pieces, size, part), lambda k, meta_ref: (0, 0, k))
                for _, size in chunks
            ],
        ),
        out_shape=[
            jax.ShapeDtypeStruct((pieces, size, QUAD * part), jnp.bfloat16) for _, size in chunks
        ],
        compiler_params=pltpu.CompilerParams(vmem_limit_bytes=58 << 20),
        cost_estimate=pl.CostEstimate(
            flops=4 * rows * rows * width, bytes_accessed=4 * rows * width, transcendentals=0
        ),
        name="pack_rows",
    )(meta, ids, ids.reshape(1, rows), tokens, tokens)


def unpack_body(size, meta_ref, column_ref, row_ref, gate_ref, near_ref, *refs):
    far_refs, out_ref = refs[:-1], refs[-1]
    expert_column, place_column = chosen_slots(meta_ref, column_ref[...], row_ref[...])
    my_expert = meta_ref[0] // GROUP
    gate = gate_ref[...]

    def blend(parts):
        total = jnp.zeros(out_ref.shape, jnp.float32)
        for expert, part in parts:
            picks = selector(expert_column, place_column, expert, 0, size)
            total = total + jnp.dot(picks, part, preferred_element_type=jnp.float32)
        out_ref[...] = (total * gate).astype(jnp.bfloat16)

    @pl.when(pl.program_id(0) == 0)
    def _():
        blend([(expert, near_ref[expert]) for expert in range(near_ref.shape[0])])

    @pl.when(pl.program_id(0) == 1)
    def _():
        blend([(my_expert ^ number, ref[...]) for number, ref in enumerate(far_refs)])


def unpack(meta, ids, gates, near, far, width):
    rows = ids.shape[0]
    part = width // GROUP
    experts, size, _ = near.shape

    def out_index(side, k, meta_ref):
        quarter = meta_ref[0] % QUAD
        high = (meta_ref[0] // QUAD) % 2
        return (0, (high ^ side) * QUAD + (quarter ^ k))

    near_index = lambda side, k, meta_ref: (0, 0, jnp.where(side == 0, k, QUAD - 1))
    far_index = lambda side, k, meta_ref: (0, jnp.where(side == 1, k, 0))
    whole = lambda side, k, meta_ref: (0, 0)
    return pl.pallas_call(
        functools.partial(unpack_body, size),
        grid_spec=pltpu.PrefetchScalarGridSpec(
            num_scalar_prefetch=1,
            grid=(2, QUAD),
            in_specs=[
                pl.BlockSpec((rows, 1), whole),
                pl.BlockSpec((1, rows), whole),
                pl.BlockSpec((rows, 1), whole),
                pl.BlockSpec((experts, size, part), near_index),
            ]
            + [pl.BlockSpec((size, part), far_index) for _ in far],
            out_specs=pl.BlockSpec((rows, part), out_index),
        ),
        out_shape=jax.ShapeDtypeStruct((rows, width), jnp.bfloat16),
        compiler_params=pltpu.CompilerParams(vmem_limit_bytes=58 << 20),
        cost_estimate=pl.CostEstimate(
            flops=4 * rows * rows * width, bytes_accessed=4 * rows * width, transcendentals=0
        ),
        name="unpack_rows",
    )(meta, ids, ids.reshape(1, rows), gates, near, *far)


def idle_body(*refs):
    del refs


def after(value, *events):
    anywhere = pl.BlockSpec(memory_space=pl.ANY)
    return pl.pallas_call(
        idle_body,
        in_specs=[anywhere] * (1 + len(events)),
        out_specs=anywhere,
        out_shape=jax.ShapeDtypeStruct(value.shape, value.dtype),
        input_output_aliases={0: 0},
        name="after",
    )(value, *events)


def together(*values):
    anywhere = pl.BlockSpec(memory_space=pl.ANY)
    return pl.pallas_call(
        idle_body,
        in_specs=[anywhere] * len(values),
        out_specs=[anywhere] * len(values),
        out_shape=[jax.ShapeDtypeStruct(value.shape, value.dtype) for value in values],
        input_output_aliases={number: number for number in range(len(values))},
        name="together",
    )(*values)


def gate_up_body(count, meta_ref, *refs):
    del meta_ref
    parts, shares, out_ref, joined = refs[:count], refs[count:-2], refs[-2], refs[-1]
    size = parts[0].shape[1]
    depth = shares[0].shape[0]

    @pl.when(pl.program_id(0) == 0)
    def _():
        for number, part in enumerate(parts):
            joined[pl.ds(number * size, size), :] = part[0]

    total = jnp.dot(joined[:, :depth], shares[0][...], preferred_element_type=jnp.float32)
    for k in range(1, QUAD):
        total += jnp.dot(
            joined[:, k * depth : (k + 1) * depth],
            shares[k][...],
            preferred_element_type=jnp.float32,
        )
    out_ref[...] = total.astype(out_ref.dtype)


def gate_up_product(meta, arrived, shares, side, dtype):
    pieces, size, width = arrived.shape
    count = pieces // 2
    rows = size * count
    depth, columns = shares[0].shape
    tile = columns // 4

    def source(number):
        def index(n, meta_ref):
            rank = meta_ref[0]
            return (2 * ((rank // GROUP) ^ number) + (((rank // QUAD) % 2) ^ side), 0, 0)

        return index

    across = lambda n, meta_ref: (0, n)
    return pl.pallas_call(
        functools.partial(gate_up_body, count),
        grid_spec=pltpu.PrefetchScalarGridSpec(
            num_scalar_prefetch=1,
            grid=(columns // tile,),
            in_specs=[pl.BlockSpec((1, size, width), source(number)) for number in range(count)]
            + [pl.BlockSpec((depth, tile), across) for _ in shares],
            out_specs=pl.BlockSpec((rows, tile), across),
            scratch_shapes=[pltpu.VMEM((rows, width), jnp.bfloat16)],
        ),
        out_shape=jax.ShapeDtypeStruct((rows, columns), dtype),
        compiler_params=pltpu.CompilerParams(vmem_limit_bytes=32 << 20),
        cost_estimate=pl.CostEstimate(
            flops=2 * rows * width * columns,
            bytes_accessed=2 * width * (rows + columns),
            transcendentals=0,
        ),
        name="gate_up_product",
    )(meta, *[arrived] * count, *shares)


def down_body(joined, meta_ref, hidden_ref, *refs):
    k = pl.program_id(0)
    shares, outs = refs[:QUAD], refs[QUAD:]
    count = outs[0].shape[0] if joined else len(outs)
    size = hidden_ref.shape[0] // count
    mine = meta_ref[0] // GROUP
    for turn in range(QUAD):

        @pl.when(k == turn)
        def _(turn=turn):
            made = jnp.dot(
                hidden_ref[...], shares[turn][...], preferred_element_type=jnp.float32
            )
            for number in range(count):
                rows = made[number * size : (number + 1) * size].astype(jnp.bfloat16)
                if joined:
                    outs[0][mine ^ number] = rows
                else:
                    outs[number][...] = rows


def down_product(meta, hidden, shares, count, joined):
    rows, depth = hidden.shape
    part = shares[0].shape[1]
    size = rows // count
    whole = lambda k, meta_ref: (0, 0)
    if joined:
        out_specs = [pl.BlockSpec((count, size, part), lambda k, meta_ref: (0, 0, k))]
        shapes = [(count, size, QUAD * part)]
    else:
        out_specs = [pl.BlockSpec((size, part), lambda k, meta_ref: (0, k))] * count
        shapes = [(size, QUAD * part)] * count
    return pl.pallas_call(
        functools.partial(down_body, joined),
        grid_spec=pltpu.PrefetchScalarGridSpec(
            num_scalar_prefetch=1,
            grid=(QUAD,),
            in_specs=[pl.BlockSpec((rows, depth), whole)]
            + [pl.BlockSpec((depth, part), whole) for _ in shares],
            out_specs=out_specs,
        ),
        out_shape=[jax.ShapeDtypeStruct(shape, jnp.bfloat16) for shape in shapes],
        compiler_params=pltpu.CompilerParams(vmem_limit_bytes=58 << 20),
        cost_estimate=pl.CostEstimate(
            flops=2 * rows * depth * QUAD * part,
            bytes_accessed=2 * (rows * depth + QUAD * part * (rows + depth)),
            transcendentals=0,
        ),
        name="down_product",
    )(meta, hidden, *shares)


def latent_finish(projected, gain, length):
    lat_width = gain.shape[0]
    compressed = projected[:, :lat_width]
    rotary = projected[:, lat_width:]
    inverse_rms = lax.rsqrt(jnp.mean(compressed * compressed, axis=1, keepdims=True) + norm_eps)
    normed = compressed * inverse_rms * gain[None, :]
    half_cols = rotary.shape[1] // 2
    positions = jnp.arange(projected.shape[0], dtype=jnp.int32)
    frequency = rope_base ** (-jnp.arange(half_cols, dtype=jnp.float32) / half_cols)
    angles = positions.astype(jnp.float32)[:, None] * frequency[None, :]
    cosine = jnp.cos(angles)
    sine_part = jnp.sin(angles)
    left_half = rotary[:, :half_cols]
    right_half = rotary[:, half_cols:]
    turned = jnp.concatenate(
        [left_half * cosine - right_half * sine_part, left_half * sine_part + right_half * cosine],
        axis=1,
    )
    result = jnp.concatenate([normed, turned], axis=1)
    return jnp.where((positions < length)[:, None], result, 0.0).astype(jnp.bfloat16)


def latent_body(codes, meta_ref, mine_ref, other_ref, *refs):
    parts, sums, weight, done = refs[: len(codes)], refs[len(codes) : -2], refs[-2], refs[-1]
    size = parts[0].shape[1]
    moves = []
    for part, group in zip(parts, codes):
        for number, code in enumerate(group):
            row = pl.multiple_of(((meta_ref[0] ^ code) // 2) * size, 16)
            move = pltpu.make_async_copy(
                part.at[number], weight.at[pl.ds(row, size), :], done.at[len(moves)]
            )
            move.start()
            moves.append(move)
    for move in moves:
        move.wait()
    for tokens_ref, sum_ref in zip((other_ref, mine_ref), sums):
        product = jnp.dot(tokens_ref[0], weight[:size, :], preferred_element_type=jnp.float32)
        for number in range(1, tokens_ref.shape[0]):
            product += jnp.dot(
                tokens_ref[number],
                weight[number * size : (number + 1) * size, :],
                preferred_element_type=jnp.float32,
            )
        sum_ref[...] = product.astype(sum_ref.dtype)


def latent_product(meta, mine, other, parts, codes):
    count, rows, size = mine.shape
    width = count * size
    columns = parts[0].shape[2]
    total = sum(len(group) for group in codes)
    inside = pl.BlockSpec(memory_space=pltpu.VMEM)
    return pl.pallas_call(
        functools.partial(latent_body, codes),
        in_specs=[pl.BlockSpec(memory_space=pltpu.SMEM), inside, inside]
        + [pl.BlockSpec(memory_space=pl.ANY)] * len(parts),
        out_specs=[inside, inside],
        out_shape=[
            jax.ShapeDtypeStruct((rows, columns), jnp.bfloat16),
            jax.ShapeDtypeStruct((rows, columns), jnp.float32),
        ],
        scratch_shapes=[
            pltpu.VMEM((width, columns), jnp.bfloat16),
            pltpu.SemaphoreType.DMA((total,)),
        ],
        compiler_params=pltpu.CompilerParams(vmem_limit_bytes=32 << 20),
        cost_estimate=pl.CostEstimate(
            flops=4 * rows * width * columns,
            bytes_accessed=2 * width * (2 * rows + columns),
            transcendentals=0,
        ),
        name="latent_product",
    )(meta, mine, other, *parts)


def latent_sums(meta, mine, other, parts, codes):
    if parts[0].shape[1] % 16 == 0:
        return latent_product(meta, mine, other, parts, codes)
    joined = jnp.concatenate(parts, axis=0)
    flat = jnp.array([code for group in codes for code in group], jnp.int32)
    order = jnp.argsort((flat ^ meta[0]) // 2)
    weight = joined[order]
    theirs, kept = [
        jnp.einsum("crs,csf->rf", half, weight, preferred_element_type=jnp.float32)
        for half in (other, mine)
    ]
    return theirs.astype(jnp.bfloat16), kept


def core_split_body(meta_ref, tokens_ref, mine_ref, other_ref):
    half = mine_ref.shape[2]
    low, high = tokens_ref[:, :half], tokens_ref[:, half:]

    @pl.when(meta_ref[0] % 2 == 0)
    def _():
        mine_ref[0], other_ref[0] = low, high

    @pl.when(meta_ref[0] % 2 == 1)
    def _():
        mine_ref[0], other_ref[0] = high, low


def core_split(meta, tokens, size):
    rows, width = tokens.shape
    count = width // size // 2
    out = pl.BlockSpec((1, rows, size), lambda n, meta_ref: (n, 0, 0))
    return pl.pallas_call(
        core_split_body,
        grid_spec=pltpu.PrefetchScalarGridSpec(
            num_scalar_prefetch=1,
            grid=(count,),
            in_specs=[pl.BlockSpec((rows, 2 * size), lambda n, meta_ref: (0, n))],
            out_specs=[out, out],
        ),
        out_shape=[jax.ShapeDtypeStruct((count, rows, size), jnp.bfloat16)] * 2,
        name="core_split",
    )(meta, tokens)


def token_halves(meta, tokens, size):
    if size % 64 == 0:
        return core_split(meta, tokens, size)
    rows, width = tokens.shape
    both = tokens.reshape(rows, width // size // 2, 2, size).transpose(2, 1, 0, 3)
    core = meta[0] % 2
    return both[core], both[1 - core]


def shards(
    tokens, lengths, latent_weight, latent_gain, expert_ids, gate_weights, gate_up, down_weight
):
    rows, width = tokens.shape
    rank_count = lax.axis_size("dp")
    rank = lax.axis_index("dp")
    experts = rank_count // GROUP
    pieces = rank_count // QUAD
    hidden_units = gate_up.shape[1] // 2
    length = lengths[rank]
    meta = jnp.stack([rank.astype(jnp.int32), length])
    capacity = rows // experts + 2
    chunks = [(0, -(-capacity // 8) * 8)]

    (packed,) = pack(meta, expert_ids, tokens, chunks, pieces)
    columns = [[QUAD * s + low for s in range(pieces)] for low in range(QUAD)]
    mine, other = token_halves(meta, tokens, latent_weight.shape[0])

    gate_2 = swapped(gate_up, 2)
    latent_1 = swapped(latent_weight[None], QUAD)
    packed = after(packed, latent_1)
    down_1 = swapped(down_weight, 1)
    arrived, gate_1, gate_3, mine, other = together(
        lax.all_to_all(packed, "dp", 0, 0, axis_index_groups=columns, tiled=True),
        swapped(gate_up, 1),
        swapped(gate_2, 1),
        mine,
        swapped(other, 1),
    )
    down_1 = after(down_1, gate_2)
    down_3 = swapped(down_1, 2)
    held, codes = jnp.concatenate([latent_weight[None], latent_1], axis=0), [0, QUAD]
    middle = pieces == 4
    if not middle:
        for level in range(3, rank_count.bit_length() - 1):
            held = jnp.concatenate([held, swapped(held, 1 << level)], axis=0)
            codes = codes + [code ^ (1 << level) for code in codes]
    cut = held
    if middle:
        cut = lax.ppermute(held, "dp", [(low, low ^ 12) for low in range(QUAD, 3 * QUAD)])

    weight_in = [gate_up, gate_1, gate_2, gate_3]
    theirs = gate_up_product(meta, arrived, weight_in, 1, jnp.bfloat16)
    ours = gate_up_product(meta, arrived, weight_in, 0, jnp.float32)
    down_3 = after(down_3, ours)
    split = down_3.shape[0] // 2
    down_2 = [swapped(piece, 1) for piece in (down_3[:split], down_3[split:])]
    came, ours, cut, *down_2 = together(swapped(theirs, QUAD), ours, cut, *down_2)
    down_2 = jnp.concatenate(down_2, axis=0)
    summed = ours + came.astype(jnp.float32)
    hidden = (jax.nn.silu(summed[:, :hidden_units]) * summed[:, hidden_units:]).astype(jnp.bfloat16)

    held = after(held, hidden)
    latent_parts, latent_codes = [held, swapped(held, 2)], [codes, [code ^ 2 for code in codes]]
    partner = swapped(hidden, QUAD)
    forward = cut
    if middle:
        forward = lax.ppermute(
            cut, "dp", [(low, low ^ QUAD) for low in range(QUAD, 3 * QUAD)]
        )

    weight_out = [down_weight, down_1, down_2, down_3]
    (made_own,) = down_product(meta, hidden, weight_out, experts, True)
    halves = [[GROUP * e + low for e in range(experts)] for low in range(GROUP)]
    near = lax.all_to_all(made_own, "dp", 0, 0, axis_index_groups=halves, tiled=True)
    partner, forward = together(partner, forward)
    partner = after(partner, made_own)
    made = down_product(meta, partner, weight_out, experts, False)
    far = [swapped(made[n], QUAD * (2 * n + 1)) for n in range(experts)]
    if middle:
        inner = (rank >> 2 & 1) != (rank >> 3 & 1)
        part = after(jnp.where(inner, cut[::-1], forward), partner)
        latent_parts += [part, swapped(part, 2)]
        latent_codes += [[8, 12], [8 ^ 2, 12 ^ 2]]
    moe_out = unpack(meta, expert_ids, gate_weights, near, far, width)
    given, kept = latent_sums(meta, mine, other, latent_parts, latent_codes)
    projected = kept + swapped(given, 1).astype(jnp.float32)
    latent_cache = latent_finish(projected, latent_gain, length)
    return (latent_cache, moe_out)


def solution(mesh):
    placed = (
        P(("groups", "dp"), None),
        P("groups"),
        P("dp", None),
        P(),
        P(("groups", "dp"), None),
        P(("groups", "dp"), None),
        P("dp", None),
        P("dp", None),
    )
    return jax.shard_map(
        shards,
        mesh=mesh,
        in_specs=placed,
        out_specs=(P(("groups", "dp"), None), P(("groups", "dp"), None)),
        check_vma=False,
    )
```

```python
import functools

import jax
import jax.numpy as jnp
from jax import lax
from jax.experimental import pallas as pl
from jax.experimental.pallas import tpu as pltpu
from jax.sharding import PartitionSpec as P

GROUP = 8
QUAD = 4

rope_base = 10000.0
norm_eps = 1e-06


def swapped(block, bits):
    count = lax.axis_size("dp")
    return lax.ppermute(block, "dp", [(low, low ^ bits) for low in range(count)])


def slots_of_rows(rank_ref, lengths_ref, ids_row):
    rows = ids_row.shape[1]
    length = lengths_ref[rank_ref[0]]
    down = lax.broadcasted_iota(jnp.int32, (rows, rows), 0)
    along = lax.broadcasted_iota(jnp.int32, (rows, rows), 1)
    ids_column = jnp.sum(
        jnp.where(down == along, ids_row.astype(jnp.float32), 0.0), axis=1, keepdims=True
    ).astype(jnp.int32)
    return length, down, along, ids_column, ids_column == ids_row


def picks_by_slot(rank_ref, lengths_ref, ids_row, experts, size, picks_ref):
    rows = ids_row.shape[1]
    length, down, along, _, same = slots_of_rows(rank_ref, lengths_ref, ids_row)
    earlier = same & (down < along) & (down < length)
    place = jnp.sum(earlier.astype(jnp.float32), axis=0, keepdims=True).astype(jnp.int32)
    live = lax.broadcasted_iota(jnp.int32, (1, rows), 1) < length
    chosen = jnp.where(live, ids_row, -1)
    slot = lax.broadcasted_iota(jnp.int32, (size, rows), 0)
    for expert in range(experts):
        hit = (place == slot) & (chosen == expert)
        picks_ref[expert] = hit.astype(jnp.float32).astype(jnp.bfloat16)


def picks_by_row(rank_ref, lengths_ref, ids_row, experts, size, picks_ref):
    rows = ids_row.shape[1]
    length, down, along, ids_column, same = slots_of_rows(rank_ref, lengths_ref, ids_row)
    earlier = same & (along < down) & (along < length)
    place = jnp.sum(earlier.astype(jnp.float32), axis=1, keepdims=True).astype(jnp.int32)
    live = lax.broadcasted_iota(jnp.int32, (rows, 1), 0) < length
    chosen = jnp.where(live, ids_column, -1)
    slot = lax.broadcasted_iota(jnp.int32, (rows, size), 1)
    for expert in range(experts):
        hit = (place == slot) & (chosen == expert)
        picks_ref[expert] = hit.astype(jnp.float32).astype(jnp.bfloat16)


def pack_body(rank_ref, lengths_ref, ids_ref, low_ref, high_ref, out_ref, picks_ref):
    experts, size, _ = picks_ref.shape

    @pl.when(pl.program_id(0) == 0)
    def _():
        picks_by_slot(rank_ref, lengths_ref, ids_ref[...], experts, size, picks_ref)

    for side, source_ref in enumerate((low_ref, high_ref)):
        for expert in range(experts):
            out_ref[2 * expert + side] = jnp.dot(
                picks_ref[expert], source_ref[...], preferred_element_type=jnp.float32
            ).astype(jnp.bfloat16)


def pack(rank_array, lengths, ids, tokens, experts, size):
    rows, width = tokens.shape
    part = width // GROUP

    def column_of(side):
        return lambda k, rank_ref, lengths_ref: (0, side * QUAD + ((rank_ref[0] % QUAD) ^ k))

    whole = lambda k, rank_ref, lengths_ref: (0, 0)
    return pl.pallas_call(
        pack_body,
        grid_spec=pltpu.PrefetchScalarGridSpec(
            num_scalar_prefetch=2,
            grid=(QUAD,),
            in_specs=[
                pl.BlockSpec((1, rows), whole),
                pl.BlockSpec((rows, part), column_of(0)),
                pl.BlockSpec((rows, part), column_of(1)),
            ],
            out_specs=pl.BlockSpec(
                (2 * experts, size, part), lambda k, rank_ref, lengths_ref: (0, 0, k)
            ),
            scratch_shapes=[pltpu.VMEM((experts, size, rows), jnp.bfloat16)],
        ),
        out_shape=jax.ShapeDtypeStruct((2 * experts, size, QUAD * part), jnp.bfloat16),
        compiler_params=pltpu.CompilerParams(vmem_limit_bytes=58 << 20),
        cost_estimate=pl.CostEstimate(
            flops=4 * rows * rows * width, bytes_accessed=4 * rows * width, transcendentals=0
        ),
        name="pack_rows",
    )(rank_array, lengths, ids.reshape(1, rows), tokens, tokens)


def unpack_body(near, rank_ref, lengths_ref, ids_ref, gate_ref, *refs):
    out_ref, picks_ref, gate_column_ref = refs[-3:]
    experts, rows, size = picks_ref.shape
    my_expert = rank_ref[0] // GROUP

    @pl.when(pl.program_id(0) == 0)
    def _():
        picks_by_row(rank_ref, lengths_ref, ids_ref[...], experts, size, picks_ref)
        down = lax.broadcasted_iota(jnp.int32, (rows, rows), 0)
        along = lax.broadcasted_iota(jnp.int32, (rows, rows), 1)
        gate_column_ref[...] = jnp.sum(
            jnp.where(down == along, gate_ref[...], 0.0), axis=1, keepdims=True
        )

    total = jnp.zeros(out_ref.shape, jnp.float32)
    for number in range(experts):
        part = refs[0][number] if near else refs[number][...]
        picks = picks_ref[number if near else my_expert ^ number]
        total += jnp.dot(picks, part, preferred_element_type=jnp.float32)
    out_ref[...] = (total * gate_column_ref[...]).astype(jnp.bfloat16)


def unpack(rank_array, lengths, ids, gates, parts, width, near, base=()):
    rows = ids.shape[0]
    part = width // GROUP
    size = parts[0].shape[-2]
    experts = parts[0].shape[0] if near else len(parts)

    def out_index(k, rank_ref, lengths_ref):
        quarter = rank_ref[0] % QUAD
        high = (rank_ref[0] // QUAD) % 2
        return (0, (high if near else 1 - high) * QUAD + (quarter ^ k))

    whole = lambda k, rank_ref, lengths_ref: (0, 0)
    if near:
        specs = [pl.BlockSpec((experts, size, part), lambda k, rank_ref, lengths_ref: (0, 0, k))]
    else:
        specs = [pl.BlockSpec((size, part), lambda k, rank_ref, lengths_ref: (0, k))] * experts
    return pl.pallas_call(
        functools.partial(unpack_body, near),
        grid_spec=pltpu.PrefetchScalarGridSpec(
            num_scalar_prefetch=2,
            grid=(QUAD,),
            in_specs=[pl.BlockSpec((1, rows), whole), pl.BlockSpec((1, rows), whole)]
            + specs
            + [pl.BlockSpec(memory_space=pl.ANY)] * len(base),
            out_specs=pl.BlockSpec((rows, part), out_index),
            scratch_shapes=[
                pltpu.VMEM((experts, rows, size), jnp.bfloat16),
                pltpu.VMEM((rows, 1), jnp.float32),
            ],
        ),
        out_shape=jax.ShapeDtypeStruct((rows, width), jnp.bfloat16),
        input_output_aliases={4 + len(specs): 0} if base else {},
        compiler_params=pltpu.CompilerParams(vmem_limit_bytes=58 << 20),
        cost_estimate=pl.CostEstimate(
            flops=2 * rows * rows * width, bytes_accessed=2 * rows * width, transcendentals=0
        ),
        name="unpack_rows",
    )(rank_array, lengths, ids.reshape(1, rows), gates.reshape(1, rows), *parts, *base)


def idle_body(*refs):
    del refs


def after(value, *events):
    anywhere = pl.BlockSpec(memory_space=pl.ANY)
    return pl.pallas_call(
        idle_body,
        in_specs=[anywhere] * (1 + len(events)),
        out_specs=anywhere,
        out_shape=jax.ShapeDtypeStruct(value.shape, value.dtype),
        input_output_aliases={0: 0},
        name="after",
    )(value, *events)


def together(*values):
    anywhere = pl.BlockSpec(memory_space=pl.ANY)
    return pl.pallas_call(
        idle_body,
        in_specs=[anywhere] * len(values),
        out_specs=[anywhere] * len(values),
        out_shape=[jax.ShapeDtypeStruct(value.shape, value.dtype) for value in values],
        input_output_aliases={number: number for number in range(len(values))},
        name="together",
    )(*values)


def gate_up_body(count, meta_ref, *refs):
    del meta_ref
    parts, shares, out_ref, joined = refs[:count], refs[count:-2], refs[-2], refs[-1]
    size = parts[0].shape[1]
    depth = shares[0].shape[0]

    @pl.when(pl.program_id(0) == 0)
    def _():
        for number, part in enumerate(parts):
            joined[pl.ds(number * size, size), :] = part[0]

    total = jnp.dot(joined[:, :depth], shares[0][...], preferred_element_type=jnp.float32)
    for k in range(1, QUAD):
        total += jnp.dot(
            joined[:, k * depth : (k + 1) * depth],
            shares[k][...],
            preferred_element_type=jnp.float32,
        )
    out_ref[...] = total.astype(out_ref.dtype)


def gate_up_product(meta, arrived, shares, side, dtype):
    pieces, size, width = arrived.shape
    count = pieces // 2
    rows = size * count
    depth, columns = shares[0].shape
    tile = columns // 4

    def source(number):
        def index(n, meta_ref):
            rank = meta_ref[0]
            return (2 * ((rank // GROUP) ^ number) + (((rank // QUAD) % 2) ^ side), 0, 0)

        return index

    across = lambda n, meta_ref: (0, n)
    return pl.pallas_call(
        functools.partial(gate_up_body, count),
        grid_spec=pltpu.PrefetchScalarGridSpec(
            num_scalar_prefetch=1,
            grid=(columns // tile,),
            in_specs=[pl.BlockSpec((1, size, width), source(number)) for number in range(count)]
            + [pl.BlockSpec((depth, tile), across) for _ in shares],
            out_specs=pl.BlockSpec((rows, tile), across),
            scratch_shapes=[pltpu.VMEM((rows, width), jnp.bfloat16)],
        ),
        out_shape=jax.ShapeDtypeStruct((rows, columns), dtype),
        compiler_params=pltpu.CompilerParams(vmem_limit_bytes=32 << 20),
        cost_estimate=pl.CostEstimate(
            flops=2 * rows * width * columns,
            bytes_accessed=2 * width * (rows + columns),
            transcendentals=0,
        ),
        name="gate_up_product",
    )(meta, *[arrived] * count, *shares)


def down_body(places, joined, meta_ref, hidden_ref, *refs):
    k = pl.program_id(0)
    weight, done = refs[-2:]
    pieces, outs = refs[: len(places)], refs[len(places) : -2]
    count = outs[0].shape[0] if joined else len(outs)
    size = hidden_ref.shape[0] // count
    mine = meta_ref[0] // GROUP
    moves = []
    for number, (piece, (turn, start)) in enumerate(zip(pieces, places)):
        target = weight.at[turn, pl.ds(start, piece.shape[0]), :]
        moves.append(pltpu.make_async_copy(piece, target, done.at[number]))

    @pl.when(k == 0)
    def _():
        for move in moves:
            move.start()

    for turn in range(QUAD):

        @pl.when(k == turn)
        def _(turn=turn):
            for move, place in zip(moves, places):
                if place[0] == turn:
                    move.wait()

    made = jnp.dot(hidden_ref[...], weight[k], preferred_element_type=jnp.float32)
    for number in range(count):
        rows = made[number * size : (number + 1) * size].astype(jnp.bfloat16)
        if joined:
            outs[0][mine ^ number] = rows
        else:
            outs[number][...] = rows


def down_product(meta, hidden, shares, count, joined):
    rows, depth = hidden.shape
    part = shares[0].shape[1]
    size = rows // count
    places, filled = [], 0
    for share in shares:
        places.append((filled // depth, filled % depth))
        filled += share.shape[0]
    whole = lambda k, meta_ref: (0, 0)
    if joined:
        out_specs = [pl.BlockSpec((count, size, part), lambda k, meta_ref: (0, 0, k))]
        shapes = [(count, size, QUAD * part)]
    else:
        out_specs = [pl.BlockSpec((size, part), lambda k, meta_ref: (0, k))] * count
        shapes = [(size, QUAD * part)] * count
    return pl.pallas_call(
        functools.partial(down_body, places, joined),
        grid_spec=pltpu.PrefetchScalarGridSpec(
            num_scalar_prefetch=1,
            grid=(QUAD,),
            in_specs=[pl.BlockSpec((rows, depth), whole)]
            + [pl.BlockSpec(memory_space=pl.ANY)] * len(shares),
            out_specs=out_specs,
            scratch_shapes=[
                pltpu.VMEM((QUAD, depth, part), jnp.bfloat16),
                pltpu.SemaphoreType.DMA((len(shares),)),
            ],
        ),
        out_shape=[jax.ShapeDtypeStruct(shape, jnp.bfloat16) for shape in shapes],
        compiler_params=pltpu.CompilerParams(vmem_limit_bytes=58 << 20),
        cost_estimate=pl.CostEstimate(
            flops=2 * rows * depth * QUAD * part,
            bytes_accessed=2 * (rows * depth + QUAD * part * (rows + depth)),
            transcendentals=0,
        ),
        name="down_product",
    )(meta, hidden, *shares)


def latent_finish(projected, gain, length):
    lat_width = gain.shape[0]
    compressed = projected[:, :lat_width]
    rotary = projected[:, lat_width:]
    inverse_rms = lax.rsqrt(jnp.mean(compressed * compressed, axis=1, keepdims=True) + norm_eps)
    normed = compressed * inverse_rms * gain[None, :]
    half_cols = rotary.shape[1] // 2
    positions = jnp.arange(projected.shape[0], dtype=jnp.int32)
    frequency = rope_base ** (-jnp.arange(half_cols, dtype=jnp.float32) / half_cols)
    angles = positions.astype(jnp.float32)[:, None] * frequency[None, :]
    cosine = jnp.cos(angles)
    sine_part = jnp.sin(angles)
    left_half = rotary[:, :half_cols]
    right_half = rotary[:, half_cols:]
    turned = jnp.concatenate(
        [left_half * cosine - right_half * sine_part, left_half * sine_part + right_half * cosine],
        axis=1,
    )
    result = jnp.concatenate([normed, turned], axis=1)
    return jnp.where((positions < length)[:, None], result, 0.0).astype(jnp.bfloat16)


def latent_body(codes, meta_ref, mine_ref, other_ref, *refs):
    parts, sums, weight, done = refs[: len(codes)], refs[len(codes) : -2], refs[-2], refs[-1]
    size = parts[0].shape[1]
    moves = []
    for part, group in zip(parts, codes):
        for number, code in enumerate(group):
            row = pl.multiple_of(((meta_ref[0] ^ code) // 2) * size, 16)
            move = pltpu.make_async_copy(
                part.at[number], weight.at[pl.ds(row, size), :], done.at[len(moves)]
            )
            move.start()
            moves.append(move)
    for move in moves:
        move.wait()
    for tokens_ref, sum_ref in zip((other_ref, mine_ref), sums):
        product = jnp.dot(tokens_ref[0], weight[:size, :], preferred_element_type=jnp.float32)
        for number in range(1, tokens_ref.shape[0]):
            product += jnp.dot(
                tokens_ref[number],
                weight[number * size : (number + 1) * size, :],
                preferred_element_type=jnp.float32,
            )
        sum_ref[...] = product.astype(sum_ref.dtype)


def latent_product(meta, mine, other, parts, codes):
    count, rows, size = mine.shape
    width = count * size
    columns = parts[0].shape[2]
    total = sum(len(group) for group in codes)
    inside = pl.BlockSpec(memory_space=pltpu.VMEM)
    return pl.pallas_call(
        functools.partial(latent_body, codes),
        in_specs=[pl.BlockSpec(memory_space=pltpu.SMEM), inside, inside]
        + [pl.BlockSpec(memory_space=pl.ANY)] * len(parts),
        out_specs=[inside, inside],
        out_shape=[
            jax.ShapeDtypeStruct((rows, columns), jnp.bfloat16),
            jax.ShapeDtypeStruct((rows, columns), jnp.float32),
        ],
        scratch_shapes=[
            pltpu.VMEM((width, columns), jnp.bfloat16),
            pltpu.SemaphoreType.DMA((total,)),
        ],
        compiler_params=pltpu.CompilerParams(vmem_limit_bytes=32 << 20),
        cost_estimate=pl.CostEstimate(
            flops=4 * rows * width * columns,
            bytes_accessed=2 * width * (2 * rows + columns),
            transcendentals=0,
        ),
        name="latent_product",
    )(meta, mine, other, *parts)


def latent_sums(meta, mine, other, parts, codes):
    if parts[0].shape[1] % 16 == 0:
        return latent_product(meta, mine, other, parts, codes)
    joined = jnp.concatenate(parts, axis=0)
    flat = jnp.array([code for group in codes for code in group], jnp.int32)
    order = jnp.argsort((flat ^ meta[0]) // 2)
    weight = joined[order]
    theirs, kept = [
        jnp.einsum("crs,csf->rf", half, weight, preferred_element_type=jnp.float32)
        for half in (other, mine)
    ]
    return theirs.astype(jnp.bfloat16), kept


def core_split_body(meta_ref, tokens_ref, mine_ref, other_ref):
    half = mine_ref.shape[2]
    low, high = tokens_ref[:, :half], tokens_ref[:, half:]

    @pl.when(meta_ref[0] % 2 == 0)
    def _():
        mine_ref[0], other_ref[0] = low, high

    @pl.when(meta_ref[0] % 2 == 1)
    def _():
        mine_ref[0], other_ref[0] = high, low


def core_split(meta, tokens, size):
    rows, width = tokens.shape
    count = width // size // 2
    out = pl.BlockSpec((1, rows, size), lambda n, meta_ref: (n, 0, 0))
    return pl.pallas_call(
        core_split_body,
        grid_spec=pltpu.PrefetchScalarGridSpec(
            num_scalar_prefetch=1,
            grid=(count,),
            in_specs=[pl.BlockSpec((rows, 2 * size), lambda n, meta_ref: (0, n))],
            out_specs=[out, out],
        ),
        out_shape=[jax.ShapeDtypeStruct((count, rows, size), jnp.bfloat16)] * 2,
        name="core_split",
    )(meta, tokens)


def token_halves(meta, tokens, size):
    if size % 64 == 0:
        return core_split(meta, tokens, size)
    rows, width = tokens.shape
    both = tokens.reshape(rows, width // size // 2, 2, size).transpose(2, 1, 0, 3)
    core = meta[0] % 2
    return both[core], both[1 - core]


def shards(
    tokens, lengths, latent_weight, latent_gain, expert_ids, gate_weights, gate_up, down_weight
):
    rows, width = tokens.shape
    rank_count = lax.axis_size("dp")
    rank = lax.axis_index("dp")
    experts = rank_count // GROUP
    pieces = rank_count // QUAD
    hidden_units = gate_up.shape[1] // 2
    length = lengths[rank]
    meta = rank.astype(jnp.int32).reshape(1)
    capacity = rows // experts + 2
    slots = -(-capacity // 8) * 8

    packed = pack(meta, lengths, expert_ids, tokens, experts, slots)
    columns = [[QUAD * s + low for s in range(pieces)] for low in range(QUAD)]
    mine, other = token_halves(meta, tokens, latent_weight.shape[0])

    half = latent_weight.shape[0] // 2
    middle = pieces == 4 and lax.axis_size("groups") == 2 and half % 16 == 0
    group = lax.axis_index("groups")
    first_group = group == 0
    sent = latent_weight[None]
    if middle:
        sent = lax.dynamic_slice_in_dim(sent, group * half, half, 1)
    latent_1 = swapped(sent, QUAD)
    packed = after(packed, latent_1)
    gate_2, mine, other = together(swapped(gate_up, 2), mine, swapped(other, 1))
    down_1 = swapped(down_weight, 1)
    arrived, gate_1, gate_3 = together(
        lax.all_to_all(packed, "dp", 0, 0, axis_index_groups=columns, tiled=True),
        swapped(gate_up, 1),
        swapped(gate_2, 1),
    )
    down_1 = after(down_1, gate_2)
    split = down_1.shape[0] // 2
    down_3 = [swapped(piece, 2) for piece in (down_1[:split], down_1[split:])]
    if middle:
        cut = swapped(after(jnp.concatenate([sent, latent_1], axis=0), arrived), 2 * QUAD)
    else:
        held, codes = jnp.concatenate([latent_weight[None], latent_1], axis=0), [0, QUAD]
        for level in range(3, rank_count.bit_length() - 1):
            held = jnp.concatenate([held, swapped(held, 1 << level)], axis=0)
            codes = codes + [code ^ (1 << level) for code in codes]

    weight_in = [gate_up, gate_1, gate_2, gate_3]
    theirs = gate_up_product(meta, arrived, weight_in, 1, jnp.bfloat16)
    ours = gate_up_product(meta, arrived, weight_in, 0, jnp.float32)
    if middle:
        ours, cut = together(ours, cut)
    down_3 = [after(piece, ours) for piece in down_3]
    down_2 = [swapped(piece, 1) for piece in down_3]
    came, *down_2 = together(swapped(theirs, QUAD), *down_2)
    summed = ours + came.astype(jnp.float32)
    hidden = (jax.nn.silu(summed[:, :hidden_units]) * summed[:, hidden_units:]).astype(jnp.bfloat16)

    partner = swapped(hidden, QUAD)
    if middle:
        mixed = jnp.concatenate([latent_1, cut], axis=0)
        swap = lax.ppermute(mixed, "groups", [(0, 1), (1, 0)])
    weight_out = [down_weight, down_1, *down_2, *down_3]
    (made_own,) = down_product(meta, hidden, weight_out, experts, True)
    halves = [[GROUP * e + low for e in range(experts)] for low in range(GROUP)]
    near = lax.all_to_all(made_own, "dp", 0, 0, axis_index_groups=halves, tiled=True)
    if middle:
        partner, swap = together(partner, swap)
    partner = after(partner, made_own)
    made = down_product(meta, partner, weight_out, experts, False)
    far = [swapped(made[n], QUAD * (2 * n + 1)) for n in range(experts)]
    if middle:
        full = jnp.where(
            first_group,
            jnp.concatenate([mixed, swap], axis=1),
            jnp.concatenate([swap, mixed], axis=1),
        )
        held = [jnp.concatenate([latent_weight[None], full[:1]], axis=0), full[1:]]
        codes = [[0, 4], [8, 12]]
    else:
        held, codes = [held], [codes]
    held = [after(block, partner) for block in held]
    latent_parts = held + [swapped(block, 2) for block in held]
    latent_codes = codes + [[code ^ 2 for code in group] for group in codes]
    given, kept = latent_sums(meta, mine, other, latent_parts, latent_codes)
    whose = (meta, lengths, expert_ids, gate_weights)
    moe_out = unpack(*whose, [near], width, True)
    projected = kept + swapped(after(given, moe_out), 1).astype(jnp.float32)
    latent_cache = latent_finish(projected, latent_gain, length)
    moe_out = unpack(*whose, far, width, False, [moe_out])
    return (latent_cache, moe_out)


def solution(mesh):
    placed = (
        P(("groups", "dp"), None),
        P("groups"),
        P("dp", None),
        P(),
        P(("groups", "dp"), None),
        P(("groups", "dp"), None),
        P("dp", None),
        P("dp", None),
    )
    return jax.shard_map(
        shards,
        mesh=mesh,
        in_specs=placed,
        out_specs=(P(("groups", "dp"), None), P(("groups", "dp"), None)),
        check_vma=False,
    )
```

```python
import functools

import jax
import jax.numpy as jnp
from jax import lax
from jax.experimental import pallas as pl
from jax.experimental.pallas import tpu as pltpu
from jax.sharding import PartitionSpec as P

GROUP = 8
QUAD = 4

rope_base = 10000.0
norm_eps = 1e-06


def swapped(block, bits):
    count = lax.axis_size("dp")
    return lax.ppermute(block, "dp", [(low, low ^ bits) for low in range(count)])


def slots_of_rows(rank_ref, lengths_ref, ids_row):
    rows = ids_row.shape[1]
    length = lengths_ref[rank_ref[0]]
    down = lax.broadcasted_iota(jnp.int32, (rows, rows), 0)
    along = lax.broadcasted_iota(jnp.int32, (rows, rows), 1)
    ids_column = jnp.sum(
        jnp.where(down == along, ids_row.astype(jnp.float32), 0.0), axis=1, keepdims=True
    ).astype(jnp.int32)
    return length, down, along, ids_column, ids_column == ids_row


def picks_by_slot(rank_ref, lengths_ref, ids_row, experts, size, picks_ref):
    rows = ids_row.shape[1]
    length, down, along, _, same = slots_of_rows(rank_ref, lengths_ref, ids_row)
    earlier = same & (down < along) & (down < length)
    place = jnp.sum(earlier.astype(jnp.float32), axis=0, keepdims=True).astype(jnp.int32)
    live = lax.broadcasted_iota(jnp.int32, (1, rows), 1) < length
    chosen = jnp.where(live, ids_row, -1)
    slot = lax.broadcasted_iota(jnp.int32, (size, rows), 0)
    for expert in range(experts):
        hit = (place == slot) & (chosen == expert)
        picks_ref[expert] = hit.astype(jnp.float32).astype(jnp.bfloat16)


def picks_by_row(rank_ref, lengths_ref, ids_row, experts, size, picks_ref):
    rows = ids_row.shape[1]
    length, down, along, ids_column, same = slots_of_rows(rank_ref, lengths_ref, ids_row)
    earlier = same & (along < down) & (along < length)
    place = jnp.sum(earlier.astype(jnp.float32), axis=1, keepdims=True).astype(jnp.int32)
    live = lax.broadcasted_iota(jnp.int32, (rows, 1), 0) < length
    chosen = jnp.where(live, ids_column, -1)
    slot = lax.broadcasted_iota(jnp.int32, (rows, size), 1)
    for expert in range(experts):
        hit = (place == slot) & (chosen == expert)
        picks_ref[expert] = hit.astype(jnp.float32).astype(jnp.bfloat16)


def pack_body(rank_ref, lengths_ref, ids_ref, low_ref, high_ref, out_ref, picks_ref):
    experts, size, _ = picks_ref.shape

    @pl.when(pl.program_id(0) == 0)
    def _():
        picks_by_slot(rank_ref, lengths_ref, ids_ref[...], experts, size, picks_ref)

    for side, source_ref in enumerate((low_ref, high_ref)):
        for expert in range(experts):
            out_ref[2 * expert + side] = jnp.dot(
                picks_ref[expert], source_ref[...], preferred_element_type=jnp.float32
            ).astype(jnp.bfloat16)


def pack(rank_array, lengths, ids, tokens, experts, size):
    rows, width = tokens.shape
    part = width // GROUP

    def column_of(side):
        return lambda k, rank_ref, lengths_ref: (0, side * QUAD + ((rank_ref[0] % QUAD) ^ k))

    whole = lambda k, rank_ref, lengths_ref: (0, 0)
    return pl.pallas_call(
        pack_body,
        grid_spec=pltpu.PrefetchScalarGridSpec(
            num_scalar_prefetch=2,
            grid=(QUAD,),
            in_specs=[
                pl.BlockSpec((1, rows), whole),
                pl.BlockSpec((rows, part), column_of(0)),
                pl.BlockSpec((rows, part), column_of(1)),
            ],
            out_specs=pl.BlockSpec(
                (2 * experts, size, part), lambda k, rank_ref, lengths_ref: (0, 0, k)
            ),
            scratch_shapes=[pltpu.VMEM((experts, size, rows), jnp.bfloat16)],
        ),
        out_shape=jax.ShapeDtypeStruct((2 * experts, size, QUAD * part), jnp.bfloat16),
        compiler_params=pltpu.CompilerParams(vmem_limit_bytes=58 << 20),
        cost_estimate=pl.CostEstimate(
            flops=4 * rows * rows * width, bytes_accessed=4 * rows * width, transcendentals=0
        ),
        name="pack_rows",
    )(rank_array, lengths, ids.reshape(1, rows), tokens, tokens)


def unpack_body(near, rank_ref, lengths_ref, ids_ref, gate_ref, *refs):
    out_ref, picks_ref, gate_column_ref = refs[-3:]
    experts, rows, size = picks_ref.shape
    my_expert = rank_ref[0] // GROUP

    @pl.when(pl.program_id(0) == 0)
    def _():
        picks_by_row(rank_ref, lengths_ref, ids_ref[...], experts, size, picks_ref)
        down = lax.broadcasted_iota(jnp.int32, (rows, rows), 0)
        along = lax.broadcasted_iota(jnp.int32, (rows, rows), 1)
        gate_column_ref[...] = jnp.sum(
            jnp.where(down == along, gate_ref[...], 0.0), axis=1, keepdims=True
        )

    total = jnp.zeros(out_ref.shape, jnp.float32)
    for number in range(experts):
        expert = my_expert ^ number
        part = refs[1][expert] if near and number else refs[number][...]
        total += jnp.dot(picks_ref[expert], part, preferred_element_type=jnp.float32)
    out_ref[...] = (total * gate_column_ref[...]).astype(jnp.bfloat16)


def unpack(rank_array, lengths, ids, gates, parts, width, near, base=()):
    rows = ids.shape[0]
    part = width // GROUP
    size = parts[0].shape[-2]
    experts = parts[1].shape[0] if near else len(parts)

    def out_index(k, rank_ref, lengths_ref):
        quarter = rank_ref[0] % QUAD
        high = (rank_ref[0] // QUAD) % 2
        return (0, (high if near else 1 - high) * QUAD + (quarter ^ k))

    whole = lambda k, rank_ref, lengths_ref: (0, 0)
    specs = [pl.BlockSpec((size, part), lambda k, rank_ref, lengths_ref: (0, k))] * experts
    if near:
        both = pl.BlockSpec((experts, size, part), lambda k, rank_ref, lengths_ref: (0, 0, k))
        specs = [specs[0], both]
    return pl.pallas_call(
        functools.partial(unpack_body, near),
        grid_spec=pltpu.PrefetchScalarGridSpec(
            num_scalar_prefetch=2,
            grid=(QUAD,),
            in_specs=[pl.BlockSpec((1, rows), whole), pl.BlockSpec((1, rows), whole)]
            + specs
            + [pl.BlockSpec(memory_space=pl.ANY)] * len(base),
            out_specs=pl.BlockSpec((rows, part), out_index),
            scratch_shapes=[
                pltpu.VMEM((experts, rows, size), jnp.bfloat16),
                pltpu.VMEM((rows, 1), jnp.float32),
            ],
        ),
        out_shape=jax.ShapeDtypeStruct((rows, width), jnp.bfloat16),
        input_output_aliases={4 + len(specs): 0} if base else {},
        compiler_params=pltpu.CompilerParams(vmem_limit_bytes=58 << 20),
        cost_estimate=pl.CostEstimate(
            flops=2 * rows * rows * width, bytes_accessed=2 * rows * width, transcendentals=0
        ),
        name="unpack_rows",
    )(rank_array, lengths, ids.reshape(1, rows), gates.reshape(1, rows), *parts, *base)


def idle_body(*refs):
    del refs


def after(value, *events):
    anywhere = pl.BlockSpec(memory_space=pl.ANY)
    return pl.pallas_call(
        idle_body,
        in_specs=[anywhere] * (1 + len(events)),
        out_specs=anywhere,
        out_shape=jax.ShapeDtypeStruct(value.shape, value.dtype),
        input_output_aliases={0: 0},
        name="after",
    )(value, *events)


def together(*values):
    anywhere = pl.BlockSpec(memory_space=pl.ANY)
    return pl.pallas_call(
        idle_body,
        in_specs=[anywhere] * len(values),
        out_specs=[anywhere] * len(values),
        out_shape=[jax.ShapeDtypeStruct(value.shape, value.dtype) for value in values],
        input_output_aliases={number: number for number in range(len(values))},
        name="together",
    )(*values)


def gate_up_body(groups, meta_ref, *refs):
    del meta_ref
    count = sum(groups)
    parts, shares = refs[:count], refs[count : count + QUAD]
    outs, joined = refs[count + QUAD : -1], refs[-1]
    size = parts[0].shape[1]
    depth = shares[0].shape[0]

    @pl.when(pl.program_id(0) == 0)
    def _():
        for number, part in enumerate(parts):
            joined[pl.ds(number * size, size), :] = part[0]

    total = jnp.dot(joined[:, :depth], shares[0][...], preferred_element_type=jnp.float32)
    for k in range(1, QUAD):
        total += jnp.dot(
            joined[:, k * depth : (k + 1) * depth],
            shares[k][...],
            preferred_element_type=jnp.float32,
        )
    start = 0
    for group, out_ref in zip(groups, outs):
        out_ref[...] = total[start : start + group * size].astype(out_ref.dtype)
        start += group * size


def gate_up_product(meta, arrived, shares, groups):
    _, size, width = arrived.shape
    depth, columns = shares[0].shape
    tile = columns // 4
    rows = size * sum(len(numbers) for numbers, _, _ in groups)

    def source(number, side):
        def index(n, meta_ref):
            rank = meta_ref[0]
            return (2 * ((rank // GROUP) ^ number) + (((rank // QUAD) % 2) ^ side), 0, 0)

        return index

    across = lambda n, meta_ref: (0, n)
    picked = [source(number, side) for numbers, side, _ in groups for number in numbers]
    heights = [size * len(numbers) for numbers, _, _ in groups]
    return pl.pallas_call(
        functools.partial(gate_up_body, [len(numbers) for numbers, _, _ in groups]),
        grid_spec=pltpu.PrefetchScalarGridSpec(
            num_scalar_prefetch=1,
            grid=(columns // tile,),
            in_specs=[pl.BlockSpec((1, size, width), index) for index in picked]
            + [pl.BlockSpec((depth, tile), across) for _ in shares],
            out_specs=[pl.BlockSpec((height, tile), across) for height in heights],
            scratch_shapes=[pltpu.VMEM((rows, width), jnp.bfloat16)],
        ),
        out_shape=[
            jax.ShapeDtypeStruct((height, columns), dtype)
            for height, (_, _, dtype) in zip(heights, groups)
        ],
        compiler_params=pltpu.CompilerParams(vmem_limit_bytes=32 << 20),
        cost_estimate=pl.CostEstimate(
            flops=2 * rows * width * columns,
            bytes_accessed=2 * width * (rows + columns),
            transcendentals=0,
        ),
        name="gate_up_product",
    )(meta, *[arrived] * len(picked), *shares)


def down_body(places, joined, meta_ref, hidden_ref, *refs):
    k = pl.program_id(0)
    weight, done = refs[-2:]
    pieces, outs = refs[: len(places)], refs[len(places) : -2]
    count = outs[0].shape[0] - 1 if joined else len(outs)
    size = hidden_ref.shape[0] // count
    mine = meta_ref[0] // GROUP
    moves = []
    for number, (piece, (turn, start)) in enumerate(zip(pieces, places)):
        target = weight.at[turn, pl.ds(start, piece.shape[0]), :]
        moves.append(pltpu.make_async_copy(piece, target, done.at[number]))

    @pl.when(k == 0)
    def _():
        for move in moves:
            move.start()

    for turn in range(QUAD):

        @pl.when(k == turn)
        def _(turn=turn):
            for move, place in zip(moves, places):
                if place[0] == turn:
                    move.wait()

    made = jnp.dot(hidden_ref[...], weight[k], preferred_element_type=jnp.float32)
    for number in range(count):
        rows = made[number * size : (number + 1) * size].astype(jnp.bfloat16)
        if joined:
            outs[0][mine ^ (number + 1)] = rows
        else:
            outs[number][...] = rows


def down_product(meta, hidden, shares, count, joined):
    rows, depth = hidden.shape
    part = shares[0].shape[1]
    size = rows // count
    places, filled = [], 0
    for share in shares:
        places.append((filled // depth, filled % depth))
        filled += share.shape[0]
    whole = lambda k, meta_ref: (0, 0)
    if joined:
        out_specs = [pl.BlockSpec((count + 1, size, part), lambda k, meta_ref: (0, 0, k))]
        shapes = [(count + 1, size, QUAD * part)]
    else:
        out_specs = [pl.BlockSpec((size, part), lambda k, meta_ref: (0, k))] * count
        shapes = [(size, QUAD * part)] * count
    return pl.pallas_call(
        functools.partial(down_body, places, joined),
        grid_spec=pltpu.PrefetchScalarGridSpec(
            num_scalar_prefetch=1,
            grid=(QUAD,),
            in_specs=[pl.BlockSpec((rows, depth), whole)]
            + [pl.BlockSpec(memory_space=pl.ANY)] * len(shares),
            out_specs=out_specs,
            scratch_shapes=[
                pltpu.VMEM((QUAD, depth, part), jnp.bfloat16),
                pltpu.SemaphoreType.DMA((len(shares),)),
            ],
        ),
        out_shape=[jax.ShapeDtypeStruct(shape, jnp.bfloat16) for shape in shapes],
        compiler_params=pltpu.CompilerParams(vmem_limit_bytes=58 << 20),
        cost_estimate=pl.CostEstimate(
            flops=2 * rows * depth * QUAD * part,
            bytes_accessed=2 * (rows * depth + QUAD * part * (rows + depth)),
            transcendentals=0,
        ),
        name="down_product",
    )(meta, hidden, *shares)


def latent_finish(projected, gain, length):
    lat_width = gain.shape[0]
    compressed = projected[:, :lat_width]
    rotary = projected[:, lat_width:]
    inverse_rms = lax.rsqrt(jnp.mean(compressed * compressed, axis=1, keepdims=True) + norm_eps)
    normed = compressed * inverse_rms * gain[None, :]
    half_cols = rotary.shape[1] // 2
    positions = jnp.arange(projected.shape[0], dtype=jnp.int32)
    frequency = rope_base ** (-jnp.arange(half_cols, dtype=jnp.float32) / half_cols)
    angles = positions.astype(jnp.float32)[:, None] * frequency[None, :]
    cosine = jnp.cos(angles)
    sine_part = jnp.sin(angles)
    left_half = rotary[:, :half_cols]
    right_half = rotary[:, half_cols:]
    turned = jnp.concatenate(
        [left_half * cosine - right_half * sine_part, left_half * sine_part + right_half * cosine],
        axis=1,
    )
    result = jnp.concatenate([normed, turned], axis=1)
    return jnp.where((positions < length)[:, None], result, 0.0).astype(jnp.bfloat16)


def latent_body(codes, meta_ref, mine_ref, other_ref, *refs):
    parts, sums, weight, done = refs[: len(codes)], refs[len(codes) : -2], refs[-2], refs[-1]
    size = parts[0].shape[1]
    moves = []
    for part, group in zip(parts, codes):
        for number, code in enumerate(group):
            row = pl.multiple_of(((meta_ref[0] ^ code) // 2) * size, 16)
            move = pltpu.make_async_copy(
                part.at[number], weight.at[pl.ds(row, size), :], done.at[len(moves)]
            )
            move.start()
            moves.append(move)
    for move in moves:
        move.wait()
    for tokens_ref, sum_ref in zip((other_ref, mine_ref), sums):
        product = jnp.dot(tokens_ref[0], weight[:size, :], preferred_element_type=jnp.float32)
        for number in range(1, tokens_ref.shape[0]):
            product += jnp.dot(
                tokens_ref[number],
                weight[number * size : (number + 1) * size, :],
                preferred_element_type=jnp.float32,
            )
        sum_ref[...] = product.astype(sum_ref.dtype)


def latent_product(meta, mine, other, parts, codes):
    count, rows, size = mine.shape
    width = count * size
    columns = parts[0].shape[2]
    total = sum(len(group) for group in codes)
    inside = pl.BlockSpec(memory_space=pltpu.VMEM)
    return pl.pallas_call(
        functools.partial(latent_body, codes),
        in_specs=[pl.BlockSpec(memory_space=pltpu.SMEM), inside, inside]
        + [pl.BlockSpec(memory_space=pl.ANY)] * len(parts),
        out_specs=[inside, inside],
        out_shape=[
            jax.ShapeDtypeStruct((rows, columns), jnp.bfloat16),
            jax.ShapeDtypeStruct((rows, columns), jnp.float32),
        ],
        scratch_shapes=[
            pltpu.VMEM((width, columns), jnp.bfloat16),
            pltpu.SemaphoreType.DMA((total,)),
        ],
        compiler_params=pltpu.CompilerParams(vmem_limit_bytes=32 << 20),
        cost_estimate=pl.CostEstimate(
            flops=4 * rows * width * columns,
            bytes_accessed=2 * width * (2 * rows + columns),
            transcendentals=0,
        ),
        name="latent_product",
    )(meta, mine, other, *parts)


def latent_sums(meta, mine, other, parts, codes):
    if parts[0].shape[1] % 16 == 0:
        return latent_product(meta, mine, other, parts, codes)
    joined = jnp.concatenate(parts, axis=0)
    flat = jnp.array([code for group in codes for code in group], jnp.int32)
    order = jnp.argsort((flat ^ meta[0]) // 2)
    weight = joined[order]
    theirs, kept = [
        jnp.einsum("crs,csf->rf", half, weight, preferred_element_type=jnp.float32)
        for half in (other, mine)
    ]
    return theirs.astype(jnp.bfloat16), kept


def core_split_body(meta_ref, tokens_ref, mine_ref, other_ref):
    half = mine_ref.shape[2]
    low, high = tokens_ref[:, :half], tokens_ref[:, half:]

    @pl.when(meta_ref[0] % 2 == 0)
    def _():
        mine_ref[0], other_ref[0] = low, high

    @pl.when(meta_ref[0] % 2 == 1)
    def _():
        mine_ref[0], other_ref[0] = high, low


def core_split(meta, tokens, size):
    rows, width = tokens.shape
    count = width // size // 2
    out = pl.BlockSpec((1, rows, size), lambda n, meta_ref: (n, 0, 0))
    return pl.pallas_call(
        core_split_body,
        grid_spec=pltpu.PrefetchScalarGridSpec(
            num_scalar_prefetch=1,
            grid=(count,),
            in_specs=[pl.BlockSpec((rows, 2 * size), lambda n, meta_ref: (0, n))],
            out_specs=[out, out],
        ),
        out_shape=[jax.ShapeDtypeStruct((count, rows, size), jnp.bfloat16)] * 2,
        name="core_split",
    )(meta, tokens)


def token_halves(meta, tokens, size):
    if size % 64 == 0:
        return core_split(meta, tokens, size)
    rows, width = tokens.shape
    both = tokens.reshape(rows, width // size // 2, 2, size).transpose(2, 1, 0, 3)
    core = meta[0] % 2
    return both[core], both[1 - core]


def shards(
    tokens, lengths, latent_weight, latent_gain, expert_ids, gate_weights, gate_up, down_weight
):
    rows, width = tokens.shape
    rank_count = lax.axis_size("dp")
    rank = lax.axis_index("dp")
    experts = rank_count // GROUP
    pieces = rank_count // QUAD
    hidden_units = gate_up.shape[1] // 2
    length = lengths[rank]
    meta = rank.astype(jnp.int32).reshape(1)
    capacity = rows // experts + 2
    slots = -(-capacity // 8) * 8

    packed = pack(meta, lengths, expert_ids, tokens, experts, slots)
    columns = [[QUAD * s + low for s in range(pieces)] for low in range(QUAD)]
    mine, other = token_halves(meta, tokens, latent_weight.shape[0])

    half = latent_weight.shape[0] // 2
    middle = pieces == 4 and lax.axis_size("groups") == 2 and half % 16 == 0
    group = lax.axis_index("groups")
    first_group = group == 0
    sent = latent_weight[None]
    if middle:
        sent = lax.dynamic_slice_in_dim(sent, group * half, half, 1)
    latent_1 = swapped(sent, QUAD)
    packed = after(packed, latent_1)
    gate_2, mine, other = together(swapped(gate_up, 2), mine, swapped(other, 1))
    down_1 = swapped(down_weight, 1)
    arrived, gate_1, gate_3 = together(
        lax.all_to_all(packed, "dp", 0, 0, axis_index_groups=columns, tiled=True),
        swapped(gate_up, 1),
        swapped(gate_2, 1),
    )
    down_1 = after(down_1, gate_2)
    down_3 = swapped(down_1, 2)
    if middle:
        cut = swapped(after(jnp.concatenate([sent, latent_1], axis=0), arrived), 2 * QUAD)
    else:
        held, codes = jnp.concatenate([latent_weight[None], latent_1], axis=0), [0, QUAD]
        for level in range(3, rank_count.bit_length() - 1):
            held = jnp.concatenate([held, swapped(held, 1 << level)], axis=0)
            codes = codes + [code ^ (1 << level) for code in codes]

    weight_in = [gate_up, gate_1, gate_2, gate_3]
    away = list(range(1, experts))
    (theirs,) = gate_up_product(meta, arrived, weight_in, [(away, 1, jnp.bfloat16)])
    ours, theirs_near, ours_near = gate_up_product(
        meta,
        arrived,
        weight_in,
        [(away, 0, jnp.float32), ([0], 1, jnp.bfloat16), ([0], 0, jnp.float32)],
    )
    if middle:
        ours, cut = together(ours, cut)
    down_3 = after(down_3, ours)
    split = down_3.shape[0] // 4
    down_2 = [swapped(down_3[n * split : (n + 1) * split], 1) for n in range(4)]
    came, *down_2 = together(swapped(theirs, QUAD), *down_2)
    weight_out = [down_weight, down_1, *down_2, down_3]

    def activated(own, other):
        summed = own + other.astype(jnp.float32)
        gate, up = summed[:, :hidden_units], summed[:, hidden_units:]
        return (jax.nn.silu(gate) * up).astype(jnp.bfloat16)

    hidden = activated(ours, came)
    partner = swapped(hidden, QUAD)
    (made_own,) = down_product(meta, hidden, weight_out, experts - 1, True)
    halves = [[GROUP * e + low for e in range(experts)] for low in range(GROUP)]
    near = lax.all_to_all(made_own, "dp", 0, 0, axis_index_groups=halves, tiled=True)
    partner = after(partner, made_own)
    made = down_product(meta, partner, weight_out, experts - 1, False)
    far = [swapped(made[n - 1], QUAD * (2 * n + 1)) for n in away]

    came_near = after(swapped(after(theirs_near, hidden), QUAD), made[0])
    hidden_near = activated(ours_near, came_near)
    both = jnp.concatenate([hidden_near, swapped(hidden_near, QUAD)], axis=0)
    here, there = down_product(meta, both, weight_out, 2, False)
    near = [here, near]
    far = [swapped(there, QUAD)] + far

    if middle:
        mixed = after(jnp.concatenate([latent_1, cut], axis=0), hidden)
        swap = lax.ppermute(mixed, "groups", [(0, 1), (1, 0)])
        full = jnp.where(
            first_group,
            jnp.concatenate([mixed, swap], axis=1),
            jnp.concatenate([swap, mixed], axis=1),
        )
        held = [jnp.concatenate([latent_weight[None], full[:1]], axis=0), full[1:]]
        codes = [[0, 4], [8, 12]]
    else:
        held, codes = [held], [codes]
    latent_parts = held + [swapped(block, 2) for block in held]
    latent_codes = codes + [[code ^ 2 for code in group] for group in codes]
    given, kept = latent_sums(meta, mine, other, latent_parts, latent_codes)
    whose = (meta, lengths, expert_ids, gate_weights)
    moe_out = unpack(*whose, near, width, True)
    projected = kept + swapped(after(given, moe_out), 1).astype(jnp.float32)
    latent_cache = latent_finish(projected, latent_gain, length)
    moe_out = unpack(*whose, far, width, False, [moe_out])
    return (latent_cache, moe_out)


def solution(mesh):
    placed = (
        P(("groups", "dp"), None),
        P("groups"),
        P("dp", None),
        P(),
        P(("groups", "dp"), None),
        P(("groups", "dp"), None),
        P("dp", None),
        P("dp", None),
    )
    return jax.shard_map(
        shards,
        mesh=mesh,
        in_specs=placed,
        out_specs=(P(("groups", "dp"), None), P(("groups", "dp"), None)),
        check_vma=False,
    )
```

```python
import functools

import jax
import jax.numpy as jnp
from jax import lax
from jax.experimental import pallas as pl
from jax.experimental.pallas import tpu as pltpu
from jax.sharding import PartitionSpec as P

GROUP = 8
QUAD = 4

rope_base = 10000.0
norm_eps = 1e-06


def swapped(block, bits):
    count = lax.axis_size("dp")
    return lax.ppermute(block, "dp", [(low, low ^ bits) for low in range(count)])


def slots_of_rows(rank_ref, lengths_ref, ids_row):
    rows = ids_row.shape[1]
    length = lengths_ref[rank_ref[0]]
    down = lax.broadcasted_iota(jnp.int32, (rows, rows), 0)
    along = lax.broadcasted_iota(jnp.int32, (rows, rows), 1)
    ids_column = jnp.sum(
        jnp.where(down == along, ids_row.astype(jnp.float32), 0.0), axis=1, keepdims=True
    ).astype(jnp.int32)
    return length, down, along, ids_column, ids_column == ids_row


def picks_by_slot(rank_ref, lengths_ref, ids_row, experts, size, picks_ref):
    rows = ids_row.shape[1]
    length, down, along, _, same = slots_of_rows(rank_ref, lengths_ref, ids_row)
    earlier = same & (down < along) & (down < length)
    place = jnp.sum(earlier.astype(jnp.float32), axis=0, keepdims=True).astype(jnp.int32)
    live = lax.broadcasted_iota(jnp.int32, (1, rows), 1) < length
    chosen = jnp.where(live, ids_row, -1)
    slot = lax.broadcasted_iota(jnp.int32, (size, rows), 0)
    for expert in range(experts):
        hit = (place == slot) & (chosen == expert)
        picks_ref[pl.ds(expert * size, size), :] = hit.astype(jnp.float32).astype(jnp.bfloat16)


def picks_by_row(rank_ref, lengths_ref, ids_row, experts, size, picks_ref):
    rows = ids_row.shape[1]
    length, down, along, ids_column, same = slots_of_rows(rank_ref, lengths_ref, ids_row)
    earlier = same & (along < down) & (along < length)
    place = jnp.sum(earlier.astype(jnp.float32), axis=1, keepdims=True).astype(jnp.int32)
    live = lax.broadcasted_iota(jnp.int32, (rows, 1), 0) < length
    chosen = jnp.where(live, ids_column, -1)
    slot = lax.broadcasted_iota(jnp.int32, (rows, size), 1)
    for expert in range(experts):
        hit = (place == slot) & (chosen == expert)
        picks_ref[expert] = hit.astype(jnp.float32).astype(jnp.bfloat16)


def pack_body(rank_ref, lengths_ref, ids_ref, tokens_ref, out_ref, rows_in, rows_out, picks_ref, came, went):
    _, experts, size, part = rows_out.shape
    quarter = rank_ref[0] % QUAD

    def fetch(turn):
        block = turn % 2 * QUAD + (quarter ^ (turn // 2))
        column = pl.multiple_of(block * part, 128)
        return pltpu.make_async_copy(
            tokens_ref.at[:, pl.ds(column, part)], rows_in.at[turn], came.at[turn]
        )

    def send(turn, expert):
        to = 2 * expert + turn % 2
        return pltpu.make_async_copy(
            rows_out.at[turn, expert],
            out_ref.at[to, :, pl.ds(turn // 2 * part, part)],
            went.at[turn, expert],
        )

    for turn in range(GROUP):
        fetch(turn).start()
    picks_by_slot(rank_ref, lengths_ref, ids_ref[...], experts, size, picks_ref)
    for turn in range(GROUP):
        fetch(turn).wait()
        made = jnp.dot(picks_ref[...], rows_in[turn], preferred_element_type=jnp.float32)
        for expert in range(experts):
            rows = made[expert * size : (expert + 1) * size]
            rows_out[turn, expert] = rows.astype(jnp.bfloat16)
            send(turn, expert).start()
    for turn in range(GROUP):
        for expert in range(experts):
            send(turn, expert).wait()


def pack(rank_array, lengths, ids, tokens, experts, size):
    rows, width = tokens.shape
    part = width // GROUP
    return pl.pallas_call(
        pack_body,
        grid_spec=pltpu.PrefetchScalarGridSpec(
            num_scalar_prefetch=2,
            grid=(),
            in_specs=[
                pl.BlockSpec(memory_space=pltpu.VMEM),
                pl.BlockSpec(memory_space=pl.ANY),
            ],
            out_specs=pl.BlockSpec(memory_space=pl.ANY),
            scratch_shapes=[
                pltpu.VMEM((GROUP, rows, part), jnp.bfloat16),
                pltpu.VMEM((GROUP, experts, size, part), jnp.bfloat16),
                pltpu.VMEM((experts * size, rows), jnp.bfloat16),
                pltpu.SemaphoreType.DMA((GROUP,)),
                pltpu.SemaphoreType.DMA((GROUP, experts)),
            ],
        ),
        out_shape=jax.ShapeDtypeStruct((2 * experts, size, QUAD * part), jnp.bfloat16),
        compiler_params=pltpu.CompilerParams(vmem_limit_bytes=58 << 20),
        cost_estimate=pl.CostEstimate(
            flops=4 * rows * rows * width, bytes_accessed=4 * rows * width, transcendentals=0
        ),
        name="pack_rows",
    )(rank_array, lengths, ids.reshape(1, rows), tokens)


def unpack_body(near, rank_ref, lengths_ref, ids_ref, gate_ref, *refs):
    out_ref, parts_in, rows_out, picks_ref, came, went = refs[-6:]
    experts, rows, size = picks_ref.shape
    part = rows_out.shape[2]
    my_expert = rank_ref[0] // GROUP
    quarter = rank_ref[0] % QUAD
    high = (rank_ref[0] // QUAD) % 2
    side = high if near else 1 - high

    def fetch(k, number):
        columns = pl.ds(k * part, part)
        if near and number:
            source = refs[1].at[my_expert ^ number, :, columns]
        else:
            source = refs[number].at[:, columns]
        return pltpu.make_async_copy(source, parts_in.at[k, number], came.at[k, number])

    def send(k):
        column = pl.multiple_of((side * QUAD + (quarter ^ k)) * part, 128)
        return pltpu.make_async_copy(
            rows_out.at[k], out_ref.at[:, pl.ds(column, part)], went.at[k]
        )

    for k in range(QUAD):
        for number in range(experts):
            fetch(k, number).start()
    picks_by_row(rank_ref, lengths_ref, ids_ref[...], experts, size, picks_ref)
    down = lax.broadcasted_iota(jnp.int32, (rows, rows), 0)
    along = lax.broadcasted_iota(jnp.int32, (rows, rows), 1)
    gate = jnp.sum(jnp.where(down == along, gate_ref[...], 0.0), axis=1, keepdims=True)
    for k in range(QUAD):
        total = jnp.zeros((rows, part), jnp.float32)
        for number in range(experts):
            fetch(k, number).wait()
            total += jnp.dot(
                picks_ref[my_expert ^ number],
                parts_in[k, number],
                preferred_element_type=jnp.float32,
            )
        rows_out[k] = (total * gate).astype(jnp.bfloat16)
        send(k).start()
    for k in range(QUAD):
        send(k).wait()


def unpack(rank_array, lengths, ids, gates, parts, width, near, base=()):
    rows = ids.shape[0]
    part = width // GROUP
    size = parts[0].shape[-2]
    experts = parts[1].shape[0] if near else len(parts)
    inside = pl.BlockSpec(memory_space=pltpu.VMEM)
    anywhere = pl.BlockSpec(memory_space=pl.ANY)
    return pl.pallas_call(
        functools.partial(unpack_body, near),
        grid_spec=pltpu.PrefetchScalarGridSpec(
            num_scalar_prefetch=2,
            grid=(),
            in_specs=[inside, inside] + [anywhere] * (len(parts) + len(base)),
            out_specs=anywhere,
            scratch_shapes=[
                pltpu.VMEM((QUAD, experts, size, part), jnp.bfloat16),
                pltpu.VMEM((QUAD, rows, part), jnp.bfloat16),
                pltpu.VMEM((experts, rows, size), jnp.bfloat16),
                pltpu.SemaphoreType.DMA((QUAD, experts)),
                pltpu.SemaphoreType.DMA((QUAD,)),
            ],
        ),
        out_shape=jax.ShapeDtypeStruct((rows, width), jnp.bfloat16),
        input_output_aliases={4 + len(parts): 0} if base else {},
        compiler_params=pltpu.CompilerParams(vmem_limit_bytes=58 << 20),
        cost_estimate=pl.CostEstimate(
            flops=2 * rows * rows * width, bytes_accessed=2 * rows * width, transcendentals=0
        ),
        name="unpack_rows",
    )(rank_array, lengths, ids.reshape(1, rows), gates.reshape(1, rows), *parts, *base)


def idle_body(*refs):
    del refs


def after(value, *events):
    anywhere = pl.BlockSpec(memory_space=pl.ANY)
    return pl.pallas_call(
        idle_body,
        in_specs=[anywhere] * (1 + len(events)),
        out_specs=anywhere,
        out_shape=jax.ShapeDtypeStruct(value.shape, value.dtype),
        input_output_aliases={0: 0},
        name="after",
    )(value, *events)


def together(*values):
    anywhere = pl.BlockSpec(memory_space=pl.ANY)
    return pl.pallas_call(
        idle_body,
        in_specs=[anywhere] * len(values),
        out_specs=[anywhere] * len(values),
        out_shape=[jax.ShapeDtypeStruct(value.shape, value.dtype) for value in values],
        input_output_aliases={number: number for number in range(len(values))},
        name="together",
    )(*values)


def gate_up_body(groups, meta_ref, *refs):
    del meta_ref
    count = sum(groups)
    parts, shares = refs[:count], refs[count : count + QUAD]
    outs, joined = refs[count + QUAD : -1], refs[-1]
    size = parts[0].shape[1]
    depth = shares[0].shape[0]

    @pl.when(pl.program_id(0) == 0)
    def _():
        for number, part in enumerate(parts):
            joined[pl.ds(number * size, size), :] = part[0]

    total = jnp.dot(joined[:, :depth], shares[0][...], preferred_element_type=jnp.float32)
    for k in range(1, QUAD):
        total += jnp.dot(
            joined[:, k * depth : (k + 1) * depth],
            shares[k][...],
            preferred_element_type=jnp.float32,
        )
    start = 0
    for group, out_ref in zip(groups, outs):
        out_ref[...] = total[start : start + group * size].astype(out_ref.dtype)
        start += group * size


def gate_up_product(meta, arrived, shares, groups):
    _, size, width = arrived.shape
    depth, columns = shares[0].shape
    tile = columns // 4
    rows = size * sum(len(numbers) for numbers, _, _ in groups)

    def source(number, side):
        def index(n, meta_ref):
            rank = meta_ref[0]
            return (2 * ((rank // GROUP) ^ number) + (((rank // QUAD) % 2) ^ side), 0, 0)

        return index

    across = lambda n, meta_ref: (0, n)
    picked = [source(number, side) for numbers, side, _ in groups for number in numbers]
    heights = [size * len(numbers) for numbers, _, _ in groups]
    return pl.pallas_call(
        functools.partial(gate_up_body, [len(numbers) for numbers, _, _ in groups]),
        grid_spec=pltpu.PrefetchScalarGridSpec(
            num_scalar_prefetch=1,
            grid=(columns // tile,),
            in_specs=[pl.BlockSpec((1, size, width), index) for index in picked]
            + [pl.BlockSpec((depth, tile), across) for _ in shares],
            out_specs=[pl.BlockSpec((height, tile), across) for height in heights],
            scratch_shapes=[pltpu.VMEM((rows, width), jnp.bfloat16)],
        ),
        out_shape=[
            jax.ShapeDtypeStruct((height, columns), dtype)
            for height, (_, _, dtype) in zip(heights, groups)
        ],
        compiler_params=pltpu.CompilerParams(vmem_limit_bytes=32 << 20),
        cost_estimate=pl.CostEstimate(
            flops=2 * rows * width * columns,
            bytes_accessed=2 * width * (rows + columns),
            transcendentals=0,
        ),
        name="gate_up_product",
    )(meta, *[arrived] * len(picked), *shares)


def down_body(places, joined, meta_ref, hidden_ref, *refs):
    k = pl.program_id(0)
    weight, done = refs[-2:]
    pieces, outs = refs[: len(places)], refs[len(places) : -2]
    count = outs[0].shape[0] - 1 if joined else len(outs)
    size = hidden_ref.shape[0] // count
    mine = meta_ref[0] // GROUP
    moves = []
    for number, (piece, (turn, start)) in enumerate(zip(pieces, places)):
        target = weight.at[turn, pl.ds(start, piece.shape[0]), :]
        moves.append(pltpu.make_async_copy(piece, target, done.at[number]))

    @pl.when(k == 0)
    def _():
        for move in moves:
            move.start()

    for turn in range(QUAD):

        @pl.when(k == turn)
        def _(turn=turn):
            for move, place in zip(moves, places):
                if place[0] == turn:
                    move.wait()

    made = jnp.dot(hidden_ref[...], weight[k], preferred_element_type=jnp.float32)
    for number in range(count):
        rows = made[number * size : (number + 1) * size].astype(jnp.bfloat16)
        if joined:
            outs[0][mine ^ (number + 1)] = rows
        else:
            outs[number][...] = rows


def down_product(meta, hidden, shares, count, joined):
    rows, depth = hidden.shape
    part = shares[0].shape[1]
    size = rows // count
    places, filled = [], 0
    for share in shares:
        places.append((filled // depth, filled % depth))
        filled += share.shape[0]
    whole = lambda k, meta_ref: (0, 0)
    if joined:
        out_specs = [pl.BlockSpec((count + 1, size, part), lambda k, meta_ref: (0, 0, k))]
        shapes = [(count + 1, size, QUAD * part)]
    else:
        out_specs = [pl.BlockSpec((size, part), lambda k, meta_ref: (0, k))] * count
        shapes = [(size, QUAD * part)] * count
    return pl.pallas_call(
        functools.partial(down_body, places, joined),
        grid_spec=pltpu.PrefetchScalarGridSpec(
            num_scalar_prefetch=1,
            grid=(QUAD,),
            in_specs=[pl.BlockSpec((rows, depth), whole)]
            + [pl.BlockSpec(memory_space=pl.ANY)] * len(shares),
            out_specs=out_specs,
            scratch_shapes=[
                pltpu.VMEM((QUAD, depth, part), jnp.bfloat16),
                pltpu.SemaphoreType.DMA((len(shares),)),
            ],
        ),
        out_shape=[jax.ShapeDtypeStruct(shape, jnp.bfloat16) for shape in shapes],
        compiler_params=pltpu.CompilerParams(vmem_limit_bytes=58 << 20),
        cost_estimate=pl.CostEstimate(
            flops=2 * rows * depth * QUAD * part,
            bytes_accessed=2 * (rows * depth + QUAD * part * (rows + depth)),
            transcendentals=0,
        ),
        name="down_product",
    )(meta, hidden, *shares)


def latent_finish(projected, gain, length):
    lat_width = gain.shape[0]
    compressed = projected[:, :lat_width]
    rotary = projected[:, lat_width:]
    inverse_rms = lax.rsqrt(jnp.mean(compressed * compressed, axis=1, keepdims=True) + norm_eps)
    normed = compressed * inverse_rms * gain[None, :]
    half_cols = rotary.shape[1] // 2
    positions = jnp.arange(projected.shape[0], dtype=jnp.int32)
    frequency = rope_base ** (-jnp.arange(half_cols, dtype=jnp.float32) / half_cols)
    angles = positions.astype(jnp.float32)[:, None] * frequency[None, :]
    cosine = jnp.cos(angles)
    sine_part = jnp.sin(angles)
    left_half = rotary[:, :half_cols]
    right_half = rotary[:, half_cols:]
    turned = jnp.concatenate(
        [left_half * cosine - right_half * sine_part, left_half * sine_part + right_half * cosine],
        axis=1,
    )
    result = jnp.concatenate([normed, turned], axis=1)
    return jnp.where((positions < length)[:, None], result, 0.0).astype(jnp.bfloat16)


def latent_body(codes, meta_ref, mine_ref, other_ref, *refs):
    parts, sums, weight, done = refs[: len(codes)], refs[len(codes) : -2], refs[-2], refs[-1]
    size = parts[0].shape[1]
    moves = []
    for part, group in zip(parts, codes):
        for number, code in enumerate(group):
            row = pl.multiple_of(((meta_ref[0] ^ code) // 2) * size, 16)
            move = pltpu.make_async_copy(
                part.at[number], weight.at[pl.ds(row, size), :], done.at[len(moves)]
            )
            move.start()
            moves.append(move)
    for move in moves:
        move.wait()
    for tokens_ref, sum_ref in zip((other_ref, mine_ref), sums):
        product = jnp.dot(tokens_ref[0], weight[:size, :], preferred_element_type=jnp.float32)
        for number in range(1, tokens_ref.shape[0]):
            product += jnp.dot(
                tokens_ref[number],
                weight[number * size : (number + 1) * size, :],
                preferred_element_type=jnp.float32,
            )
        sum_ref[...] = product.astype(sum_ref.dtype)


def latent_product(meta, mine, other, parts, codes):
    count, rows, size = mine.shape
    width = count * size
    columns = parts[0].shape[2]
    total = sum(len(group) for group in codes)
    inside = pl.BlockSpec(memory_space=pltpu.VMEM)
    return pl.pallas_call(
        functools.partial(latent_body, codes),
        in_specs=[pl.BlockSpec(memory_space=pltpu.SMEM), inside, inside]
        + [pl.BlockSpec(memory_space=pl.ANY)] * len(parts),
        out_specs=[inside, inside],
        out_shape=[
            jax.ShapeDtypeStruct((rows, columns), jnp.bfloat16),
            jax.ShapeDtypeStruct((rows, columns), jnp.float32),
        ],
        scratch_shapes=[
            pltpu.VMEM((width, columns), jnp.bfloat16),
            pltpu.SemaphoreType.DMA((total,)),
        ],
        compiler_params=pltpu.CompilerParams(vmem_limit_bytes=32 << 20),
        cost_estimate=pl.CostEstimate(
            flops=4 * rows * width * columns,
            bytes_accessed=2 * width * (2 * rows + columns),
            transcendentals=0,
        ),
        name="latent_product",
    )(meta, mine, other, *parts)


def latent_sums(meta, mine, other, parts, codes):
    if parts[0].shape[1] % 16 == 0:
        return latent_product(meta, mine, other, parts, codes)
    joined = jnp.concatenate(parts, axis=0)
    flat = jnp.array([code for group in codes for code in group], jnp.int32)
    order = jnp.argsort((flat ^ meta[0]) // 2)
    weight = joined[order]
    theirs, kept = [
        jnp.einsum("crs,csf->rf", half, weight, preferred_element_type=jnp.float32)
        for half in (other, mine)
    ]
    return theirs.astype(jnp.bfloat16), kept


def core_split_body(meta_ref, tokens_ref, mine_ref, other_ref):
    half = mine_ref.shape[2]
    low, high = tokens_ref[:, :half], tokens_ref[:, half:]

    @pl.when(meta_ref[0] % 2 == 0)
    def _():
        mine_ref[0], other_ref[0] = low, high

    @pl.when(meta_ref[0] % 2 == 1)
    def _():
        mine_ref[0], other_ref[0] = high, low


def core_split(meta, tokens, size):
    rows, width = tokens.shape
    count = width // size // 2
    out = pl.BlockSpec((1, rows, size), lambda n, meta_ref: (n, 0, 0))
    return pl.pallas_call(
        core_split_body,
        grid_spec=pltpu.PrefetchScalarGridSpec(
            num_scalar_prefetch=1,
            grid=(count,),
            in_specs=[pl.BlockSpec((rows, 2 * size), lambda n, meta_ref: (0, n))],
            out_specs=[out, out],
        ),
        out_shape=[jax.ShapeDtypeStruct((count, rows, size), jnp.bfloat16)] * 2,
        name="core_split",
    )(meta, tokens)


def token_halves(meta, tokens, size):
    if size % 64 == 0:
        return core_split(meta, tokens, size)
    rows, width = tokens.shape
    both = tokens.reshape(rows, width // size // 2, 2, size).transpose(2, 1, 0, 3)
    core = meta[0] % 2
    return both[core], both[1 - core]


def shards(
    tokens, lengths, latent_weight, latent_gain, expert_ids, gate_weights, gate_up, down_weight
):
    rows, width = tokens.shape
    rank_count = lax.axis_size("dp")
    rank = lax.axis_index("dp")
    experts = rank_count // GROUP
    pieces = rank_count // QUAD
    hidden_units = gate_up.shape[1] // 2
    length = lengths[rank]
    meta = rank.astype(jnp.int32).reshape(1)
    capacity = rows // experts + 2
    slots = -(-capacity // 8) * 8

    packed = pack(meta, lengths, expert_ids, tokens, experts, slots)
    columns = [[QUAD * s + low for s in range(pieces)] for low in range(QUAD)]
    mine, other = token_halves(meta, tokens, latent_weight.shape[0])

    half = latent_weight.shape[0] // 2
    middle = pieces == 4 and lax.axis_size("groups") == 2 and half % 16 == 0
    group = lax.axis_index("groups")
    first_group = group == 0
    sent = latent_weight[None]
    if middle:
        sent = lax.dynamic_slice_in_dim(sent, group * half, half, 1)
    latent_1 = swapped(sent, QUAD)
    packed = after(packed, latent_1)
    gate_2, mine, other = together(swapped(gate_up, 2), mine, swapped(other, 1))
    mid = down_weight.shape[0] // 2
    down_1 = [swapped(half_rows, 1) for half_rows in (down_weight[:mid], down_weight[mid:])]
    arrived, gate_1, gate_3 = together(
        lax.all_to_all(packed, "dp", 0, 0, axis_index_groups=columns, tiled=True),
        swapped(gate_up, 1),
        swapped(gate_2, 1),
    )
    down_1 = [after(piece, gate_2) for piece in down_1]
    down_3 = [swapped(piece, 2) for piece in down_1]
    if middle:
        cut = swapped(after(jnp.concatenate([sent, latent_1], axis=0), arrived), 2 * QUAD)
    else:
        held, codes = jnp.concatenate([latent_weight[None], latent_1], axis=0), [0, QUAD]
        for level in range(3, rank_count.bit_length() - 1):
            held = jnp.concatenate([held, swapped(held, 1 << level)], axis=0)
            codes = codes + [code ^ (1 << level) for code in codes]

    weight_in = [gate_up, gate_1, gate_2, gate_3]
    away = list(range(1, experts))
    (theirs,) = gate_up_product(meta, arrived, weight_in, [(away, 1, jnp.bfloat16)])
    ours, theirs_near, ours_near = gate_up_product(
        meta,
        arrived,
        weight_in,
        [(away, 0, jnp.float32), ([0], 1, jnp.bfloat16), ([0], 0, jnp.float32)],
    )
    if middle:
        ours, cut = together(ours, cut)
    down_3 = [after(piece, ours) for piece in down_3]
    quarter = mid // 2
    down_2 = [
        swapped(part, 1)
        for piece in down_3
        for part in (piece[:quarter], piece[quarter:])
    ]
    came, *down_2 = together(swapped(theirs, QUAD), *down_2)
    weight_out = [down_weight, *down_1, *down_2, *down_3]

    def activated(own, other):
        summed = own + other.astype(jnp.float32)
        gate, up = summed[:, :hidden_units], summed[:, hidden_units:]
        return (jax.nn.silu(gate) * up).astype(jnp.bfloat16)

    hidden = activated(ours, came)
    partner = swapped(hidden, QUAD)
    (made_own,) = down_product(meta, hidden, weight_out, experts - 1, True)
    halves = [[GROUP * e + low for e in range(experts)] for low in range(GROUP)]
    near = lax.all_to_all(made_own, "dp", 0, 0, axis_index_groups=halves, tiled=True)
    partner, theirs_near = together(after(partner, made_own), theirs_near)
    made = down_product(meta, partner, weight_out, experts - 1, False)
    far = [swapped(made[n - 1], QUAD * (2 * n + 1)) for n in away]

    came_near = after(swapped(theirs_near, QUAD), made[0])
    hidden_near = activated(ours_near, came_near)
    both = jnp.concatenate([hidden_near, swapped(hidden_near, QUAD)], axis=0)
    here, there = down_product(meta, both, weight_out, 2, False)
    near = [here, near]
    far = [swapped(there, QUAD)] + far

    if middle:
        mixed = after(jnp.concatenate([latent_1, cut], axis=0), hidden)
        swap = lax.ppermute(mixed, "groups", [(0, 1), (1, 0)])
        full = jnp.where(
            first_group,
            jnp.concatenate([mixed, swap], axis=1),
            jnp.concatenate([swap, mixed], axis=1),
        )
        held = [jnp.concatenate([latent_weight[None], full[:1]], axis=0), full[1:]]
        codes = [[0, 4], [8, 12]]
    else:
        held, codes = [held], [codes]
    latent_parts = held + [swapped(block, 2) for block in held]
    latent_codes = codes + [[code ^ 2 for code in group] for group in codes]
    given, kept = latent_sums(meta, mine, other, latent_parts, latent_codes)
    whose = (meta, lengths, expert_ids, gate_weights)
    moe_out = unpack(*whose, near, width, True)
    projected = kept + swapped(after(given, moe_out), 1).astype(jnp.float32)
    latent_cache = latent_finish(projected, latent_gain, length)
    moe_out = unpack(*whose, far, width, False, [moe_out])
    return (latent_cache, moe_out)


def solution(mesh):
    placed = (
        P(("groups", "dp"), None),
        P("groups"),
        P("dp", None),
        P(),
        P(("groups", "dp"), None),
        P(("groups", "dp"), None),
        P("dp", None),
        P("dp", None),
    )
    return jax.shard_map(
        shards,
        mesh=mesh,
        in_specs=placed,
        out_specs=(P(("groups", "dp"), None), P(("groups", "dp"), None)),
        check_vma=False,
    )
```

```python
import functools

import jax
import jax.numpy as jnp
from jax import lax
from jax.experimental import pallas as pl
from jax.experimental.pallas import tpu as pltpu
from jax.sharding import PartitionSpec as P

GROUP = 8
QUAD = 4

rope_base = 10000.0
norm_eps = 1e-06


def swapped(block, bits):
    count = lax.axis_size("dp")
    return lax.ppermute(block, "dp", [(low, low ^ bits) for low in range(count)])


def slots_of_rows(rank_ref, lengths_ref, ids_row):
    rows = ids_row.shape[1]
    length = lengths_ref[rank_ref[0]]
    down = lax.broadcasted_iota(jnp.int32, (rows, rows), 0)
    along = lax.broadcasted_iota(jnp.int32, (rows, rows), 1)
    ids_column = jnp.sum(
        jnp.where(down == along, ids_row.astype(jnp.float32), 0.0), axis=1, keepdims=True
    ).astype(jnp.int32)
    return length, down, along, ids_column, ids_column == ids_row


def picks_by_slot(rank_ref, lengths_ref, ids_row, experts, size, picks_ref):
    rows = ids_row.shape[1]
    length, down, along, _, same = slots_of_rows(rank_ref, lengths_ref, ids_row)
    earlier = same & (down < along) & (down < length)
    place = jnp.sum(earlier.astype(jnp.float32), axis=0, keepdims=True).astype(jnp.int32)
    live = lax.broadcasted_iota(jnp.int32, (1, rows), 1) < length
    chosen = jnp.where(live, ids_row, -1)
    slot = lax.broadcasted_iota(jnp.int32, (size, rows), 0)
    for expert in range(experts):
        hit = (place == slot) & (chosen == expert)
        picks_ref[expert] = hit.astype(jnp.float32).astype(jnp.bfloat16)


def picks_by_row(rank_ref, lengths_ref, ids_row, experts, size, picks_ref):
    rows = ids_row.shape[1]
    length, down, along, ids_column, same = slots_of_rows(rank_ref, lengths_ref, ids_row)
    earlier = same & (along < down) & (along < length)
    place = jnp.sum(earlier.astype(jnp.float32), axis=1, keepdims=True).astype(jnp.int32)
    live = lax.broadcasted_iota(jnp.int32, (rows, 1), 0) < length
    chosen = jnp.where(live, ids_column, -1)
    slot = lax.broadcasted_iota(jnp.int32, (rows, size), 1)
    for expert in range(experts):
        hit = (place == slot) & (chosen == expert)
        picks_ref[expert] = hit.astype(jnp.float32).astype(jnp.bfloat16)


def pack_body(rank_ref, lengths_ref, ids_ref, low_ref, high_ref, out_ref, picks_ref):
    experts, size, _ = picks_ref.shape

    @pl.when(pl.program_id(0) == 0)
    def _():
        picks_by_slot(rank_ref, lengths_ref, ids_ref[...], experts, size, picks_ref)

    for side, source_ref in enumerate((low_ref, high_ref)):
        for expert in range(experts):
            out_ref[2 * expert + side] = jnp.dot(
                picks_ref[expert], source_ref[...], preferred_element_type=jnp.float32
            ).astype(jnp.bfloat16)


def pack(rank_array, lengths, ids, tokens, experts, size):
    rows, width = tokens.shape
    part = width // GROUP

    def column_of(side):
        return lambda k, rank_ref, lengths_ref: (0, side * QUAD + ((rank_ref[0] % QUAD) ^ k))

    whole = lambda k, rank_ref, lengths_ref: (0, 0)
    return pl.pallas_call(
        pack_body,
        grid_spec=pltpu.PrefetchScalarGridSpec(
            num_scalar_prefetch=2,
            grid=(QUAD,),
            in_specs=[
                pl.BlockSpec((1, rows), whole),
                pl.BlockSpec((rows, part), column_of(0)),
                pl.BlockSpec((rows, part), column_of(1)),
            ],
            out_specs=pl.BlockSpec(
                (2 * experts, size, part), lambda k, rank_ref, lengths_ref: (0, 0, k)
            ),
            scratch_shapes=[pltpu.VMEM((experts, size, rows), jnp.bfloat16)],
        ),
        out_shape=jax.ShapeDtypeStruct((2 * experts, size, QUAD * part), jnp.bfloat16),
        compiler_params=pltpu.CompilerParams(vmem_limit_bytes=58 << 20),
        cost_estimate=pl.CostEstimate(
            flops=4 * rows * rows * width, bytes_accessed=4 * rows * width, transcendentals=0
        ),
        name="pack_rows",
    )(rank_array, lengths, ids.reshape(1, rows), tokens, tokens)


def unpack_body(near, rank_ref, lengths_ref, ids_ref, gate_ref, *refs):
    out_ref, picks_ref, gate_column_ref = refs[-3:]
    experts, rows, size = picks_ref.shape
    my_expert = rank_ref[0] // GROUP

    @pl.when(pl.program_id(0) == 0)
    def _():
        picks_by_row(rank_ref, lengths_ref, ids_ref[...], experts, size, picks_ref)
        down = lax.broadcasted_iota(jnp.int32, (rows, rows), 0)
        along = lax.broadcasted_iota(jnp.int32, (rows, rows), 1)
        gate_column_ref[...] = jnp.sum(
            jnp.where(down == along, gate_ref[...], 0.0), axis=1, keepdims=True
        )

    total = jnp.zeros(out_ref.shape, jnp.float32)
    for number in range(experts):
        expert = my_expert ^ number
        part = refs[1][expert] if near and number else refs[number][...]
        total += jnp.dot(picks_ref[expert], part, preferred_element_type=jnp.float32)
    out_ref[...] = (total * gate_column_ref[...]).astype(jnp.bfloat16)


def unpack(rank_array, lengths, ids, gates, parts, width, near, base=()):
    rows = ids.shape[0]
    part = width // GROUP
    size = parts[0].shape[-2]
    experts = parts[1].shape[0] if near else len(parts)

    def out_index(k, rank_ref, lengths_ref):
        quarter = rank_ref[0] % QUAD
        high = (rank_ref[0] // QUAD) % 2
        return (0, (high if near else 1 - high) * QUAD + (quarter ^ k))

    whole = lambda k, rank_ref, lengths_ref: (0, 0)
    specs = [pl.BlockSpec((size, part), lambda k, rank_ref, lengths_ref: (0, k))] * experts
    if near:
        both = pl.BlockSpec((experts, size, part), lambda k, rank_ref, lengths_ref: (0, 0, k))
        specs = [specs[0], both]
    return pl.pallas_call(
        functools.partial(unpack_body, near),
        grid_spec=pltpu.PrefetchScalarGridSpec(
            num_scalar_prefetch=2,
            grid=(QUAD,),
            in_specs=[pl.BlockSpec((1, rows), whole), pl.BlockSpec((1, rows), whole)]
            + specs
            + [pl.BlockSpec(memory_space=pl.ANY)] * len(base),
            out_specs=pl.BlockSpec((rows, part), out_index),
            scratch_shapes=[
                pltpu.VMEM((experts, rows, size), jnp.bfloat16),
                pltpu.VMEM((rows, 1), jnp.float32),
            ],
        ),
        out_shape=jax.ShapeDtypeStruct((rows, width), jnp.bfloat16),
        input_output_aliases={4 + len(specs): 0} if base else {},
        compiler_params=pltpu.CompilerParams(vmem_limit_bytes=58 << 20),
        cost_estimate=pl.CostEstimate(
            flops=2 * rows * rows * width, bytes_accessed=2 * rows * width, transcendentals=0
        ),
        name="unpack_rows",
    )(rank_array, lengths, ids.reshape(1, rows), gates.reshape(1, rows), *parts, *base)


def idle_body(*refs):
    del refs


def after(value, *events):
    anywhere = pl.BlockSpec(memory_space=pl.ANY)
    return pl.pallas_call(
        idle_body,
        in_specs=[anywhere] * (1 + len(events)),
        out_specs=anywhere,
        out_shape=jax.ShapeDtypeStruct(value.shape, value.dtype),
        input_output_aliases={0: 0},
        name="after",
    )(value, *events)


def together(*values):
    anywhere = pl.BlockSpec(memory_space=pl.ANY)
    return pl.pallas_call(
        idle_body,
        in_specs=[anywhere] * len(values),
        out_specs=[anywhere] * len(values),
        out_shape=[jax.ShapeDtypeStruct(value.shape, value.dtype) for value in values],
        input_output_aliases={number: number for number in range(len(values))},
        name="together",
    )(*values)


def gate_up_body(groups, meta_ref, *refs):
    del meta_ref
    count = sum(groups)
    parts, shares = refs[:count], refs[count : count + QUAD]
    outs, joined = refs[count + QUAD : -1], refs[-1]
    size = parts[0].shape[1]
    depth = shares[0].shape[0]

    @pl.when(pl.program_id(0) == 0)
    def _():
        for number, part in enumerate(parts):
            joined[pl.ds(number * size, size), :] = part[0]

    total = jnp.dot(joined[:, :depth], shares[0][...], preferred_element_type=jnp.float32)
    for k in range(1, QUAD):
        total += jnp.dot(
            joined[:, k * depth : (k + 1) * depth],
            shares[k][...],
            preferred_element_type=jnp.float32,
        )
    start = 0
    for group, out_ref in zip(groups, outs):
        out_ref[...] = total[start : start + group * size].astype(out_ref.dtype)
        start += group * size


def gate_up_product(meta, arrived, shares, groups):
    _, size, width = arrived.shape
    depth, columns = shares[0].shape
    tile = columns // 4
    rows = size * sum(len(numbers) for numbers, _, _ in groups)

    def source(number, side):
        def index(n, meta_ref):
            rank = meta_ref[0]
            return (2 * ((rank // GROUP) ^ number) + (((rank // QUAD) % 2) ^ side), 0, 0)

        return index

    across = lambda n, meta_ref: (0, n)
    picked = [source(number, side) for numbers, side, _ in groups for number in numbers]
    heights = [size * len(numbers) for numbers, _, _ in groups]
    return pl.pallas_call(
        functools.partial(gate_up_body, [len(numbers) for numbers, _, _ in groups]),
        grid_spec=pltpu.PrefetchScalarGridSpec(
            num_scalar_prefetch=1,
            grid=(columns // tile,),
            in_specs=[pl.BlockSpec((1, size, width), index) for index in picked]
            + [pl.BlockSpec((depth, tile), across) for _ in shares],
            out_specs=[pl.BlockSpec((height, tile), across) for height in heights],
            scratch_shapes=[pltpu.VMEM((rows, width), jnp.bfloat16)],
        ),
        out_shape=[
            jax.ShapeDtypeStruct((height, columns), dtype)
            for height, (_, _, dtype) in zip(heights, groups)
        ],
        compiler_params=pltpu.CompilerParams(vmem_limit_bytes=32 << 20),
        cost_estimate=pl.CostEstimate(
            flops=2 * rows * width * columns,
            bytes_accessed=2 * width * (rows + columns),
            transcendentals=0,
        ),
        name="gate_up_product",
    )(meta, *[arrived] * len(picked), *shares)


def down_body(places, joined, meta_ref, hidden_ref, *refs):
    k = pl.program_id(0)
    weight, done = refs[-2:]
    pieces, outs = refs[: len(places)], refs[len(places) : -2]
    count = outs[0].shape[0] - 1 if joined else len(outs)
    size = hidden_ref.shape[0] // count
    mine = meta_ref[0] // GROUP
    moves = []
    for number, (piece, (turn, start)) in enumerate(zip(pieces, places)):
        target = weight.at[turn, pl.ds(start, piece.shape[0]), :]
        moves.append(pltpu.make_async_copy(piece, target, done.at[number]))

    @pl.when(k == 0)
    def _():
        for move in moves:
            move.start()

    for turn in range(QUAD):

        @pl.when(k == turn)
        def _(turn=turn):
            for move, place in zip(moves, places):
                if place[0] == turn:
                    move.wait()

    made = jnp.dot(hidden_ref[...], weight[k], preferred_element_type=jnp.float32)
    for number in range(count):
        rows = made[number * size : (number + 1) * size].astype(jnp.bfloat16)
        if joined:
            outs[0][mine ^ (number + 1)] = rows
        else:
            outs[number][...] = rows


def down_product(meta, hidden, shares, count, joined):
    rows, depth = hidden.shape
    part = shares[0].shape[1]
    size = rows // count
    places, filled = [], 0
    for share in shares:
        places.append((filled // depth, filled % depth))
        filled += share.shape[0]
    whole = lambda k, meta_ref: (0, 0)
    if joined:
        out_specs = [pl.BlockSpec((count + 1, size, part), lambda k, meta_ref: (0, 0, k))]
        shapes = [(count + 1, size, QUAD * part)]
    else:
        out_specs = [pl.BlockSpec((size, part), lambda k, meta_ref: (0, k))] * count
        shapes = [(size, QUAD * part)] * count
    return pl.pallas_call(
        functools.partial(down_body, places, joined),
        grid_spec=pltpu.PrefetchScalarGridSpec(
            num_scalar_prefetch=1,
            grid=(QUAD,),
            in_specs=[pl.BlockSpec((rows, depth), whole)]
            + [pl.BlockSpec(memory_space=pl.ANY)] * len(shares),
            out_specs=out_specs,
            scratch_shapes=[
                pltpu.VMEM((QUAD, depth, part), jnp.bfloat16),
                pltpu.SemaphoreType.DMA((len(shares),)),
            ],
        ),
        out_shape=[jax.ShapeDtypeStruct(shape, jnp.bfloat16) for shape in shapes],
        compiler_params=pltpu.CompilerParams(vmem_limit_bytes=58 << 20),
        cost_estimate=pl.CostEstimate(
            flops=2 * rows * depth * QUAD * part,
            bytes_accessed=2 * (rows * depth + QUAD * part * (rows + depth)),
            transcendentals=0,
        ),
        name="down_product",
    )(meta, hidden, *shares)


def latent_finish(projected, gain, length):
    lat_width = gain.shape[0]
    compressed = projected[:, :lat_width]
    rotary = projected[:, lat_width:]
    inverse_rms = lax.rsqrt(jnp.mean(compressed * compressed, axis=1, keepdims=True) + norm_eps)
    normed = compressed * inverse_rms * gain[None, :]
    half_cols = rotary.shape[1] // 2
    positions = jnp.arange(projected.shape[0], dtype=jnp.int32)
    frequency = rope_base ** (-jnp.arange(half_cols, dtype=jnp.float32) / half_cols)
    angles = positions.astype(jnp.float32)[:, None] * frequency[None, :]
    cosine = jnp.cos(angles)
    sine_part = jnp.sin(angles)
    left_half = rotary[:, :half_cols]
    right_half = rotary[:, half_cols:]
    turned = jnp.concatenate(
        [left_half * cosine - right_half * sine_part, left_half * sine_part + right_half * cosine],
        axis=1,
    )
    result = jnp.concatenate([normed, turned], axis=1)
    return jnp.where((positions < length)[:, None], result, 0.0).astype(jnp.bfloat16)


def latent_body(codes, meta_ref, mine_ref, other_ref, *refs):
    parts, sums, weight, done = refs[: len(codes)], refs[len(codes) : -2], refs[-2], refs[-1]
    size = parts[0].shape[1]
    moves = []
    for part, group in zip(parts, codes):
        for number, code in enumerate(group):
            row = pl.multiple_of(((meta_ref[0] ^ code) // 2) * size, 16)
            move = pltpu.make_async_copy(
                part.at[number], weight.at[pl.ds(row, size), :], done.at[len(moves)]
            )
            move.start()
            moves.append(move)
    for move in moves:
        move.wait()
    for tokens_ref, sum_ref in zip((other_ref, mine_ref), sums):
        product = jnp.dot(tokens_ref[0], weight[:size, :], preferred_element_type=jnp.float32)
        for number in range(1, tokens_ref.shape[0]):
            product += jnp.dot(
                tokens_ref[number],
                weight[number * size : (number + 1) * size, :],
                preferred_element_type=jnp.float32,
            )
        sum_ref[...] = product.astype(sum_ref.dtype)


def latent_product(meta, mine, other, parts, codes):
    count, rows, size = mine.shape
    width = count * size
    columns = parts[0].shape[2]
    total = sum(len(group) for group in codes)
    inside = pl.BlockSpec(memory_space=pltpu.VMEM)
    return pl.pallas_call(
        functools.partial(latent_body, codes),
        in_specs=[pl.BlockSpec(memory_space=pltpu.SMEM), inside, inside]
        + [pl.BlockSpec(memory_space=pl.ANY)] * len(parts),
        out_specs=[inside, inside],
        out_shape=[
            jax.ShapeDtypeStruct((rows, columns), jnp.bfloat16),
            jax.ShapeDtypeStruct((rows, columns), jnp.float32),
        ],
        scratch_shapes=[
            pltpu.VMEM((width, columns), jnp.bfloat16),
            pltpu.SemaphoreType.DMA((total,)),
        ],
        compiler_params=pltpu.CompilerParams(vmem_limit_bytes=32 << 20),
        cost_estimate=pl.CostEstimate(
            flops=4 * rows * width * columns,
            bytes_accessed=2 * width * (2 * rows + columns),
            transcendentals=0,
        ),
        name="latent_product",
    )(meta, mine, other, *parts)


def latent_sums(meta, mine, other, parts, codes):
    if parts[0].shape[1] % 16 == 0:
        return latent_product(meta, mine, other, parts, codes)
    joined = jnp.concatenate(parts, axis=0)
    flat = jnp.array([code for group in codes for code in group], jnp.int32)
    order = jnp.argsort((flat ^ meta[0]) // 2)
    weight = joined[order]
    theirs, kept = [
        jnp.einsum("crs,csf->rf", half, weight, preferred_element_type=jnp.float32)
        for half in (other, mine)
    ]
    return theirs.astype(jnp.bfloat16), kept


def core_split_body(meta_ref, tokens_ref, mine_ref, other_ref):
    half = mine_ref.shape[2]
    low, high = tokens_ref[:, :half], tokens_ref[:, half:]

    @pl.when(meta_ref[0] % 2 == 0)
    def _():
        mine_ref[0], other_ref[0] = low, high

    @pl.when(meta_ref[0] % 2 == 1)
    def _():
        mine_ref[0], other_ref[0] = high, low


def core_split(meta, tokens, size):
    rows, width = tokens.shape
    count = width // size // 2
    out = pl.BlockSpec((1, rows, size), lambda n, meta_ref: (n, 0, 0))
    return pl.pallas_call(
        core_split_body,
        grid_spec=pltpu.PrefetchScalarGridSpec(
            num_scalar_prefetch=1,
            grid=(count,),
            in_specs=[pl.BlockSpec((rows, 2 * size), lambda n, meta_ref: (0, n))],
            out_specs=[out, out],
        ),
        out_shape=[jax.ShapeDtypeStruct((count, rows, size), jnp.bfloat16)] * 2,
        name="core_split",
    )(meta, tokens)


def token_halves(meta, tokens, size):
    if size % 64 == 0:
        return core_split(meta, tokens, size)
    rows, width = tokens.shape
    both = tokens.reshape(rows, width // size // 2, 2, size).transpose(2, 1, 0, 3)
    core = meta[0] % 2
    return both[core], both[1 - core]


def shards(
    tokens, lengths, latent_weight, latent_gain, expert_ids, gate_weights, gate_up, down_weight
):
    rows, width = tokens.shape
    rank_count = lax.axis_size("dp")
    rank = lax.axis_index("dp")
    experts = rank_count // GROUP
    pieces = rank_count // QUAD
    hidden_units = gate_up.shape[1] // 2
    length = lengths[rank]
    meta = rank.astype(jnp.int32).reshape(1)
    capacity = rows // experts + 2
    slots = -(-capacity // 8) * 8

    packed = pack(meta, lengths, expert_ids, tokens, experts, slots)
    columns = [[QUAD * s + low for s in range(pieces)] for low in range(QUAD)]
    mine, other = token_halves(meta, tokens, latent_weight.shape[0])

    half = latent_weight.shape[0] // 2
    middle = pieces == 4 and lax.axis_size("groups") == 2 and half % 16 == 0
    group = lax.axis_index("groups")
    first_group = group == 0
    sent = latent_weight[None]
    if middle:
        sent = lax.dynamic_slice_in_dim(sent, group * half, half, 1)
    latent_1 = swapped(sent, QUAD)
    packed = after(packed, latent_1)
    gate_2, mine, other = together(swapped(gate_up, 2), mine, swapped(other, 1))
    mid = down_weight.shape[0] // 2
    down_1 = [swapped(half_rows, 1) for half_rows in (down_weight[:mid], down_weight[mid:])]
    arrived, gate_1, gate_3 = together(
        lax.all_to_all(packed, "dp", 0, 0, axis_index_groups=columns, tiled=True),
        swapped(gate_up, 1),
        swapped(gate_2, 1),
    )
    down_1 = [after(piece, gate_2) for piece in down_1]
    down_3 = [swapped(piece, 2) for piece in down_1]
    if middle:
        cut = swapped(after(jnp.concatenate([sent, latent_1], axis=0), arrived), 2 * QUAD)
    else:
        held, codes = jnp.concatenate([latent_weight[None], latent_1], axis=0), [0, QUAD]
        for level in range(3, rank_count.bit_length() - 1):
            held = jnp.concatenate([held, swapped(held, 1 << level)], axis=0)
            codes = codes + [code ^ (1 << level) for code in codes]

    weight_in = [gate_up, gate_1, gate_2, gate_3]
    away = list(range(1, experts))
    (theirs,) = gate_up_product(meta, arrived, weight_in, [(away, 1, jnp.bfloat16)])
    ours, theirs_near, ours_near = gate_up_product(
        meta,
        arrived,
        weight_in,
        [(away, 0, jnp.float32), ([0], 1, jnp.bfloat16), ([0], 0, jnp.float32)],
    )
    if middle:
        ours, cut = together(ours, cut)
    down_3 = [after(piece, ours) for piece in down_3]
    quarter = mid // 2
    down_2 = [
        swapped(part, 1)
        for piece in down_3
        for part in (piece[:quarter], piece[quarter:])
    ]
    came, *down_2 = together(swapped(theirs, QUAD), *down_2)
    weight_out = [down_weight, *down_1, *down_2, *down_3]

    def activated(own, other):
        summed = own + other.astype(jnp.float32)
        gate, up = summed[:, :hidden_units], summed[:, hidden_units:]
        return (jax.nn.silu(gate) * up).astype(jnp.bfloat16)

    hidden = activated(ours, came)
    partner = swapped(hidden, QUAD)
    (made_own,) = down_product(meta, hidden, weight_out, experts - 1, True)
    halves = [[GROUP * e + low for e in range(experts)] for low in range(GROUP)]
    near = lax.all_to_all(made_own, "dp", 0, 0, axis_index_groups=halves, tiled=True)
    partner, theirs_near = together(after(partner, made_own), theirs_near)
    made = down_product(meta, partner, weight_out, experts - 1, False)
    far = [swapped(made[n - 1], QUAD * (2 * n + 1)) for n in away]

    came_near = after(swapped(theirs_near, QUAD), made[0])
    hidden_near = activated(ours_near, came_near)
    both = jnp.concatenate([hidden_near, swapped(hidden_near, QUAD)], axis=0)
    here, there = down_product(meta, both, weight_out, 2, False)
    near = [here, near]
    far = [swapped(there, QUAD)] + far

    if middle:
        mixed = after(jnp.concatenate([latent_1, cut], axis=0), hidden)
        swap = lax.ppermute(mixed, "groups", [(0, 1), (1, 0)])
        full = jnp.where(
            first_group,
            jnp.concatenate([mixed, swap], axis=1),
            jnp.concatenate([swap, mixed], axis=1),
        )
        held = [jnp.concatenate([latent_weight[None], full[:1]], axis=0), full[1:]]
        codes = [[0, 4], [8, 12]]
    else:
        held, codes = [held], [codes]
    latent_parts = held + [swapped(block, 2) for block in held]
    latent_codes = codes + [[code ^ 2 for code in group] for group in codes]
    given, kept = latent_sums(meta, mine, other, latent_parts, latent_codes)
    whose = (meta, lengths, expert_ids, gate_weights)
    moe_out = unpack(*whose, near, width, True)
    projected = kept + swapped(after(given, moe_out), 1).astype(jnp.float32)
    latent_cache = latent_finish(projected, latent_gain, length)
    moe_out = unpack(*whose, far, width, False, [moe_out])
    return (latent_cache, moe_out)


def solution(mesh):
    placed = (
        P(("groups", "dp"), None),
        P("groups"),
        P("dp", None),
        P(),
        P(("groups", "dp"), None),
        P(("groups", "dp"), None),
        P("dp", None),
        P("dp", None),
    )
    return jax.shard_map(
        shards,
        mesh=mesh,
        in_specs=placed,
        out_specs=(P(("groups", "dp"), None), P(("groups", "dp"), None)),
        check_vma=False,
    )
```

```python
import functools

import jax
import jax.numpy as jnp
from jax import lax
from jax.experimental import pallas as pl
from jax.experimental.pallas import tpu as pltpu
from jax.sharding import PartitionSpec as P

GROUP = 8
QUAD = 4

rope_base = 10000.0
norm_eps = 1e-06


def swapped(block, bits):
    count = lax.axis_size("dp")
    return lax.ppermute(block, "dp", [(low, low ^ bits) for low in range(count)])


def slots_of_rows(rank_ref, lengths_ref, ids_row):
    rows = ids_row.shape[1]
    length = lengths_ref[rank_ref[0]]
    down = lax.broadcasted_iota(jnp.int32, (rows, rows), 0)
    along = lax.broadcasted_iota(jnp.int32, (rows, rows), 1)
    ids_column = jnp.sum(
        jnp.where(down == along, ids_row.astype(jnp.float32), 0.0), axis=1, keepdims=True
    ).astype(jnp.int32)
    return length, down, along, ids_column, ids_column == ids_row


def picks_by_slot(rank_ref, lengths_ref, ids_row, experts, size, picks_ref):
    rows = ids_row.shape[1]
    length, down, along, _, same = slots_of_rows(rank_ref, lengths_ref, ids_row)
    earlier = same & (down < along) & (down < length)
    place = jnp.sum(earlier.astype(jnp.float32), axis=0, keepdims=True).astype(jnp.int32)
    live = lax.broadcasted_iota(jnp.int32, (1, rows), 1) < length
    chosen = jnp.where(live, ids_row, -1)
    slot = lax.broadcasted_iota(jnp.int32, (size, rows), 0)
    for expert in range(experts):
        hit = (place == slot) & (chosen == expert)
        picks_ref[expert] = hit.astype(jnp.float32).astype(jnp.bfloat16)


def picks_by_row(rank_ref, lengths_ref, ids_row, experts, size, picks_ref):
    rows = ids_row.shape[1]
    length, down, along, ids_column, same = slots_of_rows(rank_ref, lengths_ref, ids_row)
    earlier = same & (along < down) & (along < length)
    place = jnp.sum(earlier.astype(jnp.float32), axis=1, keepdims=True).astype(jnp.int32)
    live = lax.broadcasted_iota(jnp.int32, (rows, 1), 0) < length
    chosen = jnp.where(live, ids_column, -1)
    slot = lax.broadcasted_iota(jnp.int32, (rows, size), 1)
    for expert in range(experts):
        hit = (place == slot) & (chosen == expert)
        picks_ref[expert] = hit.astype(jnp.float32).astype(jnp.bfloat16)


def pack_body(rank_ref, lengths_ref, ids_ref, low_ref, high_ref, out_ref, picks_ref):
    experts, size, _ = picks_ref.shape

    @pl.when(pl.program_id(0) == 0)
    def _():
        picks_by_slot(rank_ref, lengths_ref, ids_ref[...], experts, size, picks_ref)

    for side, source_ref in enumerate((low_ref, high_ref)):
        for expert in range(experts):
            out_ref[2 * expert + side] = jnp.dot(
                picks_ref[expert], source_ref[...], preferred_element_type=jnp.float32
            ).astype(jnp.bfloat16)


def pack(rank_array, lengths, ids, tokens, experts, size):
    rows, width = tokens.shape
    part = width // GROUP

    def column_of(side):
        return lambda k, rank_ref, lengths_ref: (0, side * QUAD + ((rank_ref[0] % QUAD) ^ k))

    whole = lambda k, rank_ref, lengths_ref: (0, 0)
    return pl.pallas_call(
        pack_body,
        grid_spec=pltpu.PrefetchScalarGridSpec(
            num_scalar_prefetch=2,
            grid=(QUAD,),
            in_specs=[
                pl.BlockSpec((1, rows), whole),
                pl.BlockSpec((rows, part), column_of(0)),
                pl.BlockSpec((rows, part), column_of(1)),
            ],
            out_specs=pl.BlockSpec(
                (2 * experts, size, part), lambda k, rank_ref, lengths_ref: (0, 0, k)
            ),
            scratch_shapes=[pltpu.VMEM((experts, size, rows), jnp.bfloat16)],
        ),
        out_shape=jax.ShapeDtypeStruct((2 * experts, size, QUAD * part), jnp.bfloat16),
        compiler_params=pltpu.CompilerParams(vmem_limit_bytes=58 << 20),
        cost_estimate=pl.CostEstimate(
            flops=4 * rows * rows * width, bytes_accessed=4 * rows * width, transcendentals=0
        ),
        name="pack_rows",
    )(rank_array, lengths, ids.reshape(1, rows), tokens, tokens)


def unpack_body(near, rank_ref, lengths_ref, ids_ref, gate_ref, *refs):
    out_ref, picks_ref, gate_column_ref = refs[-3:]
    experts, rows, size = picks_ref.shape
    my_expert = rank_ref[0] // GROUP

    @pl.when(pl.program_id(0) == 0)
    def _():
        picks_by_row(rank_ref, lengths_ref, ids_ref[...], experts, size, picks_ref)
        down = lax.broadcasted_iota(jnp.int32, (rows, rows), 0)
        along = lax.broadcasted_iota(jnp.int32, (rows, rows), 1)
        gate_column_ref[...] = jnp.sum(
            jnp.where(down == along, gate_ref[...], 0.0), axis=1, keepdims=True
        )

    total = jnp.zeros(out_ref.shape, jnp.float32)
    for number in range(experts):
        expert = my_expert ^ number
        part = refs[1][expert] if near and number else refs[number][...]
        total += jnp.dot(picks_ref[expert], part, preferred_element_type=jnp.float32)
    out_ref[...] = (total * gate_column_ref[...]).astype(jnp.bfloat16)


def unpack(rank_array, lengths, ids, gates, parts, width, near, base=()):
    rows = ids.shape[0]
    part = width // GROUP
    size = parts[0].shape[-2]
    experts = parts[1].shape[0] if near else len(parts)

    def out_index(k, rank_ref, lengths_ref):
        quarter = rank_ref[0] % QUAD
        high = (rank_ref[0] // QUAD) % 2
        return (0, (high if near else 1 - high) * QUAD + (quarter ^ k))

    whole = lambda k, rank_ref, lengths_ref: (0, 0)
    specs = [pl.BlockSpec((size, part), lambda k, rank_ref, lengths_ref: (0, k))] * experts
    if near:
        both = pl.BlockSpec((experts, size, part), lambda k, rank_ref, lengths_ref: (0, 0, k))
        specs = [specs[0], both]
    return pl.pallas_call(
        functools.partial(unpack_body, near),
        grid_spec=pltpu.PrefetchScalarGridSpec(
            num_scalar_prefetch=2,
            grid=(QUAD,),
            in_specs=[pl.BlockSpec((1, rows), whole), pl.BlockSpec((1, rows), whole)]
            + specs
            + [pl.BlockSpec(memory_space=pl.ANY)] * len(base),
            out_specs=pl.BlockSpec((rows, part), out_index),
            scratch_shapes=[
                pltpu.VMEM((experts, rows, size), jnp.bfloat16),
                pltpu.VMEM((rows, 1), jnp.float32),
            ],
        ),
        out_shape=jax.ShapeDtypeStruct((rows, width), jnp.bfloat16),
        input_output_aliases={4 + len(specs): 0} if base else {},
        compiler_params=pltpu.CompilerParams(vmem_limit_bytes=58 << 20),
        cost_estimate=pl.CostEstimate(
            flops=2 * rows * rows * width, bytes_accessed=2 * rows * width, transcendentals=0
        ),
        name="unpack_rows",
    )(rank_array, lengths, ids.reshape(1, rows), gates.reshape(1, rows), *parts, *base)


def idle_body(*refs):
    del refs


def after(value, *events):
    anywhere = pl.BlockSpec(memory_space=pl.ANY)
    return pl.pallas_call(
        idle_body,
        in_specs=[anywhere] * (1 + len(events)),
        out_specs=anywhere,
        out_shape=jax.ShapeDtypeStruct(value.shape, value.dtype),
        input_output_aliases={0: 0},
        name="after",
    )(value, *events)


def together(*values):
    anywhere = pl.BlockSpec(memory_space=pl.ANY)
    return pl.pallas_call(
        idle_body,
        in_specs=[anywhere] * len(values),
        out_specs=[anywhere] * len(values),
        out_shape=[jax.ShapeDtypeStruct(value.shape, value.dtype) for value in values],
        input_output_aliases={number: number for number in range(len(values))},
        name="together",
    )(*values)


def gate_up_body(groups, meta_ref, *refs):
    del meta_ref
    count = sum(groups)
    parts, shares = refs[:count], refs[count : count + QUAD]
    outs, joined = refs[count + QUAD : -1], refs[-1]
    size = parts[0].shape[1]
    depth = shares[0].shape[0]

    @pl.when(pl.program_id(0) == 0)
    def _():
        for number, part in enumerate(parts):
            joined[pl.ds(number * size, size), :] = part[0]

    total = jnp.dot(joined[:, :depth], shares[0][...], preferred_element_type=jnp.float32)
    for k in range(1, QUAD):
        total += jnp.dot(
            joined[:, k * depth : (k + 1) * depth],
            shares[k][...],
            preferred_element_type=jnp.float32,
        )
    start = 0
    for group, out_ref in zip(groups, outs):
        out_ref[...] = total[start : start + group * size].astype(out_ref.dtype)
        start += group * size


def gate_up_product(meta, arrived, shares, groups):
    _, size, width = arrived.shape
    depth, columns = shares[0].shape
    tile = columns // 4
    rows = size * sum(len(numbers) for numbers, _, _ in groups)

    def source(number, side):
        def index(n, meta_ref):
            rank = meta_ref[0]
            return (2 * ((rank // GROUP) ^ number) + (((rank // QUAD) % 2) ^ side), 0, 0)

        return index

    across = lambda n, meta_ref: (0, n)
    picked = [source(number, side) for numbers, side, _ in groups for number in numbers]
    heights = [size * len(numbers) for numbers, _, _ in groups]
    return pl.pallas_call(
        functools.partial(gate_up_body, [len(numbers) for numbers, _, _ in groups]),
        grid_spec=pltpu.PrefetchScalarGridSpec(
            num_scalar_prefetch=1,
            grid=(columns // tile,),
            in_specs=[pl.BlockSpec((1, size, width), index) for index in picked]
            + [pl.BlockSpec((depth, tile), across) for _ in shares],
            out_specs=[pl.BlockSpec((height, tile), across) for height in heights],
            scratch_shapes=[pltpu.VMEM((rows, width), jnp.bfloat16)],
        ),
        out_shape=[
            jax.ShapeDtypeStruct((height, columns), dtype)
            for height, (_, _, dtype) in zip(heights, groups)
        ],
        compiler_params=pltpu.CompilerParams(vmem_limit_bytes=32 << 20),
        cost_estimate=pl.CostEstimate(
            flops=2 * rows * width * columns,
            bytes_accessed=2 * width * (rows + columns),
            transcendentals=0,
        ),
        name="gate_up_product",
    )(meta, *[arrived] * len(picked), *shares)


def down_body(places, joined, meta_ref, hidden_ref, *refs):
    k = pl.program_id(0)
    weight, done = refs[-2:]
    pieces, outs = refs[: len(places)], refs[len(places) : -2]
    count = outs[0].shape[0] - 1 if joined else len(outs)
    size = hidden_ref.shape[0] // count
    mine = meta_ref[0] // GROUP
    moves = []
    for number, (piece, (turn, start)) in enumerate(zip(pieces, places)):
        target = weight.at[turn, pl.ds(start, piece.shape[0]), :]
        moves.append(pltpu.make_async_copy(piece, target, done.at[number]))

    @pl.when(k == 0)
    def _():
        for move in moves:
            move.start()

    for turn in range(QUAD):

        @pl.when(k == turn)
        def _(turn=turn):
            for move, place in zip(moves, places):
                if place[0] == turn:
                    move.wait()

    made = jnp.dot(hidden_ref[...], weight[k], preferred_element_type=jnp.float32)
    for number in range(count):
        rows = made[number * size : (number + 1) * size].astype(jnp.bfloat16)
        if joined:
            outs[0][mine ^ (number + 1)] = rows
        else:
            outs[number][...] = rows


def down_product(meta, hidden, shares, count, joined):
    rows, depth = hidden.shape
    part = shares[0].shape[1]
    size = rows // count
    places, filled = [], 0
    for share in shares:
        places.append((filled // depth, filled % depth))
        filled += share.shape[0]
    whole = lambda k, meta_ref: (0, 0)
    if joined:
        out_specs = [pl.BlockSpec((count + 1, size, part), lambda k, meta_ref: (0, 0, k))]
        shapes = [(count + 1, size, QUAD * part)]
    else:
        out_specs = [pl.BlockSpec((size, part), lambda k, meta_ref: (0, k))] * count
        shapes = [(size, QUAD * part)] * count
    return pl.pallas_call(
        functools.partial(down_body, places, joined),
        grid_spec=pltpu.PrefetchScalarGridSpec(
            num_scalar_prefetch=1,
            grid=(QUAD,),
            in_specs=[pl.BlockSpec((rows, depth), whole)]
            + [pl.BlockSpec(memory_space=pl.ANY)] * len(shares),
            out_specs=out_specs,
            scratch_shapes=[
                pltpu.VMEM((QUAD, depth, part), jnp.bfloat16),
                pltpu.SemaphoreType.DMA((len(shares),)),
            ],
        ),
        out_shape=[jax.ShapeDtypeStruct(shape, jnp.bfloat16) for shape in shapes],
        compiler_params=pltpu.CompilerParams(vmem_limit_bytes=58 << 20),
        cost_estimate=pl.CostEstimate(
            flops=2 * rows * depth * QUAD * part,
            bytes_accessed=2 * (rows * depth + QUAD * part * (rows + depth)),
            transcendentals=0,
        ),
        name="down_product",
    )(meta, hidden, *shares)


def latent_finish(projected, gain, length):
    lat_width = gain.shape[0]
    compressed = projected[:, :lat_width]
    rotary = projected[:, lat_width:]
    inverse_rms = lax.rsqrt(jnp.mean(compressed * compressed, axis=1, keepdims=True) + norm_eps)
    normed = compressed * inverse_rms * gain[None, :]
    half_cols = rotary.shape[1] // 2
    positions = jnp.arange(projected.shape[0], dtype=jnp.int32)
    frequency = rope_base ** (-jnp.arange(half_cols, dtype=jnp.float32) / half_cols)
    angles = positions.astype(jnp.float32)[:, None] * frequency[None, :]
    cosine = jnp.cos(angles)
    sine_part = jnp.sin(angles)
    left_half = rotary[:, :half_cols]
    right_half = rotary[:, half_cols:]
    turned = jnp.concatenate(
        [left_half * cosine - right_half * sine_part, left_half * sine_part + right_half * cosine],
        axis=1,
    )
    result = jnp.concatenate([normed, turned], axis=1)
    return jnp.where((positions < length)[:, None], result, 0.0).astype(jnp.bfloat16)


def latent_body(codes, meta_ref, mine_ref, other_ref, *refs):
    parts, sums, weight, done = refs[: len(codes)], refs[len(codes) : -2], refs[-2], refs[-1]
    size = parts[0].shape[1]
    moves = []
    for part, group in zip(parts, codes):
        for number, code in enumerate(group):
            row = pl.multiple_of(((meta_ref[0] ^ code) // 2) * size, 16)
            move = pltpu.make_async_copy(
                part.at[number], weight.at[pl.ds(row, size), :], done.at[len(moves)]
            )
            move.start()
            moves.append(move)
    for move in moves:
        move.wait()
    for tokens_ref, sum_ref in zip((other_ref, mine_ref), sums):
        product = jnp.dot(tokens_ref[0], weight[:size, :], preferred_element_type=jnp.float32)
        for number in range(1, tokens_ref.shape[0]):
            product += jnp.dot(
                tokens_ref[number],
                weight[number * size : (number + 1) * size, :],
                preferred_element_type=jnp.float32,
            )
        sum_ref[...] = product.astype(sum_ref.dtype)


def latent_product(meta, mine, other, parts, codes):
    count, rows, size = mine.shape
    width = count * size
    columns = parts[0].shape[2]
    total = sum(len(group) for group in codes)
    inside = pl.BlockSpec(memory_space=pltpu.VMEM)
    return pl.pallas_call(
        functools.partial(latent_body, codes),
        in_specs=[pl.BlockSpec(memory_space=pltpu.SMEM), inside, inside]
        + [pl.BlockSpec(memory_space=pl.ANY)] * len(parts),
        out_specs=[inside, inside],
        out_shape=[
            jax.ShapeDtypeStruct((rows, columns), jnp.bfloat16),
            jax.ShapeDtypeStruct((rows, columns), jnp.float32),
        ],
        scratch_shapes=[
            pltpu.VMEM((width, columns), jnp.bfloat16),
            pltpu.SemaphoreType.DMA((total,)),
        ],
        compiler_params=pltpu.CompilerParams(vmem_limit_bytes=32 << 20),
        cost_estimate=pl.CostEstimate(
            flops=4 * rows * width * columns,
            bytes_accessed=2 * width * (2 * rows + columns),
            transcendentals=0,
        ),
        name="latent_product",
    )(meta, mine, other, *parts)


def latent_sums(meta, mine, other, parts, codes):
    if parts[0].shape[1] % 16 == 0:
        return latent_product(meta, mine, other, parts, codes)
    joined = jnp.concatenate(parts, axis=0)
    flat = jnp.array([code for group in codes for code in group], jnp.int32)
    order = jnp.argsort((flat ^ meta[0]) // 2)
    weight = joined[order]
    theirs, kept = [
        jnp.einsum("crs,csf->rf", half, weight, preferred_element_type=jnp.float32)
        for half in (other, mine)
    ]
    return theirs.astype(jnp.bfloat16), kept


def core_split_body(meta_ref, tokens_ref, mine_ref, other_ref):
    half = mine_ref.shape[2]
    low, high = tokens_ref[:, :half], tokens_ref[:, half:]

    @pl.when(meta_ref[0] % 2 == 0)
    def _():
        mine_ref[0], other_ref[0] = low, high

    @pl.when(meta_ref[0] % 2 == 1)
    def _():
        mine_ref[0], other_ref[0] = high, low


def core_split(meta, tokens, size):
    rows, width = tokens.shape
    count = width // size // 2
    out = pl.BlockSpec((1, rows, size), lambda n, meta_ref: (n, 0, 0))
    return pl.pallas_call(
        core_split_body,
        grid_spec=pltpu.PrefetchScalarGridSpec(
            num_scalar_prefetch=1,
            grid=(count,),
            in_specs=[pl.BlockSpec((rows, 2 * size), lambda n, meta_ref: (0, n))],
            out_specs=[out, out],
        ),
        out_shape=[jax.ShapeDtypeStruct((count, rows, size), jnp.bfloat16)] * 2,
        name="core_split",
    )(meta, tokens)


def token_halves(meta, tokens, size):
    if size % 64 == 0:
        return core_split(meta, tokens, size)
    rows, width = tokens.shape
    both = tokens.reshape(rows, width // size // 2, 2, size).transpose(2, 1, 0, 3)
    core = meta[0] % 2
    return both[core], both[1 - core]


def shards(
    tokens, lengths, latent_weight, latent_gain, expert_ids, gate_weights, gate_up, down_weight
):
    rows, width = tokens.shape
    rank_count = lax.axis_size("dp")
    rank = lax.axis_index("dp")
    experts = rank_count // GROUP
    pieces = rank_count // QUAD
    hidden_units = gate_up.shape[1] // 2
    length = lengths[rank]
    meta = rank.astype(jnp.int32).reshape(1)
    capacity = rows // experts + 2
    slots = -(-capacity // 8) * 8

    packed = pack(meta, lengths, expert_ids, tokens, experts, slots)
    columns = [[QUAD * s + low for s in range(pieces)] for low in range(QUAD)]
    mine, other = token_halves(meta, tokens, latent_weight.shape[0])

    half = latent_weight.shape[0] // 2
    middle = pieces == 4 and lax.axis_size("groups") == 2 and half % 16 == 0
    group = lax.axis_index("groups")
    first_group = group == 0
    sent = latent_weight[None]
    if middle:
        sent = lax.dynamic_slice_in_dim(sent, group * half, half, 1)
    latent_1 = swapped(sent, QUAD)
    packed = after(packed, latent_1)
    gate_2, mine, other = together(swapped(gate_up, 2), mine, swapped(other, 1))
    mid = down_weight.shape[0] // 2
    down_1 = [swapped(half_rows, 1) for half_rows in (down_weight[:mid], down_weight[mid:])]
    arrived, gate_1, gate_3 = together(
        lax.all_to_all(packed, "dp", 0, 0, axis_index_groups=columns, tiled=True),
        swapped(gate_up, 1),
        swapped(gate_2, 1),
    )
    down_1 = [after(piece, gate_2) for piece in down_1]
    down_3 = [swapped(piece, 2) for piece in down_1]
    if middle:
        cut = swapped(after(jnp.concatenate([sent, latent_1], axis=0), arrived), 2 * QUAD)
    else:
        held, codes = jnp.concatenate([latent_weight[None], latent_1], axis=0), [0, QUAD]
        for level in range(3, rank_count.bit_length() - 1):
            held = jnp.concatenate([held, swapped(held, 1 << level)], axis=0)
            codes = codes + [code ^ (1 << level) for code in codes]

    weight_in = [gate_up, gate_1, gate_2, gate_3]
    away = list(range(1, experts))
    (theirs,) = gate_up_product(meta, arrived, weight_in, [(away, 1, jnp.bfloat16)])
    ours, theirs_near, ours_near = gate_up_product(
        meta,
        arrived,
        weight_in,
        [(away, 0, jnp.float32), ([0], 1, jnp.bfloat16), ([0], 0, jnp.float32)],
    )
    if middle:
        ours, cut = together(ours, cut)
    down_3 = [after(piece, ours) for piece in down_3]
    quarter = mid // 2
    down_2 = [
        swapped(part, 1)
        for piece in down_3
        for part in (piece[:quarter], piece[quarter:])
    ]
    came, *down_2 = together(swapped(theirs, QUAD), *down_2)
    weight_out = [down_weight, *down_1, *down_2, *down_3]

    def activated(own, other):
        summed = own + other.astype(jnp.float32)
        gate, up = summed[:, :hidden_units], summed[:, hidden_units:]
        return (jax.nn.silu(gate) * up).astype(jnp.bfloat16)

    hidden = activated(ours, came)
    partner = swapped(hidden, QUAD)
    (made_own,) = down_product(meta, hidden, weight_out, experts - 1, True)
    halves = [[GROUP * e + low for e in range(experts)] for low in range(GROUP)]
    near = lax.all_to_all(made_own, "dp", 0, 0, axis_index_groups=halves, tiled=True)
    partner = after(partner, made_own)
    made = down_product(meta, partner, weight_out, experts - 1, False)
    far = [swapped(made[n - 1], QUAD * (2 * n + 1)) for n in away]

    came_near = after(swapped(after(theirs_near, hidden), QUAD), made[0])
    hidden_near = activated(ours_near, came_near)
    both = jnp.concatenate([hidden_near, swapped(hidden_near, QUAD)], axis=0)
    here, there = down_product(meta, both, weight_out, 2, False)
    near = [here, near]
    far = [swapped(there, QUAD)] + far

    if middle:
        mixed = after(jnp.concatenate([latent_1, cut], axis=0), hidden)
        swap = lax.ppermute(mixed, "groups", [(0, 1), (1, 0)])
        full = jnp.where(
            first_group,
            jnp.concatenate([mixed, swap], axis=1),
            jnp.concatenate([swap, mixed], axis=1),
        )
        held = [jnp.concatenate([latent_weight[None], full[:1]], axis=0), full[1:]]
        codes = [[0, 4], [8, 12]]
    else:
        held, codes = [held], [codes]
    latent_parts = held + [swapped(block, 2) for block in held]
    latent_codes = codes + [[code ^ 2 for code in group] for group in codes]
    given, kept = latent_sums(meta, mine, other, latent_parts, latent_codes)
    whose = (meta, lengths, expert_ids, gate_weights)
    moe_out = unpack(*whose, near, width, True)
    projected = kept + swapped(after(given, moe_out), 1).astype(jnp.float32)
    latent_cache = latent_finish(projected, latent_gain, length)
    moe_out = unpack(*whose, far, width, False, [moe_out])
    return (latent_cache, moe_out)


def solution(mesh):
    placed = (
        P(("groups", "dp"), None),
        P("groups"),
        P("dp", None),
        P(),
        P(("groups", "dp"), None),
        P(("groups", "dp"), None),
        P("dp", None),
        P("dp", None),
    )
    return jax.shard_map(
        shards,
        mesh=mesh,
        in_specs=placed,
        out_specs=(P(("groups", "dp"), None), P(("groups", "dp"), None)),
        check_vma=False,
    )
```

```python
import functools

import jax
import jax.numpy as jnp
from jax import lax
from jax.experimental import pallas as pl
from jax.experimental.pallas import tpu as pltpu
from jax.sharding import PartitionSpec as P

GROUP = 8
QUAD = 4

rope_base = 10000.0
norm_eps = 1e-06


def swapped(block, bits):
    count = lax.axis_size("dp")
    return lax.ppermute(block, "dp", [(low, low ^ bits) for low in range(count)])


def slots_of_rows(rank_ref, lengths_ref, ids_row):
    rows = ids_row.shape[1]
    length = lengths_ref[rank_ref[0]]
    down = lax.broadcasted_iota(jnp.int32, (rows, rows), 0)
    along = lax.broadcasted_iota(jnp.int32, (rows, rows), 1)
    ids_column = jnp.sum(
        jnp.where(down == along, ids_row.astype(jnp.float32), 0.0), axis=1, keepdims=True
    ).astype(jnp.int32)
    return length, down, along, ids_column, ids_column == ids_row


def picks_by_slot(rank_ref, lengths_ref, ids_row, experts, size, picks_ref):
    rows = ids_row.shape[1]
    length, down, along, _, same = slots_of_rows(rank_ref, lengths_ref, ids_row)
    earlier = same & (down < along) & (down < length)
    place = jnp.sum(earlier.astype(jnp.float32), axis=0, keepdims=True).astype(jnp.int32)
    live = lax.broadcasted_iota(jnp.int32, (1, rows), 1) < length
    chosen = jnp.where(live, ids_row, -1)
    slot = lax.broadcasted_iota(jnp.int32, (size, rows), 0)
    for expert in range(experts):
        hit = (place == slot) & (chosen == expert)
        picks_ref[expert] = hit.astype(jnp.float32).astype(jnp.bfloat16)


def picks_by_row(rank_ref, lengths_ref, ids_row, experts, size, picks_ref):
    rows = ids_row.shape[1]
    length, down, along, ids_column, same = slots_of_rows(rank_ref, lengths_ref, ids_row)
    earlier = same & (along < down) & (along < length)
    place = jnp.sum(earlier.astype(jnp.float32), axis=1, keepdims=True).astype(jnp.int32)
    live = lax.broadcasted_iota(jnp.int32, (rows, 1), 0) < length
    chosen = jnp.where(live, ids_column, -1)
    slot = lax.broadcasted_iota(jnp.int32, (rows, size), 1)
    for expert in range(experts):
        hit = (place == slot) & (chosen == expert)
        picks_ref[expert] = hit.astype(jnp.float32).astype(jnp.bfloat16)


def pack_body(rank_ref, lengths_ref, ids_ref, low_ref, high_ref, out_ref, picks_ref):
    experts, size, _ = picks_ref.shape

    @pl.when(pl.program_id(0) == 0)
    def _():
        picks_by_slot(rank_ref, lengths_ref, ids_ref[...], experts, size, picks_ref)

    for side, source_ref in enumerate((low_ref, high_ref)):
        for expert in range(experts):
            out_ref[2 * expert + side] = jnp.dot(
                picks_ref[expert], source_ref[...], preferred_element_type=jnp.float32
            ).astype(jnp.bfloat16)


def pack(rank_array, lengths, ids, tokens, experts, size):
    rows, width = tokens.shape
    part = width // GROUP

    def column_of(side):
        return lambda k, rank_ref, lengths_ref: (0, side * QUAD + ((rank_ref[0] % QUAD) ^ k))

    whole = lambda k, rank_ref, lengths_ref: (0, 0)
    return pl.pallas_call(
        pack_body,
        grid_spec=pltpu.PrefetchScalarGridSpec(
            num_scalar_prefetch=2,
            grid=(QUAD,),
            in_specs=[
                pl.BlockSpec((1, rows), whole),
                pl.BlockSpec((rows, part), column_of(0)),
                pl.BlockSpec((rows, part), column_of(1)),
            ],
            out_specs=pl.BlockSpec(
                (2 * experts, size, part), lambda k, rank_ref, lengths_ref: (0, 0, k)
            ),
            scratch_shapes=[pltpu.VMEM((experts, size, rows), jnp.bfloat16)],
        ),
        out_shape=jax.ShapeDtypeStruct((2 * experts, size, QUAD * part), jnp.bfloat16),
        compiler_params=pltpu.CompilerParams(vmem_limit_bytes=58 << 20),
        cost_estimate=pl.CostEstimate(
            flops=4 * rows * rows * width, bytes_accessed=4 * rows * width, transcendentals=0
        ),
        name="pack_rows",
    )(rank_array, lengths, ids.reshape(1, rows), tokens, tokens)


def unpack_body(near, rank_ref, lengths_ref, ids_ref, gate_ref, *refs):
    out_ref, picks_ref, gate_column_ref = refs[-3:]
    experts, rows, size = picks_ref.shape
    my_expert = rank_ref[0] // GROUP

    @pl.when(pl.program_id(0) == 0)
    def _():
        picks_by_row(rank_ref, lengths_ref, ids_ref[...], experts, size, picks_ref)
        down = lax.broadcasted_iota(jnp.int32, (rows, rows), 0)
        along = lax.broadcasted_iota(jnp.int32, (rows, rows), 1)
        gate_column_ref[...] = jnp.sum(
            jnp.where(down == along, gate_ref[...], 0.0), axis=1, keepdims=True
        )

    total = jnp.zeros(out_ref.shape, jnp.float32)
    for number in range(experts):
        expert = my_expert ^ number
        part = refs[1][expert] if near and number else refs[number][...]
        total += jnp.dot(picks_ref[expert], part, preferred_element_type=jnp.float32)
    out_ref[...] = (total * gate_column_ref[...]).astype(jnp.bfloat16)


def unpack(rank_array, lengths, ids, gates, parts, width, near, base=()):
    rows = ids.shape[0]
    part = width // GROUP
    size = parts[0].shape[-2]
    experts = parts[1].shape[0] if near else len(parts)

    def out_index(k, rank_ref, lengths_ref):
        quarter = rank_ref[0] % QUAD
        high = (rank_ref[0] // QUAD) % 2
        return (0, (high if near else 1 - high) * QUAD + (quarter ^ k))

    whole = lambda k, rank_ref, lengths_ref: (0, 0)
    specs = [pl.BlockSpec((size, part), lambda k, rank_ref, lengths_ref: (0, k))] * experts
    if near:
        both = pl.BlockSpec((experts, size, part), lambda k, rank_ref, lengths_ref: (0, 0, k))
        specs = [specs[0], both]
    return pl.pallas_call(
        functools.partial(unpack_body, near),
        grid_spec=pltpu.PrefetchScalarGridSpec(
            num_scalar_prefetch=2,
            grid=(QUAD,),
            in_specs=[pl.BlockSpec((1, rows), whole), pl.BlockSpec((1, rows), whole)]
            + specs
            + [pl.BlockSpec(memory_space=pl.ANY)] * len(base),
            out_specs=pl.BlockSpec((rows, part), out_index),
            scratch_shapes=[
                pltpu.VMEM((experts, rows, size), jnp.bfloat16),
                pltpu.VMEM((rows, 1), jnp.float32),
            ],
        ),
        out_shape=jax.ShapeDtypeStruct((rows, width), jnp.bfloat16),
        input_output_aliases={4 + len(specs): 0} if base else {},
        compiler_params=pltpu.CompilerParams(vmem_limit_bytes=58 << 20),
        cost_estimate=pl.CostEstimate(
            flops=2 * rows * rows * width, bytes_accessed=2 * rows * width, transcendentals=0
        ),
        name="unpack_rows",
    )(rank_array, lengths, ids.reshape(1, rows), gates.reshape(1, rows), *parts, *base)


def idle_body(*refs):
    del refs


def after(value, *events):
    anywhere = pl.BlockSpec(memory_space=pl.ANY)
    return pl.pallas_call(
        idle_body,
        in_specs=[anywhere] * (1 + len(events)),
        out_specs=anywhere,
        out_shape=jax.ShapeDtypeStruct(value.shape, value.dtype),
        input_output_aliases={0: 0},
        name="after",
    )(value, *events)


def together(*values):
    anywhere = pl.BlockSpec(memory_space=pl.ANY)
    return pl.pallas_call(
        idle_body,
        in_specs=[anywhere] * len(values),
        out_specs=[anywhere] * len(values),
        out_shape=[jax.ShapeDtypeStruct(value.shape, value.dtype) for value in values],
        input_output_aliases={number: number for number in range(len(values))},
        name="together",
    )(*values)


def gate_up_body(groups, meta_ref, *refs):
    del meta_ref
    count = sum(groups)
    parts, shares = refs[:count], refs[count : count + QUAD]
    outs, joined = refs[count + QUAD : -1], refs[-1]
    size = parts[0].shape[1]
    depth = shares[0].shape[0]

    @pl.when(pl.program_id(0) == 0)
    def _():
        for number, part in enumerate(parts):
            joined[pl.ds(number * size, size), :] = part[0]

    total = jnp.dot(joined[:, :depth], shares[0][...], preferred_element_type=jnp.float32)
    for k in range(1, QUAD):
        total += jnp.dot(
            joined[:, k * depth : (k + 1) * depth],
            shares[k][...],
            preferred_element_type=jnp.float32,
        )
    start = 0
    for group, out_ref in zip(groups, outs):
        out_ref[...] = total[start : start + group * size].astype(out_ref.dtype)
        start += group * size


def gate_up_product(meta, arrived, shares, groups):
    _, size, width = arrived.shape
    depth, columns = shares[0].shape
    tile = columns // 4
    rows = size * sum(len(numbers) for numbers, _, _ in groups)

    def source(number, side):
        def index(n, meta_ref):
            rank = meta_ref[0]
            return (2 * ((rank // GROUP) ^ number) + (((rank // QUAD) % 2) ^ side), 0, 0)

        return index

    across = lambda n, meta_ref: (0, n)
    picked = [source(number, side) for numbers, side, _ in groups for number in numbers]
    heights = [size * len(numbers) for numbers, _, _ in groups]
    return pl.pallas_call(
        functools.partial(gate_up_body, [len(numbers) for numbers, _, _ in groups]),
        grid_spec=pltpu.PrefetchScalarGridSpec(
            num_scalar_prefetch=1,
            grid=(columns // tile,),
            in_specs=[pl.BlockSpec((1, size, width), index) for index in picked]
            + [pl.BlockSpec((depth, tile), across) for _ in shares],
            out_specs=[pl.BlockSpec((height, tile), across) for height in heights],
            scratch_shapes=[pltpu.VMEM((rows, width), jnp.bfloat16)],
        ),
        out_shape=[
            jax.ShapeDtypeStruct((height, columns), dtype)
            for height, (_, _, dtype) in zip(heights, groups)
        ],
        compiler_params=pltpu.CompilerParams(vmem_limit_bytes=24 << 20),
        cost_estimate=pl.CostEstimate(
            flops=2 * rows * width * columns,
            bytes_accessed=2 * width * (rows + columns),
            transcendentals=0,
        ),
        name="gate_up_product",
    )(meta, *[arrived] * len(picked), *shares)


def down_body(places, joined, meta_ref, hidden_ref, *refs):
    k = pl.program_id(0)
    weight, done = refs[-2:]
    pieces, outs = refs[: len(places)], refs[len(places) : -2]
    count = outs[0].shape[0] - 1 if joined else len(outs)
    size = hidden_ref.shape[0] // count
    mine = meta_ref[0] // GROUP
    moves = []
    for number, (piece, (turn, start)) in enumerate(zip(pieces, places)):
        target = weight.at[turn, pl.ds(start, piece.shape[0]), :]
        moves.append(pltpu.make_async_copy(piece, target, done.at[number]))

    @pl.when(k == 0)
    def _():
        for move in moves:
            move.start()

    for turn in range(QUAD):

        @pl.when(k == turn)
        def _(turn=turn):
            for move, place in zip(moves, places):
                if place[0] == turn:
                    move.wait()

    made = jnp.dot(hidden_ref[...], weight[k], preferred_element_type=jnp.float32)
    for number in range(count):
        rows = made[number * size : (number + 1) * size].astype(jnp.bfloat16)
        if joined:
            outs[0][mine ^ (number + 1)] = rows
        else:
            outs[number][...] = rows


def down_product(meta, hidden, shares, count, joined):
    rows, depth = hidden.shape
    part = shares[0].shape[1]
    size = rows // count
    places, filled = [], 0
    for share in shares:
        places.append((filled // depth, filled % depth))
        filled += share.shape[0]
    whole = lambda k, meta_ref: (0, 0)
    if joined:
        out_specs = [pl.BlockSpec((count + 1, size, part), lambda k, meta_ref: (0, 0, k))]
        shapes = [(count + 1, size, QUAD * part)]
    else:
        out_specs = [pl.BlockSpec((size, part), lambda k, meta_ref: (0, k))] * count
        shapes = [(size, QUAD * part)] * count
    return pl.pallas_call(
        functools.partial(down_body, places, joined),
        grid_spec=pltpu.PrefetchScalarGridSpec(
            num_scalar_prefetch=1,
            grid=(QUAD,),
            in_specs=[pl.BlockSpec((rows, depth), whole)]
            + [pl.BlockSpec(memory_space=pl.ANY)] * len(shares),
            out_specs=out_specs,
            scratch_shapes=[
                pltpu.VMEM((QUAD, depth, part), jnp.bfloat16),
                pltpu.SemaphoreType.DMA((len(shares),)),
            ],
        ),
        out_shape=[jax.ShapeDtypeStruct(shape, jnp.bfloat16) for shape in shapes],
        compiler_params=pltpu.CompilerParams(vmem_limit_bytes=58 << 20),
        cost_estimate=pl.CostEstimate(
            flops=2 * rows * depth * QUAD * part,
            bytes_accessed=2 * (rows * depth + QUAD * part * (rows + depth)),
            transcendentals=0,
        ),
        name="down_product",
    )(meta, hidden, *shares)


def latent_finish(projected, gain, length):
    lat_width = gain.shape[0]
    compressed = projected[:, :lat_width]
    rotary = projected[:, lat_width:]
    inverse_rms = lax.rsqrt(jnp.mean(compressed * compressed, axis=1, keepdims=True) + norm_eps)
    normed = compressed * inverse_rms * gain[None, :]
    half_cols = rotary.shape[1] // 2
    positions = jnp.arange(projected.shape[0], dtype=jnp.int32)
    frequency = rope_base ** (-jnp.arange(half_cols, dtype=jnp.float32) / half_cols)
    angles = positions.astype(jnp.float32)[:, None] * frequency[None, :]
    cosine = jnp.cos(angles)
    sine_part = jnp.sin(angles)
    left_half = rotary[:, :half_cols]
    right_half = rotary[:, half_cols:]
    turned = jnp.concatenate(
        [left_half * cosine - right_half * sine_part, left_half * sine_part + right_half * cosine],
        axis=1,
    )
    result = jnp.concatenate([normed, turned], axis=1)
    return jnp.where((positions < length)[:, None], result, 0.0).astype(jnp.bfloat16)


def latent_body(codes, meta_ref, mine_ref, other_ref, *refs):
    parts, sums, weight, done = refs[: len(codes)], refs[len(codes) : -2], refs[-2], refs[-1]
    size = parts[0].shape[1]
    moves = []
    for part, group in zip(parts, codes):
        for number, code in enumerate(group):
            row = pl.multiple_of(((meta_ref[0] ^ code) // 2) * size, 16)
            move = pltpu.make_async_copy(
                part.at[number], weight.at[pl.ds(row, size), :], done.at[len(moves)]
            )
            move.start()
            moves.append(move)
    for move in moves:
        move.wait()
    for tokens_ref, sum_ref in zip((other_ref, mine_ref), sums):
        product = jnp.dot(tokens_ref[0], weight[:size, :], preferred_element_type=jnp.float32)
        for number in range(1, tokens_ref.shape[0]):
            product += jnp.dot(
                tokens_ref[number],
                weight[number * size : (number + 1) * size, :],
                preferred_element_type=jnp.float32,
            )
        sum_ref[...] = product.astype(sum_ref.dtype)


def latent_product(meta, mine, other, parts, codes):
    count, rows, size = mine.shape
    width = count * size
    columns = parts[0].shape[2]
    total = sum(len(group) for group in codes)
    inside = pl.BlockSpec(memory_space=pltpu.VMEM)
    return pl.pallas_call(
        functools.partial(latent_body, codes),
        in_specs=[pl.BlockSpec(memory_space=pltpu.SMEM), inside, inside]
        + [pl.BlockSpec(memory_space=pl.ANY)] * len(parts),
        out_specs=[inside, inside],
        out_shape=[
            jax.ShapeDtypeStruct((rows, columns), jnp.bfloat16),
            jax.ShapeDtypeStruct((rows, columns), jnp.float32),
        ],
        scratch_shapes=[
            pltpu.VMEM((width, columns), jnp.bfloat16),
            pltpu.SemaphoreType.DMA((total,)),
        ],
        compiler_params=pltpu.CompilerParams(vmem_limit_bytes=32 << 20),
        cost_estimate=pl.CostEstimate(
            flops=4 * rows * width * columns,
            bytes_accessed=2 * width * (2 * rows + columns),
            transcendentals=0,
        ),
        name="latent_product",
    )(meta, mine, other, *parts)


def latent_sums(meta, mine, other, parts, codes):
    if parts[0].shape[1] % 16 == 0:
        return latent_product(meta, mine, other, parts, codes)
    joined = jnp.concatenate(parts, axis=0)
    flat = jnp.array([code for group in codes for code in group], jnp.int32)
    order = jnp.argsort((flat ^ meta[0]) // 2)
    weight = joined[order]
    theirs, kept = [
        jnp.einsum("crs,csf->rf", half, weight, preferred_element_type=jnp.float32)
        for half in (other, mine)
    ]
    return theirs.astype(jnp.bfloat16), kept


def core_split_body(meta_ref, tokens_ref, mine_ref, other_ref):
    half = mine_ref.shape[2]
    low, high = tokens_ref[:, :half], tokens_ref[:, half:]

    @pl.when(meta_ref[0] % 2 == 0)
    def _():
        mine_ref[0], other_ref[0] = low, high

    @pl.when(meta_ref[0] % 2 == 1)
    def _():
        mine_ref[0], other_ref[0] = high, low


def core_split(meta, tokens, size):
    rows, width = tokens.shape
    count = width // size // 2
    out = pl.BlockSpec((1, rows, size), lambda n, meta_ref: (n, 0, 0))
    return pl.pallas_call(
        core_split_body,
        grid_spec=pltpu.PrefetchScalarGridSpec(
            num_scalar_prefetch=1,
            grid=(count,),
            in_specs=[pl.BlockSpec((rows, 2 * size), lambda n, meta_ref: (0, n))],
            out_specs=[out, out],
        ),
        out_shape=[jax.ShapeDtypeStruct((count, rows, size), jnp.bfloat16)] * 2,
        name="core_split",
    )(meta, tokens)


def token_halves(meta, tokens, size):
    if size % 64 == 0:
        return core_split(meta, tokens, size)
    rows, width = tokens.shape
    both = tokens.reshape(rows, width // size // 2, 2, size).transpose(2, 1, 0, 3)
    core = meta[0] % 2
    return both[core], both[1 - core]


def shards(
    tokens, lengths, latent_weight, latent_gain, expert_ids, gate_weights, gate_up, down_weight
):
    rows, width = tokens.shape
    rank_count = lax.axis_size("dp")
    rank = lax.axis_index("dp")
    experts = rank_count // GROUP
    pieces = rank_count // QUAD
    hidden_units = gate_up.shape[1] // 2
    length = lengths[rank]
    meta = rank.astype(jnp.int32).reshape(1)
    capacity = rows // experts + 2
    slots = -(-capacity // 8) * 8

    packed = pack(meta, lengths, expert_ids, tokens, experts, slots)
    columns = [[QUAD * s + low for s in range(pieces)] for low in range(QUAD)]
    mine, other = token_halves(meta, tokens, latent_weight.shape[0])

    half = latent_weight.shape[0] // 2
    middle = pieces == 4 and lax.axis_size("groups") == 2 and half % 16 == 0
    group = lax.axis_index("groups")
    first_group = group == 0
    sent = latent_weight[None]
    if middle:
        sent = lax.dynamic_slice_in_dim(sent, group * half, half, 1)
    latent_1 = swapped(sent, QUAD)
    packed = after(packed, latent_1)
    gate_2, mine, other = together(swapped(gate_up, 2), mine, swapped(other, 1))
    mid = down_weight.shape[0] // 2
    down_1 = [swapped(half_rows, 1) for half_rows in (down_weight[:mid], down_weight[mid:])]
    arrived, gate_1, gate_3 = together(
        lax.all_to_all(packed, "dp", 0, 0, axis_index_groups=columns, tiled=True),
        swapped(gate_up, 1),
        swapped(gate_2, 1),
    )
    down_1 = [after(piece, gate_2) for piece in down_1]
    down_3 = [swapped(piece, 2) for piece in down_1]
    if middle:
        cut = swapped(after(jnp.concatenate([sent, latent_1], axis=0), arrived), 2 * QUAD)
    else:
        held, codes = jnp.concatenate([latent_weight[None], latent_1], axis=0), [0, QUAD]
        for level in range(3, rank_count.bit_length() - 1):
            held = jnp.concatenate([held, swapped(held, 1 << level)], axis=0)
            codes = codes + [code ^ (1 << level) for code in codes]

    weight_in = [gate_up, gate_1, gate_2, gate_3]
    away = list(range(1, experts))
    (theirs,) = gate_up_product(meta, arrived, weight_in, [(away, 1, jnp.bfloat16)])
    ours, theirs_near, ours_near = gate_up_product(
        meta,
        arrived,
        weight_in,
        [(away, 0, jnp.float32), ([0], 1, jnp.bfloat16), ([0], 0, jnp.float32)],
    )
    if middle:
        ours, cut = together(ours, cut)
    down_3 = [after(piece, ours) for piece in down_3]
    quarter = mid // 2
    down_2 = [
        swapped(part, 1)
        for piece in down_3
        for part in (piece[:quarter], piece[quarter:])
    ]
    came, *down_2 = together(swapped(theirs, QUAD), *down_2)
    weight_out = [down_weight, *down_1, *down_2, *down_3]

    def activated(own, other):
        summed = own + other.astype(jnp.float32)
        gate, up = summed[:, :hidden_units], summed[:, hidden_units:]
        return (jax.nn.silu(gate) * up).astype(jnp.bfloat16)

    hidden = activated(ours, came)
    partner = swapped(hidden, QUAD)
    (made_own,) = down_product(meta, hidden, weight_out, experts - 1, True)
    halves = [[GROUP * e + low for e in range(experts)] for low in range(GROUP)]
    near = lax.all_to_all(made_own, "dp", 0, 0, axis_index_groups=halves, tiled=True)
    partner = after(partner, made_own)
    made = down_product(meta, partner, weight_out, experts - 1, False)
    far = [swapped(made[n - 1], QUAD * (2 * n + 1)) for n in away]

    came_near = after(swapped(after(theirs_near, hidden), QUAD), made[0])
    hidden_near = activated(ours_near, came_near)
    both = jnp.concatenate([hidden_near, swapped(hidden_near, QUAD)], axis=0)
    here, there = down_product(meta, both, weight_out, 2, False)
    near = [here, near]
    far = [swapped(there, QUAD)] + far

    if middle:
        mixed = after(jnp.concatenate([latent_1, cut], axis=0), hidden)
        swap = lax.ppermute(mixed, "groups", [(0, 1), (1, 0)])
        full = jnp.where(
            first_group,
            jnp.concatenate([mixed, swap], axis=1),
            jnp.concatenate([swap, mixed], axis=1),
        )
        held = [jnp.concatenate([latent_weight[None], full[:1]], axis=0), full[1:]]
        codes = [[0, 4], [8, 12]]
    else:
        held, codes = [held], [codes]
    latent_parts = held + [swapped(block, 2) for block in held]
    latent_codes = codes + [[code ^ 2 for code in group] for group in codes]
    given, kept = latent_sums(meta, mine, other, latent_parts, latent_codes)
    whose = (meta, lengths, expert_ids, gate_weights)
    moe_out = unpack(*whose, near, width, True)
    projected = kept + swapped(after(given, moe_out), 1).astype(jnp.float32)
    latent_cache = latent_finish(projected, latent_gain, length)
    moe_out = unpack(*whose, far, width, False, [moe_out])
    return (latent_cache, moe_out)


def solution(mesh):
    placed = (
        P(("groups", "dp"), None),
        P("groups"),
        P("dp", None),
        P(),
        P(("groups", "dp"), None),
        P(("groups", "dp"), None),
        P("dp", None),
        P("dp", None),
    )
    return jax.shard_map(
        shards,
        mesh=mesh,
        in_specs=placed,
        out_specs=(P(("groups", "dp"), None), P(("groups", "dp"), None)),
        check_vma=False,
    )
```
